32 devices in a mesh: dp: 8 (over y, x, core), cross: 4 (over z).
Axes of the slice: x: 2, y: 2, z: 4, core: 2. Of those that a mesh axis runs over, the one named last changes fastest.
Arguments:
- emb_table: bfloat16 [4096, 1014], P('cross'), may hold values from -6 to 6
- dense_input: bfloat16 [8192, 13], P('dp'), may hold values from -6 to 6
- feature_ids: int32 [8192, 26], P('dp'), may hold values from 0 to 4095
- labels: int32 [8192], P(('dp', 'cross')), may hold values 0 or 1
- cross_weight: bfloat16 [3, 1040, 1040], P(None, 'cross'), may hold values from -0.1875 to 0.1875
- cross_bias: bfloat16 [3, 1040], P(None, 'cross'), may hold values from -3 to 3
- tower_one: bfloat16 [1040, 1024], replicated, may hold values from -0.1875 to 0.1875
- bias_one: float32 [1024], replicated, may hold values from -3 to 3
- tower_two: bfloat16 [1024, 1024], replicated, may hold values from -0.1875 to 0.1875
- bias_two: float32 [1024], replicated, may hold values from -3 to 3
- out_weight: bfloat16 [2064], replicated, may hold values from -0.125 to 0.125
- out_bias: float32 [1], replicated, may hold values from -3 to 3
Outputs:
- loss_value: float32 [], replicated
- logits: float32 [8192], P(('dp', 'cross'))
- dense_grad: float32 [8192, 13], P(('dp', 'cross'))
- table_grad: float32 [4096, 1014], P('cross')
- cross_weight_grad: float32 [3, 1040, 1040], P(None, 'cross')
- cross_bias_grad: float32 [3, 1040], P(None, 'cross')
- tower_one_grad: float32 [1040, 1024], replicated
- bias_one_grad: float32 [1024], replicated
- tower_two_grad: float32 [1024, 1024], replicated
- bias_two_grad: float32 [1024], replicated
- out_weight_grad: float32 [2064], replicated
- out_bias_grad: float32 [1], replicated
- row_counts: int32 [4096, 26], P('cross')
The draws below stay inside these ranges and needn't reach their ends.
All inputs are finite; a program needn't handle non-finite values. No bound on the sum of `labels` on one device may be relied on, other than what follows from the above.
Results may differ from the reference program's by a relative error of at most 0.008.
Values may be sent and summed in bfloat16 or wider, within the bound.
No kernel may reach another device: no remote copies, remote signals or barrier semaphores. Data moves between devices by JAX's collectives and lax.ppermute only.
A program may use at most 128 MiB of HBM per device.

```python
import math
import jax
import jax.numpy as jnp
import numpy as np
from jax import lax

FIELDS = 26
EMB = 39
DENSE = 13
WIDTH = 1040
HIDDEN_SIZE = 1024
LAYERS = 3
EX_DEV = 1024
EXAMPLES = 8192
VOCAB = 4096


def set_ends(entries, stream_key, least, largest):
    longest = entries.shape.index(max(entries.shape))
    spots = []
    for shift in (0, 1):
        where = [jax.random.randint(jax.random.fold_in(stream_key, axis), (), 0, length) for axis, length in enumerate(entries.shape)]
        where[longest] = (where[longest] + shift) % entries.shape[longest]
        spots.append(tuple(where))
    return entries.at[spots[0]].set(least).at[spots[1]].set(largest)


def block_scale(stream_key, extent, cuts, low, top_value):
    factor_of, own = 1.0, jax.random.fold_in(stream_key, 6)
    for dim, parts in cuts:
        steps = jnp.exp(jax.random.uniform(jax.random.fold_in(own, dim), (parts,), jnp.float32, low / len(cuts), top_value / len(cuts)))
        factor_of = factor_of * jnp.repeat(steps, extent[dim] // parts).reshape([-1 if axis == dim else 1 for axis in range(len(extent))])
    return factor_of


def rank_table(number_of, skew):
    portions = [(1 << 20) // math.isqrt(grade ** skew) + 1 for grade in range(1, number_of + 1)]
    scale = 1 + sum(portions) // (1 << 30)
    return np.cumsum(np.array([max(1, weight // scale) for weight in portions]))


def ranked(rng, shape, count, lean):
    table = rank_table(count, lean)
    lot = jax.random.randint(jax.random.fold_in(rng, 1), shape, 0, int(table[count - 1]))
    rank = jnp.searchsorted(jnp.asarray(table, jnp.int32), lot, side="right")
    return jax.random.permutation(jax.random.fold_in(rng, 2), count)[rank].astype(jnp.int32)


def gaussian(key, extent, width, most, split=(), kind=jnp.bfloat16):
    result = width * jax.random.normal(key, extent, jnp.float32)
    if split:
        result = result * block_scale(key, extent, split, -0.22, 0.18)
    return jnp.clip(result, -most, most).astype(kind)


def setup_inputs(seed: int = 0) -> dict:
    key_of = jax.random.split(jax.random.key(seed), 13)
    emb_table = gaussian(key_of[0], (VOCAB, FIELDS * EMB), 1.0, 6.0, ((0, 4),))
    dense_input = gaussian(key_of[1], (EXAMPLES, DENSE), 1.0, 6.0, ((0, 8),))
    feature_ids = set_ends(ranked(key_of[2], (EXAMPLES, FIELDS), VOCAB, 2), jax.random.fold_in(key_of[2], 3), 0, VOCAB - 1).astype(jnp.int32)
    labels = set_ends((jax.random.randint(key_of[3], (EXAMPLES,), 0, 4) < 1).astype(jnp.int32), jax.random.fold_in(key_of[3], 1), 0, 1)
    cross_weight = gaussian(key_of[4], (LAYERS, WIDTH, WIDTH), WIDTH ** -0.5, 0.1875, ((1, 4),))
    cross_bias = gaussian(key_of[5], (LAYERS, WIDTH), 0.5, 3.0, ((1, 4),))
    tower_one = gaussian(key_of[6], (WIDTH, HIDDEN_SIZE), WIDTH ** -0.5, 0.1875)
    bias_one = gaussian(key_of[7], (HIDDEN_SIZE,), 0.5, 3.0, (), jnp.float32)
    tower_two = gaussian(key_of[8], (HIDDEN_SIZE, HIDDEN_SIZE), HIDDEN_SIZE ** -0.5, 0.1875)
    bias_two = gaussian(key_of[9], (HIDDEN_SIZE,), 0.5, 3.0, (), jnp.float32)
    out_weight = gaussian(key_of[10], (WIDTH + HIDDEN_SIZE,), (WIDTH + HIDDEN_SIZE) ** -0.5, 0.125)
    out_bias = gaussian(key_of[11], (1,), 0.5, 3.0, (), jnp.float32)
    return dict(emb_table=emb_table, dense_input=dense_input, feature_ids=feature_ids, labels=labels, cross_weight=cross_weight, cross_bias=cross_bias, tower_one=tower_one, bias_one=bias_one, tower_two=tower_two, bias_two=bias_two, out_weight=out_weight, out_bias=out_bias)


@jax.custom_vjp
def low(v):
    return lax.optimization_barrier(v.astype(jnp.bfloat16)).astype(jnp.float32)

@jax.custom_vjp
def low_back(v):
    return v

def low_keep(v):
    return (low(v), None)

def low_pass(kept, grad):
    return (grad,)

def back_keep(v):
    return (v, None)

def back_low(kept, grad):
    return (low(grad),)
low.defvjp(low_keep, low_pass)
low_back.defvjp(back_keep, back_low)
exact_mode = lax.Precision.HIGHEST

def silu(pre_act):
    return pre_act * jax.nn.sigmoid(pre_act)

def forward(weights, dense_block, id_block, label_block):
    table_all, cross_all, cross_shift, first_tower, first_shift, second_tower, second_shift, logit_weight, logit_shift = weights
    row_count = id_block.shape[0]
    table_cube = table_all.reshape(VOCAB, FIELDS, EMB)
    field_index = jnp.arange(FIELDS, dtype=jnp.int32)[None, :]
    looked = table_cube[id_block, field_index].reshape(row_count, FIELDS * EMB)
    padding = jnp.zeros((row_count, WIDTH - FIELDS * EMB - DENSE), jnp.float32)
    first_input = jnp.concatenate([looked, dense_block, padding], axis=1)
    cross_state = first_input
    for layer_index in range(LAYERS):
        mixed_term = low_back(jnp.dot(low(cross_state), cross_all[layer_index], precision=exact_mode) + cross_shift[layer_index])
        cross_state = first_input * mixed_term + cross_state
    top_values = low_back(low(cross_state))
    hid_one = low_back(jnp.dot(top_values, first_tower, precision=exact_mode) + first_shift)
    act_one = low(silu(hid_one))
    hid_two = low_back(jnp.dot(act_one, second_tower, precision=exact_mode) + second_shift)
    act_two = low(silu(hid_two))
    logit_values = low_back(jnp.dot(top_values, logit_weight[:WIDTH], precision=exact_mode) + jnp.dot(act_two, logit_weight[WIDTH:], precision=exact_mode) + logit_shift[0])
    loss_part = jnp.sum(jax.nn.softplus(logit_values) - label_block * logit_values) / EXAMPLES
    return (loss_part, logit_values)

def reference(emb_table, dense_input, feature_ids, labels, cross_weight, cross_bias, tower_one, bias_one, tower_two, bias_two, out_weight, out_bias):
    weights = (emb_table.astype(jnp.float32), cross_weight.astype(jnp.float32), cross_bias.astype(jnp.float32), tower_one.astype(jnp.float32), bias_one, tower_two.astype(jnp.float32), bias_two, out_weight.astype(jnp.float32), out_bias)
    blocks = EXAMPLES // EX_DEV
    dense_blocks = dense_input.astype(jnp.float32).reshape(blocks, EX_DEV, DENSE)
    id_blocks = feature_ids.reshape(blocks, EX_DEV, FIELDS)
    label_blocks = labels.astype(jnp.float32).reshape(blocks, EX_DEV)
    zero_grads = jax.tree.map(jnp.zeros_like, weights)

    def scan_step(carry_pair, block_data):
        grad_sums, loss_total = carry_pair
        id_block, dense_block, label_block = block_data

        def run_block(weight_set, dense_part):
            return forward(weight_set, dense_part, id_block, label_block)
        loss_part, pull_back, logit_values = jax.vjp(run_block, weights, dense_block, has_aux=True)
        weight_grads, dense_grads = pull_back(jnp.ones_like(loss_part))
        grad_sums = jax.tree.map(jnp.add, grad_sums, weight_grads)
        return ((grad_sums, loss_total + loss_part), (logit_values, dense_grads))
    start_pair = (zero_grads, jnp.zeros((), jnp.float32))
    (grad_sums, loss_total), (logit_blocks, dense_grads) = lax.scan(scan_step, start_pair, (id_blocks, dense_blocks, label_blocks))
    count_keys = (feature_ids * FIELDS + jnp.arange(FIELDS, dtype=jnp.int32)[None, :]).reshape(-1)
    row_counts = jax.ops.segment_sum(jnp.ones_like(count_keys), count_keys, num_segments=VOCAB * FIELDS).reshape(VOCAB, FIELDS)
    return (loss_total, logit_blocks.reshape(EXAMPLES), dense_grads.reshape(EXAMPLES, DENSE), grad_sums[0], grad_sums[1], grad_sums[2], grad_sums[3], grad_sums[4], grad_sums[5], grad_sums[6], grad_sums[7], grad_sums[8], row_counts)
```

```python
import functools

import jax
import jax.numpy as jnp
from jax import lax
from jax.experimental import pallas as pl
from jax.experimental.pallas import tpu as pltpu
from jax.sharding import PartitionSpec as P

F32 = jnp.float32
BF16 = jnp.bfloat16
ROWS_IN_ROWS = (((0,), (0,)), ((), ()))
LANES_IN_LANES = (((1,), (1,)), ((), ()))
LANES = 128
LOW_BITS = 8
LOW_ROWS = 1 << LOW_BITS
CHIPS = 4
MARGIN = 48
IN_VMEM = pl.BlockSpec(memory_space=pltpu.VMEM)
IN_SMEM = pl.BlockSpec(memory_space=pltpu.SMEM)
IN_PLACE = pl.BlockSpec(memory_space=pl.ANY)
Shape = jax.ShapeDtypeStruct


def round_up(size, step):
    return -(-size // step) * step


def dot(left, right, dims=(((1,), (0,)), ((), ()))):
    return lax.dot_general(left, right, dims, preferred_element_type=F32)


def silu_slope(pre_act):
    sigmoid_part = jax.nn.sigmoid(pre_act)
    return sigmoid_part * (1.0 + pre_act * (1.0 - sigmoid_part))


def params(mebibytes=56):
    return pltpu.CompilerParams(vmem_limit_bytes=mebibytes * 1024 * 1024)


def lookup_kernel(at, table, ids, *rest, fields, emb, ways):
    outs, gathered = rest[:ways], rest[ways]
    highs = table.shape[1] // LOW_ROWS
    group = ids.shape[1]
    part = group // ways
    slab = emb + 1
    low_iota = lax.broadcasted_iota(jnp.int32, (LOW_ROWS, group), 0)
    for field in range(fields):
        left = jnp.concatenate(
            [table[pl.ds(field * emb, slab), pl.ds(high * LOW_ROWS, LOW_ROWS)] for high in range(highs)], axis=0
        ).astype(BF16)
        local = ids[pl.ds(field, 1), :]
        low = jnp.bitwise_and(local, LOW_ROWS - 1)
        high_id = jnp.right_shift(local, LOW_BITS)
        hot = jnp.where(low_iota == low, 1.0, 0.0).astype(BF16)
        picked = dot(left, hot)
        total = jnp.zeros((slab, group), F32)
        for high in range(highs):
            total = total + jnp.where(high_id == high, picked[high * slab : (high + 1) * slab], 0.0)
        gathered[pl.ds(field * emb, slab), :] = total
    for step in range(ways):
        start = pl.multiple_of((at[0] ^ step) * part, part)
        outs[step][...] = gathered[:, pl.ds(start, part)].astype(BF16)


def count_kernel(ids, out, *, fields):
    highs = out.shape[1] // LOW_ROWS
    group = ids.shape[1]
    low_iota = lax.broadcasted_iota(jnp.int32, (LOW_ROWS, group), 0)
    high_iota = lax.broadcasted_iota(jnp.int32, (8, group), 0)
    for field in range(fields):
        local = ids[pl.ds(field, 1), :]
        low = jnp.bitwise_and(local, LOW_ROWS - 1)
        hot = jnp.where(low_iota == low, 1.0, 0.0).astype(BF16)
        marks = jnp.where(high_iota == jnp.right_shift(local, LOW_BITS), 1.0, 0.0).astype(BF16)
        got = dot(marks, hot, LANES_IN_LANES)
        for high in range(highs):
            out[pl.ds(field, 1), pl.ds(high * LOW_ROWS, LOW_ROWS)] = got[high : high + 1].astype(jnp.int32)


def weight_copies(own, pieces, weights, sems, at):
    ways, width = weights.shape[0], weights.shape[3]
    copies = [pltpu.make_async_copy(own.at[:, :, pl.ds(0, width)], weights.at[at[0]], sems.at[0])]
    for rel, piece in enumerate(pieces):
        column = pl.multiple_of(((at[1] ^ (rel // 2)) * 2 + (at[2] ^ (rel % 2))) * LANES, LANES)
        for step in range(1, ways):
            target = weights.at[at[0] ^ step, :, :, pl.ds(column, LANES)]
            copies.append(pltpu.make_async_copy(piece.at[step - 1], target, sems.at[len(copies)]))
    return copies


def split_cores(keep, send, core, value, chip_step, place_step, row):
    count = value.shape[0]
    first, second = value[:, :LANES], value[:, LANES:]
    keep[chip_step, place_step, pl.ds(row, count), :] = jnp.where(core == 0, first, second)
    send[chip_step, place_step, pl.ds(row, count), :] = jnp.where(core == 0, second, first).astype(BF16)


def forward_kernel(at, *refs, ways, emb_end, scale):
    refs = list(refs)
    take = lambda count: [refs.pop(0) for _ in range(count)]
    parts = take(ways)
    dense_t, own = take(2)
    pieces = take(2 * CHIPS)
    tails, bias, one_w, one_b, two_w, two_b, out_w, out_b, labels = take(9)
    first_out, lows, mixes, top_grad, logits_out, keep, send, small = take(8)
    weights, turned, first, state, sems = take(5)
    place, chip, core = at[0], at[1], at[2]
    layers, shard, full = own.shape
    rows = parts[0].shape[1]
    main = weights.shape[3]
    extra = full - main
    hidden = one_w.shape[1]
    copies = weight_copies(own, pieces, weights, sems, at)
    for copy in copies:
        copy.start()
    looked = parts[0][...].astype(F32)
    for piece in parts[1:]:
        looked = looked + piece[...].astype(F32)
    turned[pl.ds(0, looked.shape[0]), :] = looked
    turned[pl.ds(emb_end, dense_t.shape[0]), :] = dense_t[...]
    used = emb_end + dense_t.shape[0]
    turned[pl.ds(used, turned.shape[0] - used), :] = jnp.zeros((turned.shape[0] - used, rows), F32)
    start = turned[...].T[:, :full]
    first[...] = start
    state[...] = start
    first_out[...] = start.astype(BF16)
    for copy in copies:
        copy.wait()

    @pl.loop(0, layers)
    def _(layer):
        low = state[...].astype(BF16)
        lows[layer] = low
        body = jnp.zeros((rows, main), F32)
        edge = jnp.zeros((rows, extra), F32)
        for block in range(ways):
            chunk = low[:, shard * block : shard * (block + 1)]
            tail = tails[block, pl.ds(pl.multiple_of(extra * layer, extra), extra), pl.ds(0, shard)]
            body = body + dot(chunk, weights[block, layer])
            edge = edge + dot(chunk, tail, LANES_IN_LANES)
        mixed = jnp.concatenate([body, edge], axis=1) + bias[pl.ds(layer, 1), :]
        mixes[layer] = mixed
        state[...] = first[...] * mixed + state[...]

    top = state[...].astype(BF16)
    hid_one = dot(top, one_w[...]) + one_b[...]
    act_one = jax.nn.silu(hid_one).astype(BF16)
    hid_two = dot(act_one, two_w[...]) + two_b[...]
    act_two = jax.nn.silu(hid_two).astype(BF16)
    top_float, act_float = top.astype(F32), act_two.astype(F32)
    weight_top = out_w[:, :full].astype(F32)
    weight_act = out_w[:, full:].astype(F32)
    logits = (
        jnp.sum(top_float * weight_top, axis=1, keepdims=True)
        + jnp.sum(act_float * weight_act, axis=1, keepdims=True)
        + out_b[...]
    )
    logits_out[...] = logits
    label = labels[...]
    loss = jnp.sum(jax.nn.softplus(logits) - label * logits, axis=0, keepdims=True) * scale
    g_logit = ((jax.nn.sigmoid(logits) - label) * scale).astype(BF16).astype(F32)
    g_two = (g_logit * weight_act * silu_slope(hid_two)).astype(BF16)
    g_one = (dot(g_two, two_w[...], LANES_IN_LANES) * silu_slope(hid_one)).astype(BF16)
    top_grad[...] = (dot(g_one, one_w[...], LANES_IN_LANES) + g_logit * weight_top).astype(BF16)
    one_float, two_float = g_one.astype(F32), g_two.astype(F32)
    lane = lax.broadcasted_iota(jnp.int32, (1, LANES), 1)
    bias_grad = jnp.sum(g_logit, axis=0, keepdims=True)
    small[...] = jnp.zeros_like(small)
    small[pl.ds(0, 1), pl.ds(0, hidden)] = jnp.sum(one_float, axis=0, keepdims=True)
    small[pl.ds(1, 1), pl.ds(0, hidden)] = jnp.sum(two_float, axis=0, keepdims=True)
    small[pl.ds(2, 1), pl.ds(0, full)] = jnp.sum(top_float * g_logit, axis=0, keepdims=True)
    small[pl.ds(3, 1), pl.ds(0, hidden)] = jnp.sum(act_float * g_logit, axis=0, keepdims=True)
    small[pl.ds(7, 1), pl.ds(0, LANES)] = jnp.where(lane == 0, loss, jnp.where(lane == 1, bias_grad, 0.0))

    top_t = top_float.T
    tail_t = top_t[main:full].astype(BF16)
    top_t = top_t[:main].astype(BF16)
    act_t = act_one.astype(F32).T.astype(BF16)
    part = hidden // ways
    wide = 2 * LANES
    edge_rows = extra // ways
    state[:, :hidden] = one_float
    first[:, :hidden] = two_float
    for step in range(CHIPS):
        lanes = pl.ds(pl.multiple_of((chip ^ step) * wide, wide), wide)
        one_cols = state[:, lanes].astype(BF16)
        two_cols = first[:, lanes].astype(BF16)
        edge = dot(tail_t, one_cols)
        rest = keep.shape[2] - 2 * part
        for block in range(ways):
            target = place ^ block
            own_rows = slice(block * part, (block + 1) * part)
            split_cores(keep, send, core, dot(top_t[own_rows], one_cols), step, target, 0)
            split_cores(keep, send, core, dot(act_t[own_rows], two_cols), step, target, part)
            ends = edge[block * edge_rows : (block + 1) * edge_rows]
            ends = jnp.concatenate([ends, jnp.zeros((rest - edge_rows, wide), F32)], axis=0)
            split_cores(keep, send, core, ends, step, target, 2 * part)


def backward_kernel(at, *refs, ways, gap, dense_at):
    refs = list(refs)
    take = lambda count: [refs.pop(0) for _ in range(count)]
    (own,) = take(1)
    pieces = take(2 * CHIPS)
    tails, first_in, lows, mixes, top_grad = take(5)
    keep, send, emb_send, dense_grad, sums = take(5)
    weights, turned, g_mixed, low_t, pack, sems = take(6)
    place, chip, core = at[0], at[1], at[2]
    layers, shard, full = own.shape
    rows = first_in.shape[0]
    main = weights.shape[3]
    extra = full - main
    wide = 2 * LANES
    copies = weight_copies(own, pieces, weights, sems, at)
    for copy in copies:
        copy.start()
    pack[...] = jnp.zeros_like(pack)
    sums[...] = jnp.zeros_like(sums)
    first = first_in[...].astype(F32)
    grad = top_grad[...].astype(F32)
    total = jnp.zeros_like(grad)
    pad = jnp.zeros((rows, turned.shape[0] - full), F32)
    for copy in copies:
        copy.wait()
    for layer in reversed(range(layers)):
        rounded = (grad * first).astype(BF16)
        values = rounded.astype(F32)
        g_mixed[layer] = values[:, :main]
        sums[pl.ds(4 + layer, 1), pl.ds(0, full)] = jnp.sum(values, axis=0, keepdims=True)
        total = total + grad * mixes[layer]
        backs = []
        for block in range(ways):
            tail = tails[block, pl.ds(extra * layer, extra), pl.ds(0, shard)]
            backs.append(dot(rounded[:, :main], weights[block, layer], LANES_IN_LANES) + dot(rounded[:, main:full], tail))
        grad = grad + jnp.concatenate(backs, axis=1)
        low = lows[layer]
        edge = dot(rounded[:, main:full], low, ROWS_IN_ROWS)
        for block in range(ways):
            pack[block, :, pl.ds(layer * shard, shard)] = edge[:, block * shard : (block + 1) * shard]
        turned[...] = jnp.concatenate([low.astype(F32), pad], axis=1).T
        for block in range(ways):
            low_t[layer, block, pl.ds(0, shard), :] = turned[pl.ds(block * shard, shard), :].astype(BF16)
    total = total + grad
    dense_grad[...] = total[:, dense_at : dense_at + dense_grad.shape[1]]
    turned[...] = jnp.concatenate([total, pad], axis=1).T
    for step in range(CHIPS):
        emb_send[step ^ chip] = turned[pl.ds(step * wide, wide), :].astype(BF16)
    for step in range(CHIPS):
        lanes = pl.ds(pl.multiple_of((chip ^ step) * wide, wide), wide)
        for layer in range(layers):
            columns = g_mixed[layer, :, lanes].astype(BF16)
            for block in range(ways):
                product = dot(low_t[layer, block], columns)[:shard]
                product = jnp.concatenate([product, jnp.zeros((gap - shard, wide), F32)], axis=0)
                split_cores(keep, send, core, product, step, place ^ block, layer * gap)
        for block in range(ways):
            split_cores(keep, send, core, pack[block, :, lanes], step, place ^ block, layers * gap)


def scatter_kernel(at, *refs, ways, emb):
    pieces, ids, keep, send, spread, table = refs[:CHIPS], *refs[CHIPS:]
    place, chip, core = at[0], at[1], at[2]
    wide, part = pieces[0].shape
    group = part * CHIPS
    highs = table.shape[0]
    per = highs // ways
    half = per // 2
    slab = emb + 1
    spread[...] = jnp.zeros_like(spread)
    for step, piece in enumerate(pieces):
        spread[pl.ds(MARGIN, wide), pl.ds(step * part, part)] = piece[...].astype(F32)
    low_iota = lax.broadcasted_iota(jnp.int32, (LOW_ROWS, group), 0)
    for mine in range(CHIPS):

        @pl.when(chip == mine)
        def _(mine=mine):
            for slot in range(ids.shape[0]):
                begin = ((mine * wide) // emb + slot) * emb - mine * wide + MARGIN
                values = spread[pl.ds(begin, slab), :]
                this = ids[pl.ds(slot, 1), :]
                high_id = jnp.right_shift(this, LOW_BITS)
                hot = jnp.where(low_iota == jnp.bitwise_and(this, LOW_ROWS - 1), 1.0, 0.0).astype(BF16)
                stacked = jnp.concatenate(
                    [jnp.where(high_id == high, values, 0.0) for high in range(highs)], axis=0
                ).astype(BF16)
                got = dot(stacked, hot, LANES_IN_LANES)
                for high in range(highs):
                    table[high, pl.ds(begin, emb), :] = got[high * slab : high * slab + emb]

    for block in range(ways):
        target = block ^ place
        for piece in range(half):
            keep[target, piece] = table[block * per + core * half + piece, pl.ds(MARGIN, wide), :]
            send[target, piece] = table[block * per + (1 - core) * half + piece, pl.ds(MARGIN, wide), :].astype(BF16)


def turn_kernel(*refs):
    parts, out = refs[:-1], refs[-1]
    for piece in range(out.shape[0]):
        total = parts[0][piece].astype(F32)
        for part in parts[1:]:
            total = total + part[piece].astype(F32)
        out[piece] = total.T.astype(BF16)


def table_kernel(at, *refs):
    pieces, out = refs[:-1], refs[-1]
    half, low, wide = pieces[0].shape
    last = CHIPS - 1
    for rel, piece in enumerate(pieces):
        chip = at[1] ^ (rel // 2)
        core = at[2] ^ (rel % 2)
        for block in range(half):
            rows = pl.ds(pl.multiple_of(core * half * low + block * low, low), low)
            values = piece[block].astype(F32)

            @pl.when(chip < last)
            def _(rows=rows, values=values, chip=chip):
                out[rows, pl.ds(pl.multiple_of(chip * wide, wide), wide)] = values

            @pl.when(chip == last)
            def _(rows=rows, values=values):
                width = out.shape[1] - last * wide
                out[rows, pl.ds(last * wide, width)] = values[:, :width]


def tower_kernel(at, *refs, ways):
    pieces, (one_out, two_out) = refs[:-2], refs[-2:]
    hidden = two_out.shape[0]
    part = hidden // ways
    ends = (one_out.shape[0] - hidden) // ways
    for rel, piece in enumerate(pieces):
        column = pl.multiple_of(((at[1] ^ (rel // 2)) * 2 + (at[2] ^ (rel % 2))) * LANES, LANES)
        lanes = pl.ds(column, LANES)
        for block in range(ways):
            source = block ^ at[0]
            one_out[pl.ds(block * part, part), lanes] = piece[source, pl.ds(0, part), :].astype(F32)
            two_out[pl.ds(block * part, part), lanes] = piece[source, pl.ds(part, part), :].astype(F32)
            one_out[pl.ds(hidden + block * ends, ends), lanes] = piece[source, pl.ds(2 * part, ends), :].astype(F32)


def cross_kernel(at, *refs, gap):
    pieces, out, pack = refs[:-2], refs[-2], refs[-1]
    layers, shard, full = out.shape
    main = pack.shape[1]
    extra = full - main
    for rel, piece in enumerate(pieces):
        column = pl.multiple_of(((at[1] ^ (rel // 2)) * 2 + (at[2] ^ (rel % 2))) * LANES, LANES)
        lanes = pl.ds(column, LANES)
        for layer in range(layers):
            out[layer, :, lanes] = piece[pl.ds(layer * gap, shard), :].astype(F32)
        pack[pl.ds(0, extra), lanes] = piece[pl.ds(layers * gap, extra), :].astype(F32)
    pack[pl.ds(extra, pack.shape[0] - extra), :] = jnp.zeros((pack.shape[0] - extra, main), F32)
    turned = pack[...].T
    for layer in range(layers):
        out[layer, :, pl.ds(main, extra)] = turned[layer * shard : (layer + 1) * shard, :extra]


class Links:
    def __init__(self, dp_size, cross_size):
        bits = dp_size.bit_length() - 1
        axis_bits = (bits - 1) // 2
        self.dp_size, self.cross_size = dp_size, cross_size
        self.core = 1
        self.chip_masks = (1 << 1, 1 << (1 + axis_bits))
        used = (self.core, *self.chip_masks)
        self.others = tuple(1 << bit for bit in range(bits) if 1 << bit not in used)

    def chip_mask(self, step):
        return sum(mask for bit, mask in enumerate(self.chip_masks) if step >> bit & 1)

    def chip(self, dp_place):
        return sum((dp_place // mask % 2) << bit for bit, mask in enumerate(self.chip_masks))

    def over_dp(self, value, mask):
        return lax.ppermute(value, "dp", [(one, one ^ mask) for one in range(self.dp_size)])

    def over_cross(self, value, mask):
        return lax.ppermute(value, "cross", [(one, one ^ mask) for one in range(self.cross_size)])

    def chips_swap(self, value_of):
        return [self.over_dp(value_of(step), self.chip_mask(step)) for step in range(1, CHIPS)]

    def cross_swap(self, value_of):
        return [self.over_cross(value_of(step), step) for step in range(1, self.cross_size)]

    def add_others(self, value):
        for mask in self.others:
            value = value + self.over_dp(value.astype(BF16), mask).astype(F32)
        return value

    def everywhere(self, value):
        for bit in range(self.dp_size.bit_length() - 1):
            value = value + self.over_dp(value, 1 << bit)
        for bit in range(self.cross_size.bit_length() - 1):
            value = value + self.over_cross(value, 1 << bit)
        return value

    def plane_gather(self, value):
        by_chip = [value, *self.chips_swap(lambda step: value)]
        return [each for one in by_chip for each in (one, self.over_dp(one, self.core))]

    def scatter_sum(self, keep, send):
        held = keep + self.over_dp(send, self.core).astype(F32)
        got = self.chips_swap(lambda step: held[step].astype(BF16))
        held = held[0] + sum(one.astype(F32) for one in got)
        held = self.add_others(held)
        got = self.cross_swap(lambda step: held[step].astype(BF16))
        return held[0] + sum(one.astype(F32) for one in got)


def body(
    emb_table,
    dense_input,
    feature_ids,
    labels,
    cross_weight,
    cross_bias,
    tower_one,
    bias_one,
    tower_two,
    bias_two,
    out_weight,
    out_bias,
):
    layers, shard, full = cross_weight.shape
    group, fields = feature_ids.shape
    rows_here, emb_end = emb_table.shape
    emb = emb_end // fields
    dense_width = dense_input.shape[1]
    hidden = tower_one.shape[1]
    main = hidden
    extra = full - main
    ways = lax.axis_size("cross")
    place = lax.axis_index("cross")
    dp_place = lax.axis_index("dp")
    links = Links(lax.axis_size("dp"), ways)
    rows = group // ways
    scale = 1.0 / (group * links.dp_size)
    chip, core = links.chip(dp_place), dp_place % 2
    at = jnp.stack([place, chip, core]).astype(jnp.int32)
    wide = 2 * LANES
    gap = round_up(shard, 16)

    column = (chip * 2 + core) * LANES
    own_block = lax.dynamic_slice_in_dim(cross_weight, column, LANES, 2)
    foreign = jnp.stack(links.cross_swap(lambda step: own_block))
    pieces = links.plane_gather(foreign)
    tail = jnp.concatenate(
        [*(cross_weight[layer, :, main:].T for layer in range(layers)), cross_bias], axis=0
    )
    tail = jnp.pad(tail, ((0, round_up(tail.shape[0], 16) - tail.shape[0]), (0, round_up(shard, LANES) - shard)))
    tails = jnp.stack([tail, *links.cross_swap(lambda step: tail)])
    tails = jnp.stack([lax.dynamic_index_in_dim(tails, block ^ place, keepdims=False) for block in range(ways)])
    bias = jnp.concatenate(
        [tails[block, layers * extra : layers * extra + layers, :shard] for block in range(ways)], axis=1
    ).astype(F32)

    ids_t = feature_ids.T
    emb_rows = round_up(emb_end + 1, 8)
    table_t = jnp.pad(emb_table.T.astype(F32), ((0, emb_rows - emb_end), (0, 0)))
    local_ids = ids_t - place * rows_here
    looked = pl.pallas_call(
        functools.partial(lookup_kernel, fields=fields, emb=emb, ways=ways),
        out_shape=[Shape((emb_rows, rows), BF16)] * ways,
        in_specs=[IN_SMEM, IN_VMEM, IN_VMEM],
        out_specs=[IN_VMEM] * ways,
        scratch_shapes=[pltpu.VMEM((emb_rows, group), F32)],
        compiler_params=params(),
        name="lookup",
    )(at, table_t, local_ids)
    parts = [looked[0], *links.cross_swap(lambda step: looked[step])]

    own_ids = lax.dynamic_slice_in_dim(ids_t, place * rows, rows, 1)
    slots = max((one * wide + wide - 1) // emb - (one * wide) // emb + 1 for one in range(CHIPS))
    slot_ids = jnp.stack(
        [own_ids[jnp.array([min((one * wide) // emb + slot, fields - 1) for slot in range(slots)])] for one in range(CHIPS)]
    )
    ids_for = lambda step: lax.dynamic_index_in_dim(slot_ids, chip ^ step, keepdims=False)
    chip_ids = jnp.concatenate([ids_for(0), *links.chips_swap(ids_for)], axis=1)

    counted = pl.pallas_call(
        functools.partial(count_kernel, fields=fields),
        out_shape=Shape((fields, rows_here), jnp.int32),
        in_specs=[IN_VMEM],
        out_specs=IN_VMEM,
        compiler_params=params(),
        name="count",
    )(local_ids)
    for bit in range(links.dp_size.bit_length() - 1):
        counted = counted + links.over_dp(counted, 1 << bit)
    row_counts = counted.T

    own_dense = lax.dynamic_slice_in_dim(dense_input, place * rows, rows, 0)
    dense_t = jnp.pad(own_dense.T.astype(F32), ((0, round_up(dense_width, 8) - dense_width), (0, 0)))
    tower_rows = round_up(2 * (hidden // ways) + extra // ways, 16)
    turned_rows = round_up(full, LANES)
    weight_scratch = pltpu.VMEM((ways, layers, shard, main), BF16)
    copy_sems = pltpu.SemaphoreType.DMA((1 + 2 * CHIPS * (ways - 1),))
    first, lows, mixes, top_grad, logits, tower_keep, tower_send, small = pl.pallas_call(
        functools.partial(forward_kernel, ways=ways, emb_end=emb_end, scale=scale),
        out_shape=[
            Shape((rows, full), BF16),
            Shape((layers, rows, full), BF16),
            Shape((layers, rows, full), F32),
            Shape((rows, full), BF16),
            Shape((rows, 1), F32),
            Shape((CHIPS, ways, tower_rows, LANES), F32),
            Shape((CHIPS, ways, tower_rows, LANES), BF16),
            Shape((8, turned_rows), F32),
        ],
        in_specs=[IN_SMEM, *[IN_VMEM] * (ways + 1), *[IN_PLACE] * (1 + 2 * CHIPS), *[IN_VMEM] * 9],
        out_specs=[IN_VMEM] * 8,
        scratch_shapes=[
            weight_scratch,
            pltpu.VMEM((turned_rows, rows), F32),
            pltpu.VMEM((rows, full), F32),
            pltpu.VMEM((rows, full), F32),
            copy_sems,
        ],
        compiler_params=params(),
        name="forward",
    )(
        at,
        *parts,
        dense_t,
        cross_weight,
        *pieces,
        tails,
        bias,
        tower_one,
        bias_one[None, :],
        tower_two,
        bias_two[None, :],
        out_weight[None, :],
        out_bias[None, :],
        labels.astype(F32)[:, None],
    )
    tower_sum = links.scatter_sum(tower_keep, tower_send).astype(BF16)
    tower_all = jnp.stack([tower_sum, *links.cross_swap(lambda step: tower_sum)])
    tower_one_grad, tower_two_grad = pl.pallas_call(
        functools.partial(tower_kernel, ways=ways),
        out_shape=[Shape((full, hidden), F32), Shape((hidden, hidden), F32)],
        in_specs=[IN_SMEM, *[IN_VMEM] * (2 * CHIPS)],
        out_specs=[IN_VMEM] * 2,
        compiler_params=params(),
        name="towers",
    )(at, *links.plane_gather(tower_all))

    cross_rows = layers * gap + extra
    cross_keep, cross_send, emb_send, dense_grad, sums = pl.pallas_call(
        functools.partial(backward_kernel, ways=ways, gap=gap, dense_at=emb_end),
        out_shape=[
            Shape((CHIPS, ways, cross_rows, LANES), F32),
            Shape((CHIPS, ways, cross_rows, LANES), BF16),
            Shape((CHIPS, wide, rows), BF16),
            Shape((rows, dense_width), F32),
            Shape((8, turned_rows), F32),
        ],
        in_specs=[IN_SMEM, *[IN_PLACE] * (1 + 2 * CHIPS), *[IN_VMEM] * 5],
        out_specs=[IN_VMEM] * 5,
        scratch_shapes=[
            weight_scratch,
            pltpu.VMEM((turned_rows, rows), F32),
            pltpu.VMEM((layers, rows, main), F32),
            pltpu.VMEM((layers, ways, gap, rows), BF16),
            pltpu.VMEM((ways, extra, main), F32),
            copy_sems,
        ],
        compiler_params=params(),
        name="backward",
    )(at, cross_weight, *pieces, tails, first, lows, mixes, top_grad)

    half = rows_here // LOW_ROWS // 2
    emb_parts = [emb_send[0], *links.chips_swap(lambda step: emb_send[step])]
    table_keep, table_send = pl.pallas_call(
        functools.partial(scatter_kernel, ways=ways, emb=emb),
        out_shape=[Shape((ways, half, wide, LOW_ROWS), F32), Shape((ways, half, wide, LOW_ROWS), BF16)],
        in_specs=[IN_SMEM, *[IN_VMEM] * (CHIPS + 1)],
        out_specs=[IN_VMEM] * 2,
        scratch_shapes=[
            pltpu.VMEM((MARGIN + wide + 64, rows * CHIPS), F32),
            pltpu.VMEM((ways * 2 * half, MARGIN + wide + 64, LOW_ROWS), F32),
        ],
        compiler_params=params(),
        name="scatter",
    )(at, *emb_parts, chip_ids)
    held = table_keep + links.over_dp(table_send, links.core).astype(F32)
    held = links.add_others(held)
    got = links.cross_swap(lambda step: held[step].astype(BF16))
    turned = pl.pallas_call(
        turn_kernel,
        out_shape=Shape((half, LOW_ROWS, wide), BF16),
        in_specs=[IN_VMEM] * ways,
        out_specs=IN_VMEM,
        compiler_params=params(),
        name="turn",
    )(held[0], *got)
    table_grad = pl.pallas_call(
        table_kernel,
        out_shape=Shape((rows_here, emb_end), F32),
        in_specs=[IN_SMEM, *[IN_VMEM] * (2 * CHIPS)],
        out_specs=IN_VMEM,
        compiler_params=params(),
        name="table",
    )(at, *links.plane_gather(turned))

    cross_sum = links.scatter_sum(cross_keep, cross_send).astype(BF16)
    cross_weight_grad = pl.pallas_call(
        functools.partial(cross_kernel, gap=gap),
        out_shape=Shape((layers, shard, full), F32),
        in_specs=[IN_SMEM, *[IN_VMEM] * (2 * CHIPS)],
        out_specs=IN_VMEM,
        scratch_shapes=[pltpu.VMEM((LANES, main), F32)],
        compiler_params=params(),
        name="cross",
    )(at, *links.plane_gather(cross_sum))

    small = links.everywhere(small + sums)
    cross_bias_grad = lax.dynamic_slice_in_dim(small[4 : 4 + layers], place * shard, shard, 1)
    return (
        small[7, 0],
        logits[:, 0],
        dense_grad,
        table_grad,
        cross_weight_grad,
        cross_bias_grad,
        tower_one_grad,
        small[0, :hidden],
        tower_two_grad,
        small[1, :hidden],
        jnp.concatenate([small[2, :full], small[3, :hidden]]),
        small[7, 1:2],
        row_counts,
    )


def solution(mesh):
    in_specs = (
        P("cross", None),
        P("dp", None),
        P("dp", None),
        P(("dp", "cross")),
        P(None, "cross", None),
        P(None, "cross"),
        P(),
        P(),
        P(),
        P(),
        P(),
        P(),
    )
    out_specs = (
        P(),
        P(("dp", "cross")),
        P(("dp", "cross"), None),
        P("cross", None),
        P(None, "cross", None),
        P(None, "cross"),
        P(),
        P(),
        P(),
        P(),
        P(),
        P(),
        P("cross", None),
    )
    return jax.shard_map(body, mesh=mesh, in_specs=in_specs, out_specs=out_specs, check_vma=False)
```

```python
import collections
import functools
import math

import jax
import jax.numpy as jnp
from jax import lax
from jax.experimental import pallas as pl
from jax.experimental.pallas import tpu as pltpu
from jax.sharding import PartitionSpec as P

F32 = jnp.float32
BF16 = jnp.bfloat16
ROWS_IN_ROWS = (((0,), (0,)), ((), ()))
LANES_IN_LANES = (((1,), (1,)), ((), ()))
LANES = 128
LOW_BITS = 8
LOW_ROWS = 1 << LOW_BITS
CHIPS = 4
MARGIN = 48
STEP_SPARE = 24 << 20
SPARE_BYTES = collections.defaultdict(lambda: 3 << 20, step=STEP_SPARE)
COST = 3.45e+09
MICROS = dict(
    lookup=7.4,
    count=5.2,
    step=23,
    tower_products=5.9,
    scatter=7,
    cross_products=8.9,
    tower_first=3.1,
    tower_second=2.3,
    table_fold=2,
    tower_fold=1.8,
    cross_first=4,
    cross_second=2.7,
    cross_fold=1.9,
    table=3.9,
    towers=6.8,
    cross=3.6,
)
IN_VMEM = pl.BlockSpec(memory_space=pltpu.VMEM)
IN_SMEM = pl.BlockSpec(memory_space=pltpu.SMEM)
IN_PLACE = pl.BlockSpec(memory_space=pl.ANY)
Shape = jax.ShapeDtypeStruct


def round_up(size, step):
    return -(-size // step) * step


def dot(left, right, dims=(((1,), (0,)), ((), ()))):
    return lax.dot_general(left, right, dims, preferred_element_type=F32)


def silu_slope(pre_act):
    sigmoid_part = jax.nn.sigmoid(pre_act)
    return sigmoid_part * (1.0 + pre_act * (1.0 - sigmoid_part))


def lookup_kernel(at, table, ids, out, floats, gathered, *, fields, emb):
    ways = out.shape[0]
    highs = table.shape[1] // LOW_ROWS
    group = ids.shape[1]
    part = group // ways
    slab = emb + 1
    floats[pl.ds(0, table.shape[0]), :] = table[...].astype(F32)
    low_iota = lax.broadcasted_iota(jnp.int32, (LOW_ROWS, group), 0)
    for field in range(fields):
        left = jnp.concatenate(
            [floats[pl.ds(field * emb, slab), pl.ds(high * LOW_ROWS, LOW_ROWS)] for high in range(highs)], axis=0
        ).astype(BF16)
        local = ids[pl.ds(field, 1), :] - at[0] * (highs * LOW_ROWS)
        low = jnp.bitwise_and(local, LOW_ROWS - 1)
        high_id = jnp.right_shift(local, LOW_BITS)
        hot = jnp.where(low_iota == low, 1.0, 0.0).astype(BF16)
        picked = dot(left, hot)
        total = jnp.zeros((slab, group), F32)
        for high in range(highs):
            total = total + jnp.where(high_id == high, picked[high * slab : (high + 1) * slab], 0.0)
        gathered[pl.ds(field * emb, slab), :] = total
    for block in range(ways):
        out[block] = gathered[:, pl.ds(block * part, part)].astype(BF16)


def count_kernel(at, ids, after, out, *, fields):
    highs = out.shape[1] // LOW_ROWS
    group = ids.shape[1]
    low_iota = lax.broadcasted_iota(jnp.int32, (LOW_ROWS, group), 0)
    high_iota = lax.broadcasted_iota(jnp.int32, (8, group), 0)
    for field in range(fields):
        local = ids[pl.ds(field, 1), :] - at[0] * (highs * LOW_ROWS)
        low = jnp.bitwise_and(local, LOW_ROWS - 1)
        hot = jnp.where(low_iota == low, 1.0, 0.0).astype(BF16)
        marks = jnp.where(high_iota == jnp.right_shift(local, LOW_BITS), 1.0, 0.0).astype(BF16)
        got = dot(marks, hot, LANES_IN_LANES)
        for high in range(highs):
            out[pl.ds(field, 1), pl.ds(high * LOW_ROWS, LOW_ROWS)] = got[high : high + 1].astype(jnp.int32)


def column_of(at, rel):
    return pl.multiple_of(((at[1] ^ (rel // 2)) * 2 + (at[2] ^ (rel % 2))) * LANES, LANES)


def column_pick(at, values, mine):
    first = at[2] == 0 if mine else at[2] == 1
    blocks = []
    for one in range(CHIPS):
        low, high = values[:, 2 * one * LANES : (2 * one + 1) * LANES], values[:, (2 * one + 1) * LANES : (2 * one + 2) * LANES]
        blocks.append(jnp.where(first, low, high))
    picked = jnp.concatenate(blocks, axis=1).astype(BF16)
    rows = values.shape[0]
    return [picked[:, begin : begin + rows] for begin in range(0, CHIPS * LANES, rows)]


def step_kernel(at, *refs, shard, emb_end, scale, waits):
    refs = list(refs)
    take = lambda count: [refs.pop(0) for _ in range(count)]
    (parts, dense_t, own, own_tail), pieces = take(4), take(2 * CHIPS)
    one_w, one_b, two_w, two_b, out_w, out_b, labels = take(7)
    take(waits)
    (logits_out, small, dense_grad), emb_send = take(3), take(CHIPS)
    tower_other, tower_mine, cross_other, cross_mine = take(4)
    weights, tails, bias, turned, first, state, lows, mixes, sems = take(9)
    place = at[0]
    ways, layers, gap, main = weights.shape
    rows = parts.shape[2]
    full = first.shape[1]
    extra = full - main
    hidden = one_w.shape[1]
    blocks = -(-shard // LANES)
    copies = [pltpu.make_async_copy(own, weights.at[place], sems.at[0])]
    for rel, piece in enumerate(pieces):
        for step in range(1, ways):
            target = weights.at[place ^ step, :, :, pl.ds(column_of(at, rel), LANES)]
            copies.append(pltpu.make_async_copy(piece.at[step - 1], target, sems.at[len(copies)]))
    for copy in copies:
        copy.start()
    looked = parts[0].astype(F32)
    for block in range(1, ways):
        looked = looked + parts[block].astype(F32)
    turned[pl.ds(0, looked.shape[0]), :] = looked
    turned[pl.ds(emb_end, dense_t.shape[0]), :] = dense_t[...]
    used = emb_end + dense_t.shape[0]
    turned[pl.ds(used, turned.shape[0] - used), :] = jnp.zeros((turned.shape[0] - used, rows), F32)
    start = turned[...].T[:, :full]
    first[...] = start
    state[...] = start
    for copy in copies:
        copy.wait()
    for block in range(ways):
        for layer in range(layers):
            ends = weights[block, layer, pl.ds(gap - 16, 16), :].astype(F32)[8:]
            for one in range(2 * CHIPS):
                tails[block, layer, pl.ds(8 * one, 8), :] = ends[:, one * LANES : (one + 1) * LANES]
    tails[place] = own_tail[...].astype(F32)
    for block in range(ways):
        for layer in range(layers):
            row = jnp.concatenate(
                [tails[block, layer, pl.ds(blocks * extra + one, 1), :] for one in range(blocks)], axis=1
            )
            bias[pl.ds(layer, 1), pl.ds(block * shard, shard)] = row[:, :shard]

    def tail_of(block, layer):
        pieces = [tails[block, layer, pl.ds(one * extra, extra), :] for one in range(blocks)]
        return jnp.concatenate(pieces, axis=1)[:, :shard].astype(BF16)

    @pl.loop(0, layers)
    def _(layer):
        low = state[...].astype(BF16)
        lows[layer] = low
        body = jnp.zeros((rows, main), F32)
        edge = jnp.zeros((rows, extra), F32)
        for block in range(ways):
            chunk = low[:, shard * block : shard * (block + 1)]
            body = body + dot(chunk, weights[block, layer, pl.ds(0, shard), :])
            edge = edge + dot(chunk, tail_of(block, layer), LANES_IN_LANES)
        mixed = jnp.concatenate([body, edge], axis=1) + bias[pl.ds(layer, 1), :full]
        mixes[layer] = mixed
        state[...] = first[...] * mixed + state[...]

    top = state[...].astype(BF16)
    hid_one = dot(top, one_w[...]) + one_b[...]
    act_one = jax.nn.silu(hid_one).astype(BF16)
    hid_two = dot(act_one, two_w[...]) + two_b[...]
    act_two = jax.nn.silu(hid_two).astype(BF16)
    top_float, act_float = top.astype(F32), act_two.astype(F32)
    weight_top = out_w[:, :full].astype(F32)
    weight_act = out_w[:, full:].astype(F32)
    logits = (
        jnp.sum(top_float * weight_top, axis=1, keepdims=True)
        + jnp.sum(act_float * weight_act, axis=1, keepdims=True)
        + out_b[...]
    )
    logits_out[...] = jnp.broadcast_to(logits, (rows, LANES)).T[:1]
    label = jnp.broadcast_to(labels[...].astype(F32), (LANES, rows)).T[:, :1]
    loss = jnp.sum(jax.nn.softplus(logits) - label * logits, axis=0, keepdims=True) * scale
    g_logit = ((jax.nn.sigmoid(logits) - label) * scale).astype(BF16).astype(F32)
    g_two = (g_logit * weight_act * silu_slope(hid_two)).astype(BF16)
    g_one = (dot(g_two, two_w[...], LANES_IN_LANES) * silu_slope(hid_one)).astype(BF16)
    grad = (dot(g_one, one_w[...], LANES_IN_LANES) + g_logit * weight_top).astype(BF16).astype(F32)
    one_float, two_float = g_one.astype(F32), g_two.astype(F32)
    lane = lax.broadcasted_iota(jnp.int32, (1, LANES), 1)
    bias_grad = jnp.sum(g_logit, axis=0, keepdims=True)
    small[...] = jnp.zeros_like(small)
    small[pl.ds(0, 1), pl.ds(0, hidden)] = jnp.sum(one_float, axis=0, keepdims=True)
    small[pl.ds(1, 1), pl.ds(0, hidden)] = jnp.sum(two_float, axis=0, keepdims=True)
    small[pl.ds(2, 1), pl.ds(0, full)] = jnp.sum(top_float * g_logit, axis=0, keepdims=True)
    small[pl.ds(3, 1), pl.ds(0, hidden)] = jnp.sum(act_float * g_logit, axis=0, keepdims=True)
    small[pl.ds(7, 1), pl.ds(0, LANES)] = jnp.where(lane == 0, loss, jnp.where(lane == 1, bias_grad, 0.0))
    tower_other[pl.ds(0, full), :] = top_float.T.astype(BF16)
    tower_other[pl.ds(full, hidden), :] = act_one.astype(F32).T.astype(BF16)
    base = round_up(full + hidden, 16)
    span = CHIPS * LANES
    for which, values in enumerate((one_float, two_float)):
        for index, block in enumerate(column_pick(at, values, False)):
            tower_other[pl.ds(base + which * span + index * rows, rows), :] = block
        for index, block in enumerate(column_pick(at, values, True)):
            tower_mine[pl.ds(which * span + index * rows, rows), :] = block

    inputs = first[...]
    pad = jnp.zeros((rows, turned.shape[0] - full), F32)
    total = jnp.zeros_like(grad)
    low_rows = layers * ways * gap
    base = low_rows + layers * extra
    for layer in reversed(range(layers)):
        rounded = (grad * inputs).astype(BF16)
        values = rounded.astype(F32)
        small[pl.ds(4 + layer, 1), pl.ds(0, full)] = jnp.sum(values, axis=0, keepdims=True)
        total = total + grad * mixes[layer]
        backs = []
        for block in range(ways):
            back = dot(rounded[:, :main], weights[block, layer, pl.ds(0, shard), :], LANES_IN_LANES)
            backs.append(back + dot(rounded[:, main:full], tail_of(block, layer)))
        grad = grad + jnp.concatenate(backs, axis=1)
        for index, block in enumerate(column_pick(at, values, False)):
            cross_other[pl.ds(base + layer * span + index * rows, rows), :] = block
        for index, block in enumerate(column_pick(at, values, True)):
            cross_mine[pl.ds(layer * span + index * rows, rows), :] = block
        edge = jnp.concatenate([values[:, main:full], jnp.zeros((rows, LANES - extra), F32)], axis=1).T
        cross_other[pl.ds(low_rows + layer * extra, extra), :] = edge[:extra].astype(BF16)
        turned[...] = jnp.concatenate([lows[layer].astype(F32), pad], axis=1).T
        for block in range(ways):
            low_t = jnp.concatenate([turned[pl.ds(block * shard, shard), :], jnp.zeros((gap - shard, rows), F32)], axis=0)
            cross_other[pl.ds((layer * ways + block) * gap, gap), :] = low_t.astype(BF16)
    total = total + grad
    turned[...] = jnp.concatenate([total, pad], axis=1).T
    dense_grad[...] = turned[pl.ds(emb_end, dense_grad.shape[0]), :]
    wide = 2 * LANES
    for step in range(CHIPS):
        emb_send[step][...] = turned[pl.ds(pl.multiple_of((at[1] ^ step) * wide, wide), wide), :].astype(BF16)


def both_cores(at, mine, theirs, start, which, step, rows):
    begin = (at[1] ^ step) * LANES
    lanes = pl.ds(pl.multiple_of(begin % rows, LANES), LANES)
    row = pl.multiple_of(which * CHIPS * LANES + begin // rows * rows, LANES)
    return jnp.concatenate([mine[pl.ds(row, rows), lanes], theirs[pl.ds(start + row, rows), lanes]], axis=0)


def halves(refs, ways):
    keep_one, send_one, keep_two, send_two = refs
    half = ways // 2

    def place_of(step, block):
        if block < half:
            return (send_one if step & 1 else keep_one), (step >> 1, block)
        return (send_two if step & 2 else keep_two), (step & 1, block - half)

    return place_of


def tower_product_kernel(at, sent, mine, theirs, *refs, full, hidden):
    refs = refs[-CHIPS:]
    ways = 2 * refs[0].shape[1]
    place_of = halves(refs, ways)
    rows = mine.shape[1]
    part = hidden // ways
    ends = (full - hidden) // ways
    last = refs[0].shape[2] - 2 * part
    base = round_up(full + hidden, 16)
    top_t = jnp.concatenate([sent[pl.ds(0, full), :], theirs[pl.ds(0, full), :]], axis=1)
    act_t = jnp.concatenate([sent[pl.ds(full, hidden), :], theirs[pl.ds(full, hidden), :]], axis=1)
    for step in range(CHIPS):
        one = dot(top_t, both_cores(at, mine, theirs, base, 0, step, rows))
        two = dot(act_t, both_cores(at, mine, theirs, base, 1, step, rows))
        for block in range(ways):
            own_rows = slice(block * part, (block + 1) * part)
            out, where = place_of(step, block)
            out[*where, pl.ds(0, part), :] = one[own_rows].astype(out.dtype)
            out[*where, pl.ds(part, part), :] = two[own_rows].astype(out.dtype)
            rest = one[hidden + block * ends : hidden + (block + 1) * ends]
            rest = jnp.concatenate([rest, jnp.zeros((last - ends, LANES), F32)], axis=0)
            out[*where, pl.ds(2 * part, last), :] = rest.astype(out.dtype)


def cross_product_kernel(at, sent, mine, theirs, *refs, layers, shard, gap):
    pack = refs[-1]
    ways, extra = pack.shape[0], pack.shape[1]
    place_of = halves(refs[-CHIPS - 1 : -1], ways)
    rows = mine.shape[1]
    low_rows = layers * ways * gap
    base = low_rows + layers * extra
    pack[...] = jnp.zeros_like(pack)

    def lows(layer, block):
        own_rows = pl.ds((layer * ways + block) * gap, gap)
        return jnp.concatenate([sent[own_rows, :], theirs[own_rows, :]], axis=1)

    for layer in range(layers):
        own_rows = pl.ds(low_rows + layer * extra, extra)
        edge = jnp.concatenate([sent[own_rows, :], theirs[own_rows, :]], axis=1)
        for block in range(ways):
            product = dot(edge, lows(layer, block), LANES_IN_LANES)
            pack[block, :, pl.ds(layer * shard, shard)] = product[:, :shard]
    for step in range(CHIPS):
        for layer in range(layers):
            columns = both_cores(at, mine, theirs, base, layer, step, rows)
            for block in range(ways):
                out, where = place_of(step, block)
                out[*where, pl.ds(layer * gap, gap), :] = dot(lows(layer, block), columns).astype(out.dtype)
        for block in range(ways):
            out, where = place_of(step, block)
            lanes = pl.ds(column_of(at, 2 * step), LANES)
            out[*where, pl.ds(layers * gap, extra), :] = pack[block, :, lanes].astype(out.dtype)


def scatter_kernel(at, sent, theirs, ids, *refs, emb):
    out, spread, table, columns = refs[-4:]
    chip, core = at[1], at[2]
    _, wide, part = sent.shape
    group = 2 * CHIPS * part
    ways, half = out.shape[0], out.shape[1]
    fields = ids.shape[1]
    slab = emb + 1
    spread[pl.ds(0, MARGIN), :] = jnp.zeros((MARGIN, group), F32)
    spread[pl.ds(MARGIN + wide, 64), :] = jnp.zeros((64, group), F32)
    pad = jnp.zeros((LANES - fields, part), F32)
    for rel in range(2 * CHIPS):
        values = (theirs if rel % 2 else sent)[rel // 2]
        spread[pl.ds(MARGIN, wide), pl.ds(rel * part, part)] = values.astype(F32)
        low = jnp.bitwise_and(ids[rel], LOW_ROWS - 1).astype(F32)
        columns[pl.ds(rel * part, part), :] = jnp.concatenate([low, pad], axis=0).T
    low_iota = lax.broadcasted_iota(jnp.int32, (group, LOW_ROWS), 1).astype(F32)
    for mine in range(CHIPS):

        @pl.when(chip == mine)
        def _(mine=mine):
            first_field = (mine * wide) // emb
            for field in range(first_field, min(fields, (mine * wide + wide - 1) // emb + 1)):
                begin = field * emb - mine * wide + MARGIN
                values = spread[pl.ds(begin, slab), :]
                this = jnp.concatenate([ids[rel, pl.ds(field, 1), :] for rel in range(2 * CHIPS)], axis=1)
                high_id = jnp.right_shift(this, LOW_BITS) - core * half
                hot = jnp.where(low_iota == columns[:, field : field + 1], 1.0, 0.0).astype(BF16)
                stacked = jnp.concatenate(
                    [
                        jnp.where(high_id == block * 2 * half + piece, values, 0.0)
                        for block in range(ways)
                        for piece in range(half)
                    ],
                    axis=0,
                ).astype(BF16)
                got = dot(stacked, hot)
                for high in range(ways * half):
                    table[high, pl.ds(begin, emb), :] = got[high * slab : high * slab + emb]

    for block in range(ways):
        for piece in range(half):
            out[block, piece] = table[block * half + piece, pl.ds(MARGIN, wide), :].astype(BF16)


def first_add_kernel(keep_one, got_one, keep_two, got_two, *refs):
    own_one, send_one, own_two, send_two = refs[-4:]
    own_one[...] = keep_one[0] + got_one[0].astype(F32)
    send_one[...] = (keep_one[1] + got_one[1].astype(F32)).astype(BF16)
    own_two[...] = keep_two[0] + got_two[0].astype(F32)
    send_two[...] = (keep_two[1] + got_two[1].astype(F32)).astype(BF16)


def second_add_kernel(at, own_one, got_one, own_two, got_two, *refs, by_step):
    out = refs[-1]
    half = own_one.shape[0]
    flip = at[0] if by_step else 0
    for block in range(half):
        out[block ^ flip] = (own_one[block] + got_one[block].astype(F32)).astype(BF16)
        out[(half + block) ^ flip] = (own_two[block] + got_two[block].astype(F32)).astype(BF16)


def add_kernel(*refs, count):
    total = refs[0][...].astype(F32)
    for other in refs[1:count]:
        total = total + other[...].astype(F32)
    refs[-1][...] = total.astype(refs[-1].dtype)


def fold_kernel(parts, *refs):
    total = parts[0].astype(F32)
    for block in range(1, parts.shape[0]):
        total = total + parts[block].astype(F32)
    refs[-1][...] = total.astype(refs[-1].dtype)


def table_kernel(at, *refs):
    pieces, out = refs[: 2 * CHIPS], refs[-1]
    half, wide, low = pieces[0].shape
    last = CHIPS - 1
    for rel, piece in enumerate(pieces):
        chip = at[1] ^ (rel // 2)
        core = at[2] ^ (rel % 2)
        for block in range(half):
            lanes = pl.ds(pl.multiple_of((core * half + block) * low, low), low)
            values = piece[block].astype(F32)

            @pl.when(chip < last)
            def _(lanes=lanes, values=values, chip=chip):
                out[pl.ds(pl.multiple_of(chip * wide, wide), wide), lanes] = values

            @pl.when(chip == last)
            def _(lanes=lanes, values=values):
                height = out.shape[0] - last * wide
                out[pl.ds(last * wide, height), lanes] = values[:height]


def tower_kernel(at, *refs):
    pieces, (one_out, two_out) = refs[: 2 * CHIPS], refs[-2:]
    ways = pieces[0].shape[0]
    hidden = two_out.shape[0]
    part = hidden // ways
    ends = (one_out.shape[0] - hidden) // ways
    for rel, piece in enumerate(pieces):
        lanes = pl.ds(column_of(at, rel), LANES)
        for block in range(ways):
            source = block ^ at[0]
            one_out[pl.ds(block * part, part), lanes] = piece[source, pl.ds(0, part), :].astype(F32)
            two_out[pl.ds(block * part, part), lanes] = piece[source, pl.ds(part, part), :].astype(F32)
            rest = piece[source, pl.ds(2 * part, 16), :].astype(F32)
            one_out[pl.ds(hidden + block * ends, ends), lanes] = rest[:ends]


def cross_kernel(at, *refs, gap):
    pieces, out, pack = refs[: 2 * CHIPS], refs[-2], refs[-1]
    layers, shard, full = out.shape
    main = pack.shape[1]
    extra = full - main
    for rel, piece in enumerate(pieces):
        lanes = pl.ds(column_of(at, rel), LANES)
        for layer in range(layers):
            out[layer, :, lanes] = piece[pl.ds(layer * gap, gap), :].astype(F32)[:shard]
        pack[pl.ds(0, extra), lanes] = piece[pl.ds(layers * gap, extra), :].astype(F32)
    pack[pl.ds(extra, pack.shape[0] - extra), :] = jnp.zeros((pack.shape[0] - extra, main), F32)
    turned = pack[...].T
    for layer in range(layers):
        out[layer, :, pl.ds(main, extra)] = turned[layer * shard : (layer + 1) * shard, :extra]


def vmem_bytes(one):
    *lead, rows, lanes = one.shape
    size = jnp.dtype(one.dtype).itemsize
    return math.prod(lead) * round_up(rows, 32 // size) * round_up(lanes, LANES) * size


def local(kernel, out_shape, operands, after=(), scratch=(), in_place=(), name=None, **options):
    operands = list(operands)
    smem = [index for index, one in enumerate(operands) if one.shape == (3,)]
    specs = [
        IN_SMEM if index in smem else IN_PLACE if index in in_place else IN_VMEM for index in range(len(operands))
    ]
    outs = out_shape if isinstance(out_shape, list) else [out_shape]
    held = [one for index, one in enumerate(operands) if index not in (*smem, *in_place)] + outs
    held += [one for one in scratch if len(one.shape) > 1]
    space = sum(vmem_bytes(one) for one in held) + SPARE_BYTES[name]
    got = pl.pallas_call(
        functools.partial(kernel, **options),
        out_shape=outs,
        in_specs=specs + [IN_PLACE] * len(after),
        out_specs=[IN_VMEM] * len(outs),
        scratch_shapes=list(scratch),
        compiler_params=pltpu.CompilerParams(vmem_limit_bytes=space),
        cost_estimate=pl.CostEstimate(flops=int(COST * MICROS[name]), bytes_accessed=0, transcendentals=0),
        name=name,
    )(*operands, *after)
    return got if isinstance(out_shape, list) else got[0]


class Links:
    def __init__(self, dp_size, cross_size):
        bits = dp_size.bit_length() - 1
        axis_bits = (bits - 1) // 2
        self.dp_size, self.cross_size = dp_size, cross_size
        self.core = 1
        self.chip_masks = (1 << 1, 1 << (1 + axis_bits))
        used = (self.core, *self.chip_masks)
        self.others = tuple(1 << bit for bit in range(bits) if 1 << bit not in used)

    def chip_mask(self, step):
        return sum(mask for bit, mask in enumerate(self.chip_masks) if step >> bit & 1)

    def chip(self, dp_place):
        return sum((dp_place // mask % 2) << bit for bit, mask in enumerate(self.chip_masks))

    def over_dp(self, value, mask):
        return lax.ppermute(value, "dp", [(one, one ^ mask) for one in range(self.dp_size)])

    def over_cross(self, value, mask):
        return lax.ppermute(value, "cross", [(one, one ^ mask) for one in range(self.cross_size)])

    def chips_swap(self, value_of):
        return [self.over_dp(value_of(step), self.chip_mask(step)) for step in range(1, CHIPS)]

    def cross_swap(self, value_of):
        return [self.over_cross(value_of(step), step) for step in range(1, self.cross_size)]

    def cross_exchange(self, value):
        return lax.all_to_all(value, "cross", split_axis=0, concat_axis=0, tiled=True)

    def add_others(self, value):
        for mask in self.others:
            value = (value.astype(F32) + self.over_dp(value, mask).astype(F32)).astype(BF16)
        return value

    def hops(self):
        def over(send, mask):
            def hop(value, *after):
                got = send(value, mask)
                value, got, *_ = lax.optimization_barrier((value, got, *after))
                return value + got

            return hop

        plane = [over(self.over_dp, 1 << bit) for bit in range(self.dp_size.bit_length() - 1)]
        return plane + [over(self.over_cross, 1 << bit) for bit in range(self.cross_size.bit_length() - 1)]

    def plane_first(self, parts, shape, after, name):
        keep_one, send_one, keep_two, send_two = parts
        one, two = self.chip_masks
        got_one, got_two = self.over_dp(send_one, one), self.over_dp(send_two, two)
        part = Shape((shape[0] // 2, *shape[1:]), F32)
        low = Shape(part.shape, BF16)
        return local(first_add_kernel, [part, low, part, low], [keep_one, got_one, keep_two, got_two], after, name=name)

    def plane_second(self, parts, shape, at, by_step, after, name):
        own_one, send_one, own_two, send_two = parts
        one, two = self.chip_masks
        got_one, got_two = self.over_dp(send_one, two), self.over_dp(send_two, one)
        total = local(
            second_add_kernel,
            Shape(shape, BF16),
            [at, own_one, got_one, own_two, got_two],
            after,
            name=name,
            by_step=by_step,
        )
        return self.add_others(total)

    def both_cores(self, arrays):
        return [each for one in arrays for each in (one, self.over_dp(one, self.core))]

    def plane_gather(self, value):
        return self.both_cores([value, *self.chips_swap(lambda step: value)])


def body(
    emb_table,
    dense_input,
    feature_ids,
    labels,
    cross_weight,
    cross_bias,
    tower_one,
    bias_one,
    tower_two,
    bias_two,
    out_weight,
    out_bias,
):
    layers, shard, full = cross_weight.shape
    group, fields = feature_ids.shape
    rows_here, emb_end = emb_table.shape
    emb = emb_end // fields
    dense_width = dense_input.shape[1]
    hidden = tower_one.shape[1]
    main = hidden
    extra = full - main
    ways = lax.axis_size("cross")
    place = lax.axis_index("cross")
    dp_place = lax.axis_index("dp")
    links = Links(lax.axis_size("dp"), ways)
    rows = group // ways
    scale = 1.0 / (group * links.dp_size)
    chip, core = links.chip(dp_place), dp_place % 2
    at = jnp.stack([place, chip, core]).astype(jnp.int32)
    wide = 2 * LANES
    gap = round_up(shard + 8, 16)

    blocks = -(-shard // LANES)
    ends = jnp.pad(cross_weight[:, :, main:].transpose(0, 2, 1), ((0, 0), (0, 0), (0, blocks * LANES - shard)))
    ends = ends.reshape(layers, extra, blocks, LANES).transpose(0, 2, 1, 3).reshape(layers, blocks * extra, LANES)
    ends_bias = jnp.pad(cross_bias, ((0, 0), (0, blocks * LANES - shard))).reshape(layers, blocks, LANES)
    own_tail = jnp.concatenate([ends, ends_bias], axis=1)
    own_tail = jnp.pad(own_tail, ((0, 0), (0, 64 - own_tail.shape[1]), (0, 0)))
    part = chip * 2 + core
    own_block = jnp.concatenate(
        [
            lax.dynamic_slice_in_dim(cross_weight, part * LANES, LANES, 2),
            jnp.zeros((layers, gap - 8 - shard, LANES), BF16),
            lax.dynamic_slice_in_dim(own_tail, part * 8, 8, 1),
        ],
        axis=1,
    )
    foreign = links.cross_swap(lambda step: own_block)

    ids_t = feature_ids.T
    emb_rows = round_up(emb_end + 1, 8)
    looked = local(
        lookup_kernel,
        Shape((ways, emb_rows, rows), BF16),
        [at, emb_table.T, ids_t],
        scratch=[pltpu.VMEM((emb_rows, rows_here), F32), pltpu.VMEM((emb_rows, group), F32)],
        name="lookup",
        fields=fields,
        emb=emb,
    )
    *foreign, looked = lax.optimization_barrier((*foreign, looked))
    parts = links.cross_exchange(looked)
    foreign = jnp.stack(foreign)
    foreign = [foreign, *links.chips_swap(lambda step: foreign)]

    plane_ids = lax.dynamic_slice_in_dim(ids_t, place * rows, rows, 1)
    plane_ids, _ = lax.optimization_barrier((plane_ids, looked))
    plane_ids = plane_ids[None]
    for mask in (*links.chip_masks, links.core):
        plane_ids = jnp.concatenate([plane_ids, links.over_dp(plane_ids, mask)], axis=0)
    plane_ids = plane_ids.reshape(2, CHIPS, fields, rows).transpose(1, 0, 2, 3).reshape(2 * CHIPS, fields, rows)
    counted = local(count_kernel, Shape((fields, rows_here), jnp.int32), [at, ids_t], [looked], name="count", fields=fields)
    for bit in range(links.dp_size.bit_length() - 1):
        counted = counted + links.over_dp(counted, 1 << bit)

    *foreign, _, _ = lax.optimization_barrier((*foreign, plane_ids, counted))
    pieces = links.both_cores(foreign)

    own_dense = lax.dynamic_slice_in_dim(dense_input.T, place * rows, rows, 1)
    dense_t = jnp.pad(own_dense.astype(F32), ((0, round_up(dense_width, 8) - dense_width), (0, 0)))
    own_full = jnp.pad(cross_weight[:, :, :main], ((0, 0), (0, gap - shard), (0, 0)))
    turned_rows = round_up(full, LANES)
    tower_factors = round_up(full + hidden, 16)
    cross_factors = layers * (ways * gap + extra)
    logits, small, dense_grad, *emb_send, tower_other, tower_mine, cross_other, cross_mine = local(
        step_kernel,
        [
            Shape((1, rows), F32),
            Shape((8, turned_rows), F32),
            Shape((dense_width, rows), F32),
            *[Shape((wide, rows), BF16)] * CHIPS,
            Shape((tower_factors + 2 * CHIPS * LANES, rows), BF16),
            Shape((2 * CHIPS * LANES, rows), BF16),
            Shape((cross_factors + layers * CHIPS * LANES, rows), BF16),
            Shape((layers * CHIPS * LANES, rows), BF16),
        ],
        [
            at,
            parts,
            dense_t,
            own_full,
            own_tail,
            *pieces,
            tower_one,
            bias_one[None, :],
            tower_two,
            bias_two[None, :],
            out_weight[None, :],
            out_bias[None, :],
            labels[None, :],
        ],
        [plane_ids, counted],
        [
            pltpu.VMEM((ways, layers, gap, main), BF16),
            pltpu.VMEM((ways, layers, 64, LANES), F32),
            pltpu.VMEM((8, turned_rows), F32),
            pltpu.VMEM((turned_rows, rows), F32),
            pltpu.VMEM((rows, full), F32),
            pltpu.VMEM((rows, full), F32),
            pltpu.VMEM((layers, rows, full), BF16),
            pltpu.VMEM((layers, rows, full), F32),
            pltpu.SemaphoreType.DMA((1 + 2 * CHIPS * (ways - 1),)),
        ],
        in_place=(3, *range(5, 5 + 2 * CHIPS)),
        name="step",
        shard=shard,
        emb_end=emb_end,
        scale=scale,
        waits=2,
    )

    hops = links.hops()
    tower_theirs = links.over_dp(tower_other, links.core)
    cross_theirs = links.over_dp(cross_other, links.core)
    emb_got = links.chips_swap(lambda step: emb_send[step])
    small = hops[0](small)

    tower_rows = round_up(2 * (hidden // ways) + extra // ways, 16)
    tower_shape = (ways, tower_rows, LANES)
    split = lambda shape, kind: Shape((2, shape[0] // 2, *shape[1:]), kind)
    tower_parts = local(
        tower_product_kernel,
        [split(tower_shape, F32), split(tower_shape, BF16)] * 2,
        [at, tower_other, tower_mine, tower_theirs],
        name="tower_products",
        full=full,
        hidden=hidden,
    )

    cross_rows = layers * gap + extra
    cross_shape = (ways, cross_rows, LANES)
    cross_parts = local(
        cross_product_kernel,
        [split(cross_shape, F32), split(cross_shape, BF16)] * 2,
        [at, cross_other, cross_mine, cross_theirs],
        [tower_parts[0]],
        [pltpu.VMEM((ways, extra, main), F32)],
        name="cross_products",
        layers=layers,
        shard=shard,
        gap=gap,
    )
    small = hops[1](small, cross_parts[0])
    tower_first = links.plane_first(tower_parts, tower_shape, [cross_parts[0]], "tower_first")

    emb_parts = jnp.stack([emb_send[0], *emb_got])
    emb_theirs = links.over_dp(emb_parts, links.core)
    half = rows_here // LOW_ROWS // 2
    table_parts = local(
        scatter_kernel,
        Shape((ways, half, wide, LOW_ROWS), BF16),
        [at, emb_parts, emb_theirs, plane_ids],
        [tower_first[0]],
        [
            pltpu.VMEM((MARGIN + wide + 64, rows * 2 * CHIPS), F32),
            pltpu.VMEM((ways * half, MARGIN + wide + 64, LOW_ROWS), F32),
            pltpu.VMEM((rows * 2 * CHIPS, LANES), F32),
        ],
        name="scatter",
        emb=emb,
    )
    small = hops[2](small, table_parts)
    table_got = links.cross_exchange(links.add_others(table_parts))
    tower_sum = links.plane_second(tower_first, tower_shape, at, True, [table_parts], "tower_second")
    tower_got = links.cross_swap(lambda step: tower_sum[step])
    cross_first = links.plane_first(cross_parts, cross_shape, [tower_sum], "cross_first")
    small = hops[3](small, cross_first[0])
    table_fold = local(fold_kernel, Shape((half, wide, LOW_ROWS), BF16), [table_got], [cross_first[0]], name="table_fold")
    table_all = links.plane_gather(table_fold)
    cross_sum = links.plane_second(cross_first, cross_shape, at, False, [table_fold], "cross_second")
    for hop in hops[4:]:
        small = hop(small, cross_sum)
    cross_got = links.cross_exchange(cross_sum)
    tower_fold = local(
        add_kernel, Shape(tower_shape[1:], BF16), [tower_sum[0], *tower_got], [cross_sum], name="tower_fold", count=ways
    )
    tower_all = jnp.stack([tower_fold, *links.cross_swap(lambda step: tower_fold)])
    tower_blocks = links.plane_gather(tower_all)
    table_grad = local(table_kernel, Shape((emb_end, rows_here), F32), [at, *table_all], [tower_fold], name="table")
    cross_fold = local(fold_kernel, Shape(cross_shape[1:], BF16), [cross_got], [table_grad], name="cross_fold")
    tower_one_grad, tower_two_grad = local(
        tower_kernel, [Shape((full, hidden), F32), Shape((hidden, hidden), F32)], [at, *tower_blocks], [cross_fold], name="towers"
    )
    cross_weight_grad = local(
        cross_kernel,
        Shape((layers, shard, full), F32),
        [at, *links.plane_gather(cross_fold)],
        scratch=[pltpu.VMEM((LANES, main), F32)],
        name="cross",
        gap=gap,
    )
    cross_bias_grad = lax.dynamic_slice_in_dim(small[4 : 4 + layers], place * shard, shard, 1)
    return (
        small[7, 0],
        logits[0],
        dense_grad.T,
        table_grad.T,
        cross_weight_grad,
        cross_bias_grad,
        tower_one_grad,
        small[0, :hidden],
        tower_two_grad,
        small[1, :hidden],
        jnp.concatenate([small[2, :full], small[3, :hidden]]),
        small[7, 1:2],
        counted.T,
    )


def solution(mesh):
    in_specs = (
        P("cross", None),
        P("dp", None),
        P("dp", None),
        P(("dp", "cross")),
        P(None, "cross", None),
        P(None, "cross"),
        P(),
        P(),
        P(),
        P(),
        P(),
        P(),
    )
    out_specs = (
        P(),
        P(("dp", "cross")),
        P(("dp", "cross"), None),
        P("cross", None),
        P(None, "cross", None),
        P(None, "cross"),
        P(),
        P(),
        P(),
        P(),
        P(),
        P(),
        P("cross", None),
    )
    return jax.shard_map(body, mesh=mesh, in_specs=in_specs, out_specs=out_specs, check_vma=False)
```

```python
import collections
import functools
import math

import jax
import jax.numpy as jnp
from jax import lax
from jax.experimental import pallas as pl
from jax.experimental.pallas import tpu as pltpu
from jax.sharding import PartitionSpec as P

F32 = jnp.float32
BF16 = jnp.bfloat16
ROWS_IN_ROWS = (((0,), (0,)), ((), ()))
LANES_IN_LANES = (((1,), (1,)), ((), ()))
LANES = 128
LOW_BITS = 8
LOW_ROWS = 1 << LOW_BITS
CHIPS = 4
MARGIN = 48
STEP_SPARE = 8 << 20
SPARE_BYTES = collections.defaultdict(lambda: 3 << 20, step=STEP_SPARE)
COST = 5.75e+09
MICROS = dict(
    lookup=7.4,
    count=5.2,
    step=23,
    tower_products=5.9,
    scatter=7,
    cross_products=8.9,
    tower_first=3.1,
    tower_second=2.3,
    table_fold=2,
    tower_fold=1.8,
    cross_first=4,
    cross_second=2.7,
    cross_fold=1.9,
    table=3.9,
    towers=6.8,
    cross=3.6,
)
IN_VMEM = pl.BlockSpec(memory_space=pltpu.VMEM)
IN_SMEM = pl.BlockSpec(memory_space=pltpu.SMEM)
IN_PLACE = pl.BlockSpec(memory_space=pl.ANY)
Shape = jax.ShapeDtypeStruct


def round_up(size, step):
    return -(-size // step) * step


def dot(left, right, dims=(((1,), (0,)), ((), ()))):
    return lax.dot_general(left, right, dims, preferred_element_type=F32)


def silu_slope(pre_act):
    sigmoid_part = jax.nn.sigmoid(pre_act)
    return sigmoid_part * (1.0 + pre_act * (1.0 - sigmoid_part))


def lookup_kernel(at, table, ids, out, floats, gathered, *, fields, emb):
    ways = out.shape[0]
    highs = table.shape[1] // LOW_ROWS
    group = ids.shape[1]
    part = group // ways
    slab = emb + 1
    floats[pl.ds(0, table.shape[0]), :] = table[...].astype(F32)
    low_iota = lax.broadcasted_iota(jnp.int32, (LOW_ROWS, group), 0)
    for field in range(fields):
        left = jnp.concatenate(
            [floats[pl.ds(field * emb, slab), pl.ds(high * LOW_ROWS, LOW_ROWS)] for high in range(highs)], axis=0
        ).astype(BF16)
        local = ids[pl.ds(field, 1), :] - at[0] * (highs * LOW_ROWS)
        low = jnp.bitwise_and(local, LOW_ROWS - 1)
        high_id = jnp.right_shift(local, LOW_BITS)
        hot = jnp.where(low_iota == low, 1.0, 0.0).astype(BF16)
        picked = dot(left, hot)
        total = jnp.zeros((slab, group), F32)
        for high in range(highs):
            total = total + jnp.where(high_id == high, picked[high * slab : (high + 1) * slab], 0.0)
        gathered[pl.ds(field * emb, slab), :] = total
    for block in range(ways):
        out[block] = gathered[:, pl.ds(block * part, part)].astype(BF16)


def count_kernel(at, ids, after, out, *, fields):
    highs = out.shape[1] // LOW_ROWS
    group = ids.shape[1]
    low_iota = lax.broadcasted_iota(jnp.int32, (LOW_ROWS, group), 0)
    high_iota = lax.broadcasted_iota(jnp.int32, (8, group), 0)
    for field in range(fields):
        local = ids[pl.ds(field, 1), :] - at[0] * (highs * LOW_ROWS)
        low = jnp.bitwise_and(local, LOW_ROWS - 1)
        hot = jnp.where(low_iota == low, 1.0, 0.0).astype(BF16)
        marks = jnp.where(high_iota == jnp.right_shift(local, LOW_BITS), 1.0, 0.0).astype(BF16)
        got = dot(marks, hot, LANES_IN_LANES)
        for high in range(highs):
            out[pl.ds(field, 1), pl.ds(high * LOW_ROWS, LOW_ROWS)] = got[high : high + 1].astype(jnp.int32)


def column_of(at, rel):
    return pl.multiple_of(((at[1] ^ (rel // 2)) * 2 + (at[2] ^ (rel % 2))) * LANES, LANES)


def column_pick(at, values, mine):
    first = at[2] == 0 if mine else at[2] == 1
    blocks = []
    for one in range(CHIPS):
        low, high = values[:, 2 * one * LANES : (2 * one + 1) * LANES], values[:, (2 * one + 1) * LANES : (2 * one + 2) * LANES]
        blocks.append(jnp.where(first, low, high))
    picked = jnp.concatenate(blocks, axis=1).astype(BF16)
    rows = values.shape[0]
    return [picked[:, begin : begin + rows] for begin in range(0, CHIPS * LANES, rows)]


def step_kernel(at, *refs, shard, emb_end, scale, waits):
    refs = list(refs)
    take = lambda count: [refs.pop(0) for _ in range(count)]
    (parts, dense_t, own, own_tail), pieces = take(4), take(2 * CHIPS)
    one_w, one_b, two_w, two_b, out_w, out_b, labels = take(7)
    take(waits)
    (logits_out, dense_grad), emb_send = take(2), take(CHIPS)
    tower_other, tower_mine, cross_other, cross_mine = take(4)
    weights, tails, bias, small, turned, first, state, lows, mixes, sems = take(10)
    place = at[0]
    ways, layers, gap, main = weights.shape
    rows = parts.shape[2]
    full = first.shape[1]
    extra = full - main
    hidden = one_w.shape[1]
    blocks = -(-shard // LANES)
    copies = [pltpu.make_async_copy(own, weights.at[place], sems.at[0])]
    for rel, piece in enumerate(pieces):
        for step in range(1, ways):
            target = weights.at[place ^ step, :, :, pl.ds(column_of(at, rel), LANES)]
            copies.append(pltpu.make_async_copy(piece.at[step - 1], target, sems.at[len(copies)]))
    for copy in copies:
        copy.start()
    looked = parts[0].astype(F32)
    for block in range(1, ways):
        looked = looked + parts[block].astype(F32)
    turned[pl.ds(0, looked.shape[0]), :] = looked
    turned[pl.ds(emb_end, dense_t.shape[0]), :] = dense_t[...]
    used = emb_end + dense_t.shape[0]
    turned[pl.ds(used, turned.shape[0] - used), :] = jnp.zeros((turned.shape[0] - used, rows), F32)
    start = turned[...].T[:, :full]
    first[...] = start
    state[...] = start
    for copy in copies:
        copy.wait()
    for block in range(ways):
        for layer in range(layers):
            ends = weights[block, layer, pl.ds(gap - 16, 16), :].astype(F32)[8:]
            for one in range(2 * CHIPS):
                tails[block, layer, pl.ds(8 * one, 8), :] = ends[:, one * LANES : (one + 1) * LANES]
    tails[place] = own_tail[...].astype(F32)
    for block in range(ways):
        for layer in range(layers):
            row = jnp.concatenate(
                [tails[block, layer, pl.ds(blocks * extra + one, 1), :] for one in range(blocks)], axis=1
            )
            bias[pl.ds(layer, 1), pl.ds(block * shard, shard)] = row[:, :shard]

    def tail_of(block, layer):
        pieces = [tails[block, layer, pl.ds(one * extra, extra), :] for one in range(blocks)]
        return jnp.concatenate(pieces, axis=1)[:, :shard].astype(BF16)

    @pl.loop(0, layers)
    def _(layer):
        low = state[...].astype(BF16)
        lows[layer] = low
        body = jnp.zeros((rows, main), F32)
        edge = jnp.zeros((rows, extra), F32)
        for block in range(ways):
            chunk = low[:, shard * block : shard * (block + 1)]
            body = body + dot(chunk, weights[block, layer, pl.ds(0, shard), :])
            edge = edge + dot(chunk, tail_of(block, layer), LANES_IN_LANES)
        mixed = jnp.concatenate([body, edge], axis=1) + bias[pl.ds(layer, 1), :full]
        mixes[layer] = mixed
        state[...] = first[...] * mixed + state[...]

    top = state[...].astype(BF16)
    hid_one = dot(top, one_w[...]) + one_b[...]
    act_one = jax.nn.silu(hid_one).astype(BF16)
    hid_two = dot(act_one, two_w[...]) + two_b[...]
    act_two = jax.nn.silu(hid_two).astype(BF16)
    top_float, act_float = top.astype(F32), act_two.astype(F32)
    weight_top = out_w[:, :full].astype(F32)
    weight_act = out_w[:, full:].astype(F32)
    logits = (
        jnp.sum(top_float * weight_top, axis=1, keepdims=True)
        + jnp.sum(act_float * weight_act, axis=1, keepdims=True)
        + out_b[...]
    )
    logits_out[...] = jnp.broadcast_to(logits, (rows, LANES)).T[:1]
    label = jnp.broadcast_to(labels[...].astype(F32), (LANES, rows)).T[:, :1]
    loss = jnp.sum(jax.nn.softplus(logits) - label * logits, axis=0, keepdims=True) * scale
    g_logit = ((jax.nn.sigmoid(logits) - label) * scale).astype(BF16).astype(F32)
    g_two = (g_logit * weight_act * silu_slope(hid_two)).astype(BF16)
    g_one = (dot(g_two, two_w[...], LANES_IN_LANES) * silu_slope(hid_one)).astype(BF16)
    grad = (dot(g_one, one_w[...], LANES_IN_LANES) + g_logit * weight_top).astype(BF16).astype(F32)
    one_float, two_float = g_one.astype(F32), g_two.astype(F32)
    lane = lax.broadcasted_iota(jnp.int32, (1, LANES), 1)
    bias_grad = jnp.sum(g_logit, axis=0, keepdims=True)
    small[...] = jnp.zeros_like(small)
    small[pl.ds(0, 1), pl.ds(0, hidden)] = jnp.sum(one_float, axis=0, keepdims=True)
    small[pl.ds(1, 1), pl.ds(0, hidden)] = jnp.sum(two_float, axis=0, keepdims=True)
    small[pl.ds(2, 1), pl.ds(0, full)] = jnp.sum(top_float * g_logit, axis=0, keepdims=True)
    small[pl.ds(3, 1), pl.ds(0, hidden)] = jnp.sum(act_float * g_logit, axis=0, keepdims=True)
    small[pl.ds(7, 1), pl.ds(0, LANES)] = jnp.where(lane == 0, loss, jnp.where(lane == 1, bias_grad, 0.0))
    tower_other[pl.ds(0, full), :] = top_float.T.astype(BF16)
    tower_other[pl.ds(full, hidden), :] = act_one.astype(F32).T.astype(BF16)
    base = round_up(full + hidden, 16)
    span = CHIPS * LANES
    for which, values in enumerate((one_float, two_float)):
        for index, block in enumerate(column_pick(at, values, False)):
            tower_other[pl.ds(base + which * span + index * rows, rows), :] = block
        for index, block in enumerate(column_pick(at, values, True)):
            tower_mine[pl.ds(which * span + index * rows, rows), :] = block

    inputs = first[...]
    pad = jnp.zeros((rows, turned.shape[0] - full), F32)
    total = jnp.zeros_like(grad)
    low_rows = layers * ways * gap
    base = low_rows + layers * extra
    for layer in reversed(range(layers)):
        rounded = (grad * inputs).astype(BF16)
        values = rounded.astype(F32)
        small[pl.ds(4 + layer, 1), pl.ds(0, full)] = jnp.sum(values, axis=0, keepdims=True)
        total = total + grad * mixes[layer]
        backs = []
        for block in range(ways):
            back = dot(rounded[:, :main], weights[block, layer, pl.ds(0, shard), :], LANES_IN_LANES)
            backs.append(back + dot(rounded[:, main:full], tail_of(block, layer)))
        grad = grad + jnp.concatenate(backs, axis=1)
        for index, block in enumerate(column_pick(at, values, False)):
            cross_other[pl.ds(base + layer * span + index * rows, rows), :] = block
        for index, block in enumerate(column_pick(at, values, True)):
            cross_mine[pl.ds(layer * span + index * rows, rows), :] = block
        edge = jnp.concatenate([values[:, main:full], jnp.zeros((rows, LANES - extra), F32)], axis=1).T
        cross_other[pl.ds(low_rows + layer * extra, extra), :] = edge[:extra].astype(BF16)
        turned[...] = jnp.concatenate([lows[layer].astype(F32), pad], axis=1).T
        for block in range(ways):
            low_t = jnp.concatenate([turned[pl.ds(block * shard, shard), :], jnp.zeros((gap - shard, rows), F32)], axis=0)
            cross_other[pl.ds((layer * ways + block) * gap, gap), :] = low_t.astype(BF16)
    total = total + grad
    turned[...] = jnp.concatenate([total, pad], axis=1).T
    dense_grad[...] = turned[pl.ds(emb_end, dense_grad.shape[0]), :]
    wide = 2 * LANES
    packed = pack_small(small[...], rows)
    for step in range(CHIPS):
        emb_send[step][pl.ds(0, wide), :] = turned[pl.ds(pl.multiple_of((at[1] ^ step) * wide, wide), wide), :].astype(BF16)
        for index, block in enumerate(packed):
            emb_send[step][pl.ds(wide + 16 * index, 16), :] = block


def both_cores(at, mine, theirs, start, which, step, rows):
    begin = (at[1] ^ step) * LANES
    lanes = pl.ds(pl.multiple_of(begin % rows, LANES), LANES)
    row = pl.multiple_of(which * CHIPS * LANES + begin // rows * rows, LANES)
    return jnp.concatenate([mine[pl.ds(row, rows), lanes], theirs[pl.ds(start + row, rows), lanes]], axis=0)


def halves(refs, ways):
    keep_one, send_one, keep_two, send_two = refs
    half = ways // 2

    def place_of(step, block):
        if block < half:
            return (send_one if step & 1 else keep_one), (step >> 1, block)
        return (send_two if step & 2 else keep_two), (step & 1, block - half)

    return place_of


def pack_small(values, lanes):
    if values.shape[1] % lanes:
        values = jnp.concatenate([values, jnp.zeros((8, -values.shape[1] % lanes), F32)], axis=1)
    packed = []
    for begin in range(0, values.shape[1], lanes):
        block = values[:, begin : begin + lanes]
        high = block.astype(BF16).astype(F32)
        packed.append(jnp.concatenate([high, block - high], axis=0).astype(BF16))
    return packed


def unpack_small(rows):
    return jnp.concatenate([one[:8] + one[8:] for one in rows], axis=1)


def tower_product_kernel(at, sent, mine, theirs, *refs, full, hidden):
    refs = refs[-CHIPS:]
    ways = 2 * refs[0].shape[1]
    place_of = halves(refs, ways)
    rows = mine.shape[1]
    part = hidden // ways
    ends = (full - hidden) // ways
    last = refs[0].shape[2] - 2 * part
    base = round_up(full + hidden, 16)
    top_t = jnp.concatenate([sent[pl.ds(0, full), :], theirs[pl.ds(0, full), :]], axis=1)
    act_t = jnp.concatenate([sent[pl.ds(full, hidden), :], theirs[pl.ds(full, hidden), :]], axis=1)
    for step in range(CHIPS):
        one = dot(top_t, both_cores(at, mine, theirs, base, 0, step, rows))
        two = dot(act_t, both_cores(at, mine, theirs, base, 1, step, rows))
        for block in range(ways):
            own_rows = slice(block * part, (block + 1) * part)
            out, where = place_of(step, block)
            out[*where, pl.ds(0, part), :] = one[own_rows].astype(out.dtype)
            out[*where, pl.ds(part, part), :] = two[own_rows].astype(out.dtype)
            rest = one[hidden + block * ends : hidden + (block + 1) * ends]
            rest = jnp.concatenate([rest, jnp.zeros((last - ends, LANES), F32)], axis=0)
            out[*where, pl.ds(2 * part, last), :] = rest.astype(out.dtype)


def cross_product_kernel(at, sent, mine, theirs, *refs, layers, shard, gap):
    pack = refs[-1]
    ways, extra = pack.shape[0], pack.shape[1]
    place_of = halves(refs[-CHIPS - 1 : -1], ways)
    rows = mine.shape[1]
    low_rows = layers * ways * gap
    base = low_rows + layers * extra
    pack[...] = jnp.zeros_like(pack)

    def lows(layer, block):
        own_rows = pl.ds((layer * ways + block) * gap, gap)
        return jnp.concatenate([sent[own_rows, :], theirs[own_rows, :]], axis=1)

    for layer in range(layers):
        own_rows = pl.ds(low_rows + layer * extra, extra)
        edge = jnp.concatenate([sent[own_rows, :], theirs[own_rows, :]], axis=1)
        for block in range(ways):
            product = dot(edge, lows(layer, block), LANES_IN_LANES)
            pack[block, :, pl.ds(layer * shard, shard)] = product[:, :shard]
    for step in range(CHIPS):
        for layer in range(layers):
            columns = both_cores(at, mine, theirs, base, layer, step, rows)
            for block in range(ways):
                out, where = place_of(step, block)
                out[*where, pl.ds(layer * gap, gap), :] = dot(lows(layer, block), columns).astype(out.dtype)
        for block in range(ways):
            out, where = place_of(step, block)
            lanes = pl.ds(column_of(at, 2 * step), LANES)
            out[*where, pl.ds(layers * gap, extra), :] = pack[block, :, lanes].astype(out.dtype)


def scatter_kernel(at, sent, theirs, *refs, emb, half):
    infos, (out, spread, table, columns) = refs[:CHIPS], refs[-4:]
    chip, core = at[1], at[2]
    part, wide = theirs.shape[2], 2 * LANES
    group = 2 * CHIPS * part
    ways = out.shape[0]
    fields = infos[0].shape[0]
    ids_at = infos[0].shape[1] - 2 * part
    slab = emb + 1
    spread[pl.ds(0, MARGIN), :] = jnp.zeros((MARGIN, group), F32)
    spread[pl.ds(MARGIN + wide, 64), :] = jnp.zeros((64, group), F32)
    pad = jnp.zeros((LANES - fields, part), F32)

    def ids_of(rel, rows=slice(None)):
        return infos[rel // 2][rows, pl.ds(ids_at + rel % 2 * part, part)]

    for rel in range(2 * CHIPS):
        values = (theirs if rel % 2 else sent)[rel // 2, pl.ds(0, wide), :]
        spread[pl.ds(MARGIN, wide), pl.ds(rel * part, part)] = values.astype(F32)
        low = jnp.bitwise_and(ids_of(rel), LOW_ROWS - 1).astype(F32)
        columns[pl.ds(rel * part, part), :] = jnp.concatenate([low, pad], axis=0).T
    low_iota = lax.broadcasted_iota(jnp.int32, (group, LOW_ROWS), 1).astype(F32)
    for mine in range(CHIPS):

        @pl.when(chip == mine)
        def _(mine=mine):
            first_field = (mine * wide) // emb
            for field in range(first_field, min(fields, (mine * wide + wide - 1) // emb + 1)):
                begin = field * emb - mine * wide + MARGIN
                values = spread[pl.ds(begin, slab), :]
                this = jnp.concatenate([ids_of(rel, pl.ds(field, 1)) for rel in range(2 * CHIPS)], axis=1)
                high_id = jnp.right_shift(this, LOW_BITS) - core * half
                hot = jnp.where(low_iota == columns[:, field : field + 1], 1.0, 0.0).astype(BF16)
                stacked = jnp.concatenate(
                    [
                        jnp.where(high_id == block * 2 * half + piece, values, 0.0)
                        for block in range(ways)
                        for piece in range(half)
                    ],
                    axis=0,
                ).astype(BF16)
                got = dot(stacked, hot)
                for high in range(ways * half):
                    table[high, pl.ds(begin, emb), :] = got[high * slab : high * slab + emb]

    for block in range(ways):
        for piece in range(half):
            values = table[block * half + piece, pl.ds(MARGIN, wide), :]
            out[block, pl.ds(piece * wide, wide), :] = values.astype(BF16)
    rows = []
    for begin in range(wide, sent.shape[1], 16):
        rows.append(sum(one[step, pl.ds(begin, 16), :].astype(F32) for one in (sent, theirs) for step in range(CHIPS)))
    for index, packed in enumerate(pack_small(unpack_small(rows), LOW_ROWS)):
        for block in range(ways):
            out[block, pl.ds(half * wide + 16 * index, 16), :] = packed


def first_add_kernel(keep_one, got_one, keep_two, got_two, *refs):
    send_one, send_two = refs[-2:]
    send_one[...] = (keep_one[1].astype(F32) + got_one[1].astype(F32)).astype(BF16)
    send_two[...] = (keep_two[1].astype(F32) + got_two[1].astype(F32)).astype(BF16)


def second_add_kernel(at, keep_one, got_one, last_one, keep_two, got_two, last_two, *refs, by_step):
    out = refs[-1]
    half = last_one.shape[0]
    flip = at[0] if by_step else 0
    for first, keep, got, last in ((0, keep_one, got_one, last_one), (half, keep_two, got_two, last_two)):
        for block in range(half):
            total = keep[0, block].astype(F32) + got[0, block].astype(F32) + last[block].astype(F32)
            out[(first + block) ^ flip] = total.astype(BF16)


def add_kernel(*refs, count):
    total = refs[0][...].astype(F32)
    for other in refs[1:count]:
        total = total + other[...].astype(F32)
    refs[-1][...] = total.astype(refs[-1].dtype)


def fold_kernel(parts, *refs):
    total = parts[0].astype(F32)
    for block in range(1, parts.shape[0]):
        total = total + parts[block].astype(F32)
    refs[-1][...] = total.astype(refs[-1].dtype)


def table_fold_kernel(parts, *refs):
    out, small = refs[-2:]
    total = parts[0].astype(F32)
    for block in range(1, parts.shape[0]):
        total = total + parts[block].astype(F32)
    out[...] = total[: out.shape[0]].astype(BF16)
    small[...] = unpack_small([total[begin : begin + 16] for begin in range(out.shape[0], total.shape[0], 16)])


def table_kernel(at, *refs):
    pieces, out = refs[: 2 * CHIPS], refs[-1]
    wide, low = 2 * LANES, LOW_ROWS
    half = pieces[0].shape[0] // wide
    last = CHIPS - 1
    for rel, piece in enumerate(pieces):
        chip = at[1] ^ (rel // 2)
        core = at[2] ^ (rel % 2)
        for block in range(half):
            lanes = pl.ds(pl.multiple_of((core * half + block) * low, low), low)
            values = piece[pl.ds(block * wide, wide), :].astype(F32)

            @pl.when(chip < last)
            def _(lanes=lanes, values=values, chip=chip):
                out[pl.ds(pl.multiple_of(chip * wide, wide), wide), lanes] = values

            @pl.when(chip == last)
            def _(lanes=lanes, values=values):
                height = out.shape[0] - last * wide
                out[pl.ds(last * wide, height), lanes] = values[:height]


def tower_kernel(at, *refs):
    pieces, (one_out, two_out) = refs[: 2 * CHIPS], refs[-2:]
    ways = pieces[0].shape[0]
    hidden = two_out.shape[0]
    part = hidden // ways
    ends = (one_out.shape[0] - hidden) // ways
    for rel, piece in enumerate(pieces):
        lanes = pl.ds(column_of(at, rel), LANES)
        for block in range(ways):
            source = block ^ at[0]
            one_out[pl.ds(block * part, part), lanes] = piece[source, pl.ds(0, part), :].astype(F32)
            two_out[pl.ds(block * part, part), lanes] = piece[source, pl.ds(part, part), :].astype(F32)
            rest = piece[source, pl.ds(2 * part, 16), :].astype(F32)
            one_out[pl.ds(hidden + block * ends, ends), lanes] = rest[:ends]


def cross_kernel(at, *refs, gap):
    pieces, out, pack = refs[: 2 * CHIPS], refs[-2], refs[-1]
    layers, shard, full = out.shape
    main = pack.shape[1]
    extra = full - main
    for rel, piece in enumerate(pieces):
        lanes = pl.ds(column_of(at, rel), LANES)
        for layer in range(layers):
            out[layer, :, lanes] = piece[pl.ds(layer * gap, gap), :].astype(F32)[:shard]
        pack[pl.ds(0, extra), lanes] = piece[pl.ds(layers * gap, extra), :].astype(F32)
    pack[pl.ds(extra, pack.shape[0] - extra), :] = jnp.zeros((pack.shape[0] - extra, main), F32)
    turned = pack[...].T
    for layer in range(layers):
        out[layer, :, pl.ds(main, extra)] = turned[layer * shard : (layer + 1) * shard, :extra]


def vmem_bytes(one):
    *lead, rows, lanes = one.shape
    size = jnp.dtype(one.dtype).itemsize
    return math.prod(lead) * round_up(rows, 32 // size) * round_up(lanes, LANES) * size


def local(kernel, out_shape, operands, after=(), scratch=(), in_place=(), name=None, **options):
    operands = list(operands)
    smem = [index for index, one in enumerate(operands) if one.shape == (3,)]
    specs = [
        IN_SMEM if index in smem else IN_PLACE if index in in_place else IN_VMEM for index in range(len(operands))
    ]
    outs = out_shape if isinstance(out_shape, list) else [out_shape]
    held = [one for index, one in enumerate(operands) if index not in (*smem, *in_place)] + outs
    held += [one for one in scratch if len(one.shape) > 1]
    space = sum(vmem_bytes(one) for one in held) + SPARE_BYTES[name]
    got = pl.pallas_call(
        functools.partial(kernel, **options),
        out_shape=outs,
        in_specs=specs + [IN_PLACE] * len(after),
        out_specs=[IN_VMEM] * len(outs),
        scratch_shapes=list(scratch),
        compiler_params=pltpu.CompilerParams(vmem_limit_bytes=space),
        cost_estimate=pl.CostEstimate(flops=int(COST * MICROS[name]), bytes_accessed=0, transcendentals=0),
        name=name,
    )(*operands, *after)
    return got if isinstance(out_shape, list) else got[0]


class Links:
    def __init__(self, dp_size, cross_size):
        bits = dp_size.bit_length() - 1
        axis_bits = (bits - 1) // 2
        self.dp_size, self.cross_size = dp_size, cross_size
        self.core = 1
        self.chip_masks = (1 << 1, 1 << (1 + axis_bits))
        used = (self.core, *self.chip_masks)
        self.others = tuple(1 << bit for bit in range(bits) if 1 << bit not in used)

    def chip_mask(self, step):
        return sum(mask for bit, mask in enumerate(self.chip_masks) if step >> bit & 1)

    def chip(self, dp_place):
        return sum((dp_place // mask % 2) << bit for bit, mask in enumerate(self.chip_masks))

    def over_dp(self, value, mask):
        return lax.ppermute(value, "dp", [(one, one ^ mask) for one in range(self.dp_size)])

    def over_cross(self, value, mask):
        return lax.ppermute(value, "cross", [(one, one ^ mask) for one in range(self.cross_size)])

    def chips_swap(self, value_of):
        return [self.over_dp(value_of(step), self.chip_mask(step)) for step in range(1, CHIPS)]

    def cross_swap(self, value_of):
        return [self.over_cross(value_of(step), step) for step in range(1, self.cross_size)]

    def cross_exchange(self, value):
        return lax.all_to_all(value, "cross", split_axis=0, concat_axis=0, tiled=True)

    def add_others(self, value):
        for mask in self.others:
            value = (value.astype(F32) + self.over_dp(value, mask).astype(F32)).astype(BF16)
        return value

    def over_others(self, value):
        for mask in self.others:
            value = value + self.over_dp(value, mask)
        return value


    def plane_first(self, parts, after, name):
        keep_one, send_one, keep_two, send_two = parts
        one, two = self.chip_masks
        got_one, got_two = self.over_dp(send_one, one), self.over_dp(send_two, two)
        part = Shape(send_one.shape[1:], BF16)
        next_one, next_two = local(first_add_kernel, [part, part], [keep_one, got_one, keep_two, got_two], after, name=name)
        return keep_one, got_one, next_one, keep_two, got_two, next_two

    def plane_second(self, parts, at, by_step, after, name):
        keep_one, got_one, next_one, keep_two, got_two, next_two = parts
        one, two = self.chip_masks
        last_one, last_two = self.over_dp(next_one, two), self.over_dp(next_two, one)
        total = local(
            second_add_kernel,
            Shape((2 * next_one.shape[0], *next_one.shape[1:]), BF16),
            [at, keep_one, got_one, last_one, keep_two, got_two, last_two],
            after,
            name=name,
            by_step=by_step,
        )
        return self.add_others(total)

    def both_cores(self, arrays):
        return [each for one in arrays for each in (one, self.over_dp(one, self.core))]

    def plane_gather(self, value):
        return self.both_cores([value, *self.chips_swap(lambda step: value)])


def body(
    emb_table,
    dense_input,
    feature_ids,
    labels,
    cross_weight,
    cross_bias,
    tower_one,
    bias_one,
    tower_two,
    bias_two,
    out_weight,
    out_bias,
):
    layers, shard, full = cross_weight.shape
    group, fields = feature_ids.shape
    rows_here, emb_end = emb_table.shape
    emb = emb_end // fields
    dense_width = dense_input.shape[1]
    hidden = tower_one.shape[1]
    main = hidden
    extra = full - main
    ways = lax.axis_size("cross")
    place = lax.axis_index("cross")
    dp_place = lax.axis_index("dp")
    links = Links(lax.axis_size("dp"), ways)
    rows = group // ways
    scale = 1.0 / (group * links.dp_size)
    chip, core = links.chip(dp_place), dp_place % 2
    at = jnp.stack([place, chip, core]).astype(jnp.int32)
    wide = 2 * LANES
    gap = round_up(shard + 8, 16)

    blocks = -(-shard // LANES)
    ends = jnp.pad(cross_weight[:, :, main:].transpose(0, 2, 1), ((0, 0), (0, 0), (0, blocks * LANES - shard)))
    ends = ends.reshape(layers, extra, blocks, LANES).transpose(0, 2, 1, 3).reshape(layers, blocks * extra, LANES)
    ends_bias = jnp.pad(cross_bias, ((0, 0), (0, blocks * LANES - shard))).reshape(layers, blocks, LANES)
    own_tail = jnp.concatenate([ends, ends_bias], axis=1)
    own_tail = jnp.pad(own_tail, ((0, 0), (0, 64 - own_tail.shape[1]), (0, 0)))
    part = chip * 2 + core
    own_block = jnp.concatenate(
        [
            lax.dynamic_slice_in_dim(cross_weight, part * LANES, LANES, 2),
            jnp.zeros((layers, gap - 8 - shard, LANES), BF16),
            lax.dynamic_slice_in_dim(own_tail, part * 8, 8, 1),
        ],
        axis=1,
    )
    foreign = links.cross_swap(lambda step: own_block)

    ids_t = feature_ids.T
    emb_rows = round_up(emb_end + 1, 8)
    looked = local(
        lookup_kernel,
        Shape((ways, emb_rows, rows), BF16),
        [at, emb_table.T, ids_t],
        scratch=[pltpu.VMEM((emb_rows, rows_here), F32), pltpu.VMEM((emb_rows, group), F32)],
        name="lookup",
        fields=fields,
        emb=emb,
    )
    *foreign, looked = lax.optimization_barrier((*foreign, looked))
    parts = links.cross_exchange(looked)
    counted = local(count_kernel, Shape((fields, rows_here), jnp.int32), [at, ids_t], [looked], name="count", fields=fields)
    own_ids = lax.dynamic_slice_in_dim(ids_t, place * rows, rows, 1)
    own_info = jnp.concatenate([counted, own_ids], axis=1)
    core_info = links.over_dp(own_info, links.core)
    info = jnp.concatenate([counted + core_info[:, :rows_here], own_ids, core_info[:, rows_here:]], axis=1)
    foreign = jnp.stack(foreign)
    foreign = [foreign, *links.chips_swap(lambda step: foreign)]
    *foreign, info = lax.optimization_barrier((*foreign, info))
    infos = [info, *links.chips_swap(lambda step: info)]
    pieces = [pltpu.with_memory_space_constraint(one, pltpu.HBM) for one in links.both_cores(foreign)]

    own_dense = lax.dynamic_slice_in_dim(dense_input.T, place * rows, rows, 1)
    dense_t = jnp.pad(own_dense.astype(F32), ((0, round_up(dense_width, 8) - dense_width), (0, 0)))
    own_full = jnp.pad(cross_weight[:, :, :main], ((0, 0), (0, gap - shard), (0, 0)))
    turned_rows = round_up(full, LANES)
    emb_shape = Shape((wide + 16 * -(-turned_rows // rows), rows), BF16)
    tower_factors = round_up(full + hidden, 16)
    cross_factors = layers * (ways * gap + extra)
    logits, dense_grad, *emb_send, tower_other, tower_mine, cross_other, cross_mine = local(
        step_kernel,
        [
            Shape((1, rows), F32),
            Shape((dense_width, rows), F32),
            *[emb_shape] * CHIPS,
            Shape((tower_factors + 2 * CHIPS * LANES, rows), BF16),
            Shape((2 * CHIPS * LANES, rows), BF16),
            Shape((cross_factors + layers * CHIPS * LANES, rows), BF16),
            Shape((layers * CHIPS * LANES, rows), BF16),
        ],
        [
            at,
            parts,
            dense_t,
            own_full,
            own_tail,
            *pieces,
            tower_one,
            bias_one[None, :],
            tower_two,
            bias_two[None, :],
            out_weight[None, :],
            out_bias[None, :],
            labels[None, :],
        ],
        infos,
        [
            pltpu.VMEM((ways, layers, gap, main), BF16),
            pltpu.VMEM((ways, layers, 64, LANES), F32),
            pltpu.VMEM((8, turned_rows), F32),
            pltpu.VMEM((8, turned_rows), F32),
            pltpu.VMEM((turned_rows, rows), F32),
            pltpu.VMEM((rows, full), F32),
            pltpu.VMEM((rows, full), F32),
            pltpu.VMEM((layers, rows, full), BF16),
            pltpu.VMEM((layers, rows, full), F32),
            pltpu.SemaphoreType.DMA((1 + 2 * CHIPS * (ways - 1),)),
        ],
        in_place=(3, *range(5, 5 + 2 * CHIPS)),
        name="step",
        shard=shard,
        emb_end=emb_end,
        scale=scale,
        waits=CHIPS,
    )

    tower_theirs = links.over_dp(tower_other, links.core)
    cross_theirs = links.over_dp(cross_other, links.core)
    emb_got = links.chips_swap(lambda step: emb_send[step])

    tower_rows = round_up(2 * (hidden // ways) + extra // ways, 16)
    tower_shape = (ways, tower_rows, LANES)
    split = lambda shape: Shape((2, shape[0] // 2, *shape[1:]), BF16)
    tower_parts = local(
        tower_product_kernel,
        [split(tower_shape)] * 4,
        [at, tower_other, tower_mine, tower_theirs],
        name="tower_products",
        full=full,
        hidden=hidden,
    )


    cross_rows = layers * gap + extra
    cross_shape = (ways, cross_rows, LANES)
    cross_parts = local(
        cross_product_kernel,
        [split(cross_shape)] * 4,
        [at, cross_other, cross_mine, cross_theirs],
        [tower_parts[0]],
        [pltpu.VMEM((ways, extra, main), F32)],
        name="cross_products",
        layers=layers,
        shard=shard,
        gap=gap,
    )
    tower_first = links.plane_first(tower_parts, [cross_parts[0]], "tower_first")

    *emb_got, _ = lax.optimization_barrier((*emb_got, cross_parts[0]))
    emb_parts = jnp.stack([emb_send[0], *emb_got])
    emb_theirs = links.over_dp(emb_parts, links.core)
    half = rows_here // LOW_ROWS // 2
    table_ends = 16 * -(-turned_rows // LOW_ROWS)
    table_parts = local(
        scatter_kernel,
        Shape((ways, half * wide + table_ends, LOW_ROWS), BF16),
        [at, emb_parts, emb_theirs, *infos],
        [tower_first[2]],
        [
            pltpu.VMEM((MARGIN + wide + 64, rows * 2 * CHIPS), F32),
            pltpu.VMEM((ways * half, MARGIN + wide + 64, LOW_ROWS), F32),
            pltpu.VMEM((rows * 2 * CHIPS, LANES), F32),
        ],
        name="scatter",
        emb=emb,
        half=half,
    )
    table_parts = links.add_others(table_parts)
    table_got = links.cross_exchange(table_parts)
    tower_sum = links.plane_second(tower_first, at, True, [table_parts], "tower_second")
    tower_got = links.cross_swap(lambda step: tower_sum[step])
    tower_fold = local(
        add_kernel, Shape(tower_shape[1:], BF16), [tower_sum[0], *tower_got], name="tower_fold", count=ways
    )
    keep_one, send_one, keep_two, send_two = cross_parts
    send_one, send_two, _ = lax.optimization_barrier((send_one, send_two, tower_sum))
    cross_first = links.plane_first((keep_one, send_one, keep_two, send_two), [tower_fold], "cross_first")
    table_fold, small = local(
        table_fold_kernel,
        [Shape((half * wide, LOW_ROWS), BF16), Shape((8, round_up(turned_rows, LOW_ROWS)), F32)],
        [table_got],
        [cross_first[2]],
        name="table_fold",
    )
    table_all = links.chips_swap(lambda step: table_fold)
    tower_all = jnp.stack([tower_fold, *links.cross_swap(lambda step: tower_fold)])
    cross_sum = links.plane_second(cross_first, at, False, [tower_fold], "cross_second")
    cross_got = links.cross_exchange(cross_sum)
    *table_all, _ = lax.optimization_barrier((*table_all, cross_sum))
    table_all = links.both_cores([table_fold, *table_all])
    tower_blocks = links.chips_swap(lambda step: tower_all)
    table_grad = local(table_kernel, Shape((emb_end, rows_here), F32), [at, *table_all], [cross_sum], name="table")
    cross_fold = local(fold_kernel, Shape(cross_shape[1:], BF16), [cross_got], [table_grad], name="cross_fold")
    *tower_blocks, _ = lax.optimization_barrier((*tower_blocks, cross_fold))
    tower_blocks = links.both_cores([tower_all, *tower_blocks])
    tower_one_grad, tower_two_grad = local(
        tower_kernel, [Shape((full, hidden), F32), Shape((hidden, hidden), F32)], [at, *tower_blocks], name="towers"
    )
    cross_weight_grad = local(
        cross_kernel,
        Shape((layers, shard, full), F32),
        [at, *links.plane_gather(cross_fold)],
        scratch=[pltpu.VMEM((LANES, main), F32)],
        name="cross",
        gap=gap,
    )
    cross_bias_grad = lax.dynamic_slice_in_dim(small[4 : 4 + layers], place * shard, shard, 1)
    return (
        small[7, 0],
        logits[0],
        dense_grad.T,
        table_grad.T,
        cross_weight_grad,
        cross_bias_grad,
        tower_one_grad,
        small[0, :hidden],
        tower_two_grad,
        small[1, :hidden],
        jnp.concatenate([small[2, :full], small[3, :hidden]]),
        small[7, 1:2],
        links.over_others(sum(one[:, :rows_here] for one in infos)).T,
    )


def solution(mesh):
    in_specs = (
        P("cross", None),
        P("dp", None),
        P("dp", None),
        P(("dp", "cross")),
        P(None, "cross", None),
        P(None, "cross"),
        P(),
        P(),
        P(),
        P(),
        P(),
        P(),
    )
    out_specs = (
        P(),
        P(("dp", "cross")),
        P(("dp", "cross"), None),
        P("cross", None),
        P(None, "cross", None),
        P(None, "cross"),
        P(),
        P(),
        P(),
        P(),
        P(),
        P(),
        P("cross", None),
    )
    return jax.shard_map(body, mesh=mesh, in_specs=in_specs, out_specs=out_specs, check_vma=False)
```

```python
import collections
import functools
import math

import jax
import jax.numpy as jnp
from jax import lax
from jax.experimental import pallas as pl
from jax.experimental.pallas import tpu as pltpu
from jax.sharding import PartitionSpec as P

F32 = jnp.float32
BF16 = jnp.bfloat16
ROWS_IN_ROWS = (((0,), (0,)), ((), ()))
LANES_IN_LANES = (((1,), (1,)), ((), ()))
LANES = 128
LOW_BITS = 8
LOW_ROWS = 1 << LOW_BITS
CHIPS = 4
MARGIN = 48
ID_ROWS = 32
STEP_SPARE = 8 << 20
SPARE_BYTES = collections.defaultdict(lambda: 3 << 20, step=STEP_SPARE)
COST = 5.75e+09
MICROS = dict(
    lookup=7.4,
    count=5.2,
    step=23,
    tower_products=5.9,
    scatter=7,
    cross_products=8.9,
    tower_first=3.1,
    tower_second=2.3,
    table_fold=2,
    tower_fold=1.8,
    cross_first=4,
    cross_second=2.7,
    cross_fold=1.9,
    table=3.9,
    towers=6.8,
    cross=3.6,
)
IN_VMEM = pl.BlockSpec(memory_space=pltpu.VMEM)
IN_SMEM = pl.BlockSpec(memory_space=pltpu.SMEM)
IN_PLACE = pl.BlockSpec(memory_space=pl.ANY)
Shape = jax.ShapeDtypeStruct


def round_up(size, step):
    return -(-size // step) * step


def dot(left, right, dims=(((1,), (0,)), ((), ()))):
    return lax.dot_general(left, right, dims, preferred_element_type=F32)


def silu_slope(pre_act):
    sigmoid_part = jax.nn.sigmoid(pre_act)
    return sigmoid_part * (1.0 + pre_act * (1.0 - sigmoid_part))


def lookup_kernel(at, table, ids, out, floats, gathered, *, fields, emb):
    ways = out.shape[0]
    highs = table.shape[1] // LOW_ROWS
    group = ids.shape[1]
    part = group // ways
    slab = emb + 1
    floats[pl.ds(0, table.shape[0]), :] = table[...].astype(F32)
    low_iota = lax.broadcasted_iota(jnp.int32, (LOW_ROWS, group), 0)
    for field in range(fields):
        left = jnp.concatenate(
            [floats[pl.ds(field * emb, slab), pl.ds(high * LOW_ROWS, LOW_ROWS)] for high in range(highs)], axis=0
        ).astype(BF16)
        local = ids[pl.ds(field, 1), :] - at[0] * (highs * LOW_ROWS)
        low = jnp.bitwise_and(local, LOW_ROWS - 1)
        high_id = jnp.right_shift(local, LOW_BITS)
        hot = jnp.where(low_iota == low, 1.0, 0.0).astype(BF16)
        picked = dot(left, hot)
        total = jnp.zeros((slab, group), F32)
        for high in range(highs):
            total = total + jnp.where(high_id == high, picked[high * slab : (high + 1) * slab], 0.0)
        gathered[pl.ds(field * emb, slab), :] = total
    for block in range(ways):
        out[block] = gathered[:, pl.ds(block * part, part)].astype(BF16)


def column_of(at, rel):
    return pl.multiple_of(((at[1] ^ (rel // 2)) * 2 + (at[2] ^ (rel % 2))) * LANES, LANES)


def column_pick(at, values, mine):
    first = at[2] == 0 if mine else at[2] == 1
    blocks = []
    for one in range(CHIPS):
        low, high = values[:, 2 * one * LANES : (2 * one + 1) * LANES], values[:, (2 * one + 1) * LANES : (2 * one + 2) * LANES]
        blocks.append(jnp.where(first, low, high))
    picked = jnp.concatenate(blocks, axis=1).astype(BF16)
    rows = values.shape[0]
    return [picked[:, begin : begin + rows] for begin in range(0, CHIPS * LANES, rows)]


def step_kernel(at, *refs, shard, emb_end, scale):
    refs = list(refs)
    take = lambda count: [refs.pop(0) for _ in range(count)]
    (parts, dense_t, own, own_tail), pieces = take(4), take(2 * CHIPS)
    one_at, one_b, two_at, two_b, out_w, out_b, labels, ids = take(8)
    (logits_out, dense_grad), emb_send = take(2), take(CHIPS)
    tower_other, tower_mine, cross_other, cross_mine = take(4)
    weights, one_w, two_w, tails, bias, small, turned, first, state, lows, mixes, sems = take(12)
    place = at[0]
    ways, layers, gap, main = weights.shape
    rows = parts.shape[2]
    full = first.shape[1]
    extra = full - main
    hidden = one_w.shape[1]
    blocks = -(-shard // LANES)
    copies = [pltpu.make_async_copy(own, weights.at[place], sems.at[0])]
    for rel, piece in enumerate(pieces):
        for step in range(1, ways):
            target = weights.at[place ^ step, :, :, pl.ds(column_of(at, rel), LANES)]
            copies.append(pltpu.make_async_copy(piece.at[step - 1], target, sems.at[len(copies)]))
    towers = [
        pltpu.make_async_copy(one_at, one_w, sems.at[len(copies)]),
        pltpu.make_async_copy(two_at, two_w, sems.at[len(copies) + 1]),
    ]
    for copy in copies + towers:
        copy.start()
    looked = parts[0].astype(F32)
    for block in range(1, ways):
        looked = looked + parts[block].astype(F32)
    turned[pl.ds(0, looked.shape[0]), :] = looked
    turned[pl.ds(emb_end, dense_t.shape[0]), :] = dense_t[...]
    used = emb_end + dense_t.shape[0]
    turned[pl.ds(used, turned.shape[0] - used), :] = jnp.zeros((turned.shape[0] - used, rows), F32)
    start = turned[...].T[:, :full]
    first[...] = start
    state[...] = start
    for copy in copies:
        copy.wait()
    for block in range(ways):
        for layer in range(layers):
            ends = weights[block, layer, pl.ds(gap - 16, 16), :].astype(F32)[8:]
            for one in range(2 * CHIPS):
                tails[block, layer, pl.ds(8 * one, 8), :] = ends[:, one * LANES : (one + 1) * LANES]
    tails[place] = own_tail[...].astype(F32)
    for block in range(ways):
        for layer in range(layers):
            row = jnp.concatenate(
                [tails[block, layer, pl.ds(blocks * extra + one, 1), :] for one in range(blocks)], axis=1
            )
            bias[pl.ds(layer, 1), pl.ds(block * shard, shard)] = row[:, :shard]

    def tail_of(block, layer):
        pieces = [tails[block, layer, pl.ds(one * extra, extra), :] for one in range(blocks)]
        return jnp.concatenate(pieces, axis=1)[:, :shard].astype(BF16)

    @pl.loop(0, layers)
    def _(layer):
        low = state[...].astype(BF16)
        lows[layer] = low
        body = jnp.zeros((rows, main), F32)
        edge = jnp.zeros((rows, extra), F32)
        for block in range(ways):
            chunk = low[:, shard * block : shard * (block + 1)]
            body = body + dot(chunk, weights[block, layer, pl.ds(0, shard), :])
            edge = edge + dot(chunk, tail_of(block, layer), LANES_IN_LANES)
        mixed = jnp.concatenate([body, edge], axis=1) + bias[pl.ds(layer, 1), :full]
        mixes[layer] = mixed
        state[...] = first[...] * mixed + state[...]

    for copy in towers:
        copy.wait()
    top = state[...].astype(BF16)
    hid_one = dot(top, one_w[...]) + one_b[...]
    act_one = jax.nn.silu(hid_one).astype(BF16)
    hid_two = dot(act_one, two_w[...]) + two_b[...]
    act_two = jax.nn.silu(hid_two).astype(BF16)
    top_float, act_float = top.astype(F32), act_two.astype(F32)
    weight_top = out_w[:, :full].astype(F32)
    weight_act = out_w[:, full:].astype(F32)
    logits = (
        jnp.sum(top_float * weight_top, axis=1, keepdims=True)
        + jnp.sum(act_float * weight_act, axis=1, keepdims=True)
        + out_b[...]
    )
    logits_out[...] = jnp.broadcast_to(logits, (rows, LANES)).T[:1]
    label = jnp.broadcast_to(labels[...].astype(F32), (LANES, rows)).T[:, :1]
    loss = jnp.sum(jax.nn.softplus(logits) - label * logits, axis=0, keepdims=True) * scale
    g_logit = ((jax.nn.sigmoid(logits) - label) * scale).astype(BF16).astype(F32)
    g_two = (g_logit * weight_act * silu_slope(hid_two)).astype(BF16)
    g_one = (dot(g_two, two_w[...], LANES_IN_LANES) * silu_slope(hid_one)).astype(BF16)
    grad = (dot(g_one, one_w[...], LANES_IN_LANES) + g_logit * weight_top).astype(BF16).astype(F32)
    one_float, two_float = g_one.astype(F32), g_two.astype(F32)
    lane = lax.broadcasted_iota(jnp.int32, (1, LANES), 1)
    bias_grad = jnp.sum(g_logit, axis=0, keepdims=True)
    small[...] = jnp.zeros_like(small)
    small[pl.ds(0, 1), pl.ds(0, hidden)] = jnp.sum(one_float, axis=0, keepdims=True)
    small[pl.ds(1, 1), pl.ds(0, hidden)] = jnp.sum(two_float, axis=0, keepdims=True)
    small[pl.ds(2, 1), pl.ds(0, full)] = jnp.sum(top_float * g_logit, axis=0, keepdims=True)
    small[pl.ds(3, 1), pl.ds(0, hidden)] = jnp.sum(act_float * g_logit, axis=0, keepdims=True)
    small[pl.ds(7, 1), pl.ds(0, LANES)] = jnp.where(lane == 0, loss, jnp.where(lane == 1, bias_grad, 0.0))
    tower_other[pl.ds(0, full), :] = top_float.T.astype(BF16)
    tower_other[pl.ds(full, hidden), :] = act_one.astype(F32).T.astype(BF16)
    base = round_up(full + hidden, 16)
    span = CHIPS * LANES
    for which, values in enumerate((one_float, two_float)):
        for index, block in enumerate(column_pick(at, values, False)):
            tower_other[pl.ds(base + which * span + index * rows, rows), :] = block
        for index, block in enumerate(column_pick(at, values, True)):
            tower_mine[pl.ds(which * span + index * rows, rows), :] = block

    inputs = first[...]
    pad = jnp.zeros((rows, turned.shape[0] - full), F32)
    total = jnp.zeros_like(grad)
    low_rows = layers * ways * gap
    base = low_rows + layers * extra
    for layer in reversed(range(layers)):
        rounded = (grad * inputs).astype(BF16)
        values = rounded.astype(F32)
        small[pl.ds(4 + layer, 1), pl.ds(0, full)] = jnp.sum(values, axis=0, keepdims=True)
        total = total + grad * mixes[layer]
        backs = []
        for block in range(ways):
            back = dot(rounded[:, :main], weights[block, layer, pl.ds(0, shard), :], LANES_IN_LANES)
            backs.append(back + dot(rounded[:, main:full], tail_of(block, layer)))
        grad = grad + jnp.concatenate(backs, axis=1)
        for index, block in enumerate(column_pick(at, values, False)):
            cross_other[pl.ds(base + layer * span + index * rows, rows), :] = block
        for index, block in enumerate(column_pick(at, values, True)):
            cross_mine[pl.ds(layer * span + index * rows, rows), :] = block
        edge = jnp.concatenate([values[:, main:full], jnp.zeros((rows, LANES - extra), F32)], axis=1).T
        cross_other[pl.ds(low_rows + layer * extra, extra), :] = edge[:extra].astype(BF16)
        turned[...] = jnp.concatenate([lows[layer].astype(F32), pad], axis=1).T
        for block in range(ways):
            low_t = jnp.concatenate([turned[pl.ds(block * shard, shard), :], jnp.zeros((gap - shard, rows), F32)], axis=0)
            cross_other[pl.ds((layer * ways + block) * gap, gap), :] = low_t.astype(BF16)
    total = total + grad
    turned[...] = jnp.concatenate([total, pad], axis=1).T
    dense_grad[...] = turned[pl.ds(emb_end, dense_grad.shape[0]), :]
    wide = 2 * LANES
    packed = pack_small(small[...], rows)
    fields = ids.shape[0]
    blank = jnp.zeros((ID_ROWS - fields, rows), F32)
    low_ids = jnp.bitwise_and(ids[...], LOW_ROWS - 1).astype(F32)
    high_ids = jnp.right_shift(ids[...], LOW_BITS).astype(F32)
    id_rows = jnp.concatenate([low_ids, blank, high_ids, blank], axis=0).astype(BF16)
    ids_at = wide + 16 * len(packed)
    for step in range(CHIPS):
        emb_send[step][pl.ds(0, wide), :] = turned[pl.ds(pl.multiple_of((at[1] ^ step) * wide, wide), wide), :].astype(BF16)
        for index, block in enumerate(packed):
            emb_send[step][pl.ds(wide + 16 * index, 16), :] = block
        emb_send[step][pl.ds(ids_at, 2 * ID_ROWS), :] = id_rows


def both_cores(at, mine, theirs, start, which, step, rows):
    begin = (at[1] ^ step) * LANES
    lanes = pl.ds(pl.multiple_of(begin % rows, LANES), LANES)
    row = pl.multiple_of(which * CHIPS * LANES + begin // rows * rows, LANES)
    return jnp.concatenate([mine[pl.ds(row, rows), lanes], theirs[pl.ds(start + row, rows), lanes]], axis=0)


def halves(refs, ways):
    keep_one, send_one, keep_two, send_two = refs
    half = ways // 2

    def place_of(step, block):
        if block < half:
            return (send_one if step & 1 else keep_one), (step >> 1, block)
        return (send_two if step & 2 else keep_two), (step & 1, block - half)

    return place_of


def pack_small(values, lanes):
    if values.shape[1] % lanes:
        values = jnp.concatenate([values, jnp.zeros((8, -values.shape[1] % lanes), F32)], axis=1)
    packed = []
    for begin in range(0, values.shape[1], lanes):
        block = values[:, begin : begin + lanes]
        high = block.astype(BF16).astype(F32)
        packed.append(jnp.concatenate([high, block - high], axis=0).astype(BF16))
    return packed


def unpack_small(rows):
    return jnp.concatenate([one[:8] + one[8:] for one in rows], axis=1)


def tower_product_kernel(at, sent, mine, theirs, *refs, full, hidden):
    refs = refs[-CHIPS:]
    ways = 2 * refs[0].shape[1]
    place_of = halves(refs, ways)
    rows = mine.shape[1]
    part = hidden // ways
    ends = (full - hidden) // ways
    last = refs[0].shape[2] - 2 * part
    base = round_up(full + hidden, 16)
    top_t = jnp.concatenate([sent[pl.ds(0, full), :], theirs[pl.ds(0, full), :]], axis=1)
    act_t = jnp.concatenate([sent[pl.ds(full, hidden), :], theirs[pl.ds(full, hidden), :]], axis=1)
    for step in range(CHIPS):
        one = dot(top_t, both_cores(at, mine, theirs, base, 0, step, rows))
        two = dot(act_t, both_cores(at, mine, theirs, base, 1, step, rows))
        for block in range(ways):
            own_rows = slice(block * part, (block + 1) * part)
            out, where = place_of(step, block)
            out[*where, pl.ds(0, part), :] = one[own_rows].astype(out.dtype)
            out[*where, pl.ds(part, part), :] = two[own_rows].astype(out.dtype)
            rest = one[hidden + block * ends : hidden + (block + 1) * ends]
            rest = jnp.concatenate([rest, jnp.zeros((last - ends, LANES), F32)], axis=0)
            out[*where, pl.ds(2 * part, last), :] = rest.astype(out.dtype)


def cross_product_kernel(at, sent, mine, theirs, *refs, layers, shard, gap):
    pack = refs[-1]
    ways, extra = pack.shape[0], pack.shape[1]
    place_of = halves(refs[-CHIPS - 1 : -1], ways)
    rows = mine.shape[1]
    low_rows = layers * ways * gap
    base = low_rows + layers * extra
    pack[...] = jnp.zeros_like(pack)

    def lows(layer, block):
        own_rows = pl.ds((layer * ways + block) * gap, gap)
        return jnp.concatenate([sent[own_rows, :], theirs[own_rows, :]], axis=1)

    for layer in range(layers):
        own_rows = pl.ds(low_rows + layer * extra, extra)
        edge = jnp.concatenate([sent[own_rows, :], theirs[own_rows, :]], axis=1)
        for block in range(ways):
            product = dot(edge, lows(layer, block), LANES_IN_LANES)
            pack[block, :, pl.ds(layer * shard, shard)] = product[:, :shard]
    for step in range(CHIPS):
        for layer in range(layers):
            columns = both_cores(at, mine, theirs, base, layer, step, rows)
            for block in range(ways):
                out, where = place_of(step, block)
                out[*where, pl.ds(layer * gap, gap), :] = dot(lows(layer, block), columns).astype(out.dtype)
        for block in range(ways):
            out, where = place_of(step, block)
            lanes = pl.ds(column_of(at, 2 * step), LANES)
            out[*where, pl.ds(layers * gap, extra), :] = pack[block, :, lanes].astype(out.dtype)


def count_rows(counts, base):
    high = jnp.floor(counts * (1.0 / base))
    return jnp.concatenate([high, counts - base * high], axis=0)


def scatter_kernel(at, sent, theirs, *refs, emb, half, fields):
    out, spread, table, columns, highs, counts = refs[-6:]
    chip, core = at[1], at[2]
    part, wide = theirs.shape[2], 2 * LANES
    group = 2 * CHIPS * part
    ways = out.shape[0]
    ids_at = theirs.shape[1] - 2 * ID_ROWS
    slab = emb + 1
    spread[pl.ds(0, MARGIN), :] = jnp.zeros((MARGIN, group), F32)
    spread[pl.ds(MARGIN + wide, 64), :] = jnp.zeros((64, group), F32)
    counts[...] = jnp.zeros_like(counts)
    pad = jnp.zeros((LANES - ID_ROWS, part), F32)
    for rel in range(2 * CHIPS):
        source = (theirs if rel % 2 else sent).at[rel // 2]
        spread[pl.ds(MARGIN, wide), pl.ds(rel * part, part)] = source[pl.ds(0, wide), :].astype(F32)
        low = source[pl.ds(ids_at, ID_ROWS), :].astype(F32)
        columns[pl.ds(rel * part, part), :] = jnp.concatenate([low, pad], axis=0).T
        highs[:, pl.ds(rel * part, part)] = source[pl.ds(ids_at + ID_ROWS, ID_ROWS), :].astype(F32)
    last_row = lax.broadcasted_iota(jnp.int32, (slab, group), 0) == emb
    first_high = (core * half).astype(F32)
    low_iota = lax.broadcasted_iota(jnp.int32, (group, LOW_ROWS), 1).astype(F32)
    for mine in range(CHIPS):

        @pl.when(chip == mine)
        def _(mine=mine):
            first_field = (mine * wide) // emb
            for field in range(first_field, min(fields, (mine * wide + wide - 1) // emb + 1)):
                begin = field * emb - mine * wide + MARGIN
                values = jnp.where(last_row, 1.0, spread[pl.ds(begin, slab), :])
                high_id = highs[pl.ds(field, 1), :] - first_high
                hot = jnp.where(low_iota == columns[:, field : field + 1], 1.0, 0.0).astype(BF16)
                stacked = jnp.concatenate(
                    [
                        jnp.where(high_id == block * 2 * half + piece, values, 0.0)
                        for block in range(ways)
                        for piece in range(half)
                    ],
                    axis=0,
                ).astype(BF16)
                got = dot(stacked, hot)
                for high in range(ways * half):
                    table[high, pl.ds(begin, emb), :] = got[high * slab : high * slab + emb]
                    counts[high, pl.ds(field - first_field, 1), :] = got[high * slab + emb : (high + 1) * slab]

    rows = []
    for begin in range(wide, ids_at, 16):
        rows.append(sum(one[step, pl.ds(begin, 16), :].astype(F32) for one in (sent, theirs) for step in range(CHIPS)))
    packed = pack_small(unpack_small(rows), LOW_ROWS)
    counts_at = half * wide + 16 * len(packed)
    for block in range(ways):
        for piece in range(half):
            values = table[block * half + piece, pl.ds(MARGIN, wide), :]
            out[block, pl.ds(piece * wide, wide), :] = values.astype(BF16)
            out[block, pl.ds(counts_at + 16 * piece, 16), :] = count_rows(counts[block * half + piece], 64.0).astype(BF16)
        for index, rows in enumerate(packed):
            out[block, pl.ds(half * wide + 16 * index, 16), :] = rows


def first_add_kernel(keep_one, got_one, keep_two, got_two, *refs):
    send_one, send_two = refs[-2:]
    send_one[...] = (keep_one[1].astype(F32) + got_one[1].astype(F32)).astype(BF16)
    send_two[...] = (keep_two[1].astype(F32) + got_two[1].astype(F32)).astype(BF16)


def second_add_kernel(at, keep_one, got_one, last_one, keep_two, got_two, last_two, *refs, by_step):
    out = refs[-1]
    half = last_one.shape[0]
    flip = at[0] if by_step else 0
    for first, keep, got, last in ((0, keep_one, got_one, last_one), (half, keep_two, got_two, last_two)):
        for block in range(half):
            total = keep[0, block].astype(F32) + got[0, block].astype(F32) + last[block].astype(F32)
            out[(first + block) ^ flip] = total.astype(BF16)


def add_kernel(*refs, count):
    total = refs[0][...].astype(F32)
    for other in refs[1:count]:
        total = total + other[...].astype(F32)
    refs[-1][...] = total.astype(refs[-1].dtype)


def fold_kernel(parts, *refs):
    total = parts[0].astype(F32)
    for block in range(1, parts.shape[0]):
        total = total + parts[block].astype(F32)
    refs[-1][...] = total.astype(refs[-1].dtype)


def table_fold_kernel(parts, *refs, half):
    out, small = refs[-2:]
    total = parts[0].astype(F32)
    for block in range(1, parts.shape[0]):
        total = total + parts[block].astype(F32)
    table_rows = out.shape[0] - 16 * half
    counts_at = total.shape[0] - 16 * half
    out[pl.ds(0, table_rows), :] = total[:table_rows].astype(BF16)
    small[...] = unpack_small([total[begin : begin + 16] for begin in range(table_rows, counts_at, 16)])
    for piece in range(half):
        rows = total[counts_at + 16 * piece : counts_at + 16 * (piece + 1)]
        out[pl.ds(table_rows + 16 * piece, 16), :] = count_rows(64.0 * rows[:8] + rows[8:], 256.0).astype(BF16)


def table_kernel(at, *refs, emb):
    pieces, (out, counts) = refs[: 2 * CHIPS], refs[-2:]
    wide, low = 2 * LANES, LOW_ROWS
    half = pieces[0].shape[0] // wide
    fields = counts.shape[0]
    last = CHIPS - 1
    for rel, piece in enumerate(pieces):
        chip = at[1] ^ (rel // 2)
        core = at[2] ^ (rel % 2)
        for block in range(half):
            lanes = pl.ds(pl.multiple_of((core * half + block) * low, low), low)
            values = piece[pl.ds(block * wide, wide), :].astype(F32)
            numbers = piece[pl.ds(half * wide + 16 * block, 16), :].astype(F32)
            numbers = (256.0 * numbers[:8] + numbers[8:]).astype(jnp.int32)
            for mine in range(CHIPS):

                @pl.when(chip == mine)
                def _(mine=mine, lanes=lanes, values=values, numbers=numbers):
                    height = wide if mine < last else out.shape[0] - last * wide
                    out[pl.ds(mine * wide, height), lanes] = values[:height]
                    first_field = (mine * wide) // emb
                    count = min(fields, (mine * wide + wide - 1) // emb + 1) - first_field
                    counts[pl.ds(first_field, count), lanes] = numbers[:count]


def tower_kernel(at, *refs):
    pieces, (one_out, two_out) = refs[: 2 * CHIPS], refs[-2:]
    ways = pieces[0].shape[0]
    hidden = two_out.shape[0]
    part = hidden // ways
    ends = (one_out.shape[0] - hidden) // ways
    for rel, piece in enumerate(pieces):
        lanes = pl.ds(column_of(at, rel), LANES)
        for block in range(ways):
            source = block ^ at[0]
            one_out[pl.ds(block * part, part), lanes] = piece[source, pl.ds(0, part), :].astype(F32)
            two_out[pl.ds(block * part, part), lanes] = piece[source, pl.ds(part, part), :].astype(F32)
            rest = piece[source, pl.ds(2 * part, 16), :].astype(F32)
            one_out[pl.ds(hidden + block * ends, ends), lanes] = rest[:ends]


def cross_kernel(at, *refs, gap):
    pieces, out, pack = refs[: 2 * CHIPS], refs[-2], refs[-1]
    layers, shard, full = out.shape
    main = pack.shape[1]
    extra = full - main
    for rel, piece in enumerate(pieces):
        lanes = pl.ds(column_of(at, rel), LANES)
        for layer in range(layers):
            out[layer, :, lanes] = piece[pl.ds(layer * gap, gap), :].astype(F32)[:shard]
        pack[pl.ds(0, extra), lanes] = piece[pl.ds(layers * gap, extra), :].astype(F32)
    pack[pl.ds(extra, pack.shape[0] - extra), :] = jnp.zeros((pack.shape[0] - extra, main), F32)
    turned = pack[...].T
    for layer in range(layers):
        out[layer, :, pl.ds(main, extra)] = turned[layer * shard : (layer + 1) * shard, :extra]


def in_hbm(value):
    return pltpu.with_memory_space_constraint(value, pltpu.HBM)


def vmem_bytes(one):
    *lead, rows, lanes = one.shape
    size = jnp.dtype(one.dtype).itemsize
    return math.prod(lead) * round_up(rows, 32 // size) * round_up(lanes, LANES) * size


def local(kernel, out_shape, operands, after=(), scratch=(), in_place=(), name=None, **options):
    operands = list(operands)
    smem = [index for index, one in enumerate(operands) if one.shape == (3,)]
    specs = [
        IN_SMEM if index in smem else IN_PLACE if index in in_place else IN_VMEM for index in range(len(operands))
    ]
    outs = out_shape if isinstance(out_shape, list) else [out_shape]
    held = [one for index, one in enumerate(operands) if index not in (*smem, *in_place)] + outs
    held += [one for one in scratch if len(one.shape) > 1]
    space = sum(vmem_bytes(one) for one in held) + SPARE_BYTES[name]
    got = pl.pallas_call(
        functools.partial(kernel, **options),
        out_shape=outs,
        in_specs=specs + [IN_PLACE] * len(after),
        out_specs=[IN_VMEM] * len(outs),
        scratch_shapes=list(scratch),
        compiler_params=pltpu.CompilerParams(vmem_limit_bytes=space),
        cost_estimate=pl.CostEstimate(flops=int(COST * MICROS[name]), bytes_accessed=0, transcendentals=0),
        name=name,
    )(*operands, *after)
    return got if isinstance(out_shape, list) else got[0]


class Links:
    def __init__(self, dp_size, cross_size):
        bits = dp_size.bit_length() - 1
        axis_bits = (bits - 1) // 2
        self.dp_size, self.cross_size = dp_size, cross_size
        self.core = 1
        self.chip_masks = (1 << 1, 1 << (1 + axis_bits))
        used = (self.core, *self.chip_masks)
        self.others = tuple(1 << bit for bit in range(bits) if 1 << bit not in used)

    def chip_mask(self, step):
        return sum(mask for bit, mask in enumerate(self.chip_masks) if step >> bit & 1)

    def chip(self, dp_place):
        return sum((dp_place // mask % 2) << bit for bit, mask in enumerate(self.chip_masks))

    def over_dp(self, value, mask):
        return lax.ppermute(value, "dp", [(one, one ^ mask) for one in range(self.dp_size)])

    def over_cross(self, value, mask):
        return lax.ppermute(value, "cross", [(one, one ^ mask) for one in range(self.cross_size)])

    def chips_swap(self, value_of):
        return [self.over_dp(value_of(step), self.chip_mask(step)) for step in range(1, CHIPS)]

    def cross_swap(self, value_of):
        return [self.over_cross(value_of(step), step) for step in range(1, self.cross_size)]

    def cross_exchange(self, value):
        return lax.all_to_all(value, "cross", split_axis=0, concat_axis=0, tiled=True)

    def add_others(self, value):
        for mask in self.others:
            value = (value.astype(F32) + self.over_dp(value, mask).astype(F32)).astype(BF16)
        return value

    def over_others(self, value):
        for mask in self.others:
            value = value + self.over_dp(value, mask)
        return value


    def plane_first(self, parts, after, name):
        keep_one, send_one, keep_two, send_two = parts
        one, two = self.chip_masks
        got_one, got_two = self.over_dp(send_one, one), self.over_dp(send_two, two)
        part = Shape(send_one.shape[1:], BF16)
        next_one, next_two = local(first_add_kernel, [part, part], [keep_one, got_one, keep_two, got_two], after, name=name)
        return keep_one, got_one, next_one, keep_two, got_two, next_two

    def plane_second(self, parts, at, by_step, after, name):
        keep_one, got_one, next_one, keep_two, got_two, next_two = parts
        one, two = self.chip_masks
        last_one, last_two = self.over_dp(next_one, two), self.over_dp(next_two, one)
        total = local(
            second_add_kernel,
            Shape((2 * next_one.shape[0], *next_one.shape[1:]), BF16),
            [at, keep_one, got_one, last_one, keep_two, got_two, last_two],
            after,
            name=name,
            by_step=by_step,
        )
        return self.add_others(total)

    def both_cores(self, arrays):
        return [each for one in arrays for each in (one, self.over_dp(one, self.core))]

    def plane_gather(self, value):
        return self.both_cores([value, *self.chips_swap(lambda step: value)])


def body(
    emb_table,
    dense_input,
    feature_ids,
    labels,
    cross_weight,
    cross_bias,
    tower_one,
    bias_one,
    tower_two,
    bias_two,
    out_weight,
    out_bias,
):
    layers, shard, full = cross_weight.shape
    group, fields = feature_ids.shape
    rows_here, emb_end = emb_table.shape
    emb = emb_end // fields
    dense_width = dense_input.shape[1]
    hidden = tower_one.shape[1]
    main = hidden
    extra = full - main
    ways = lax.axis_size("cross")
    place = lax.axis_index("cross")
    dp_place = lax.axis_index("dp")
    links = Links(lax.axis_size("dp"), ways)
    rows = group // ways
    scale = 1.0 / (group * links.dp_size)
    chip, core = links.chip(dp_place), dp_place % 2
    at = jnp.stack([place, chip, core]).astype(jnp.int32)
    wide = 2 * LANES
    gap = round_up(shard + 8, 16)

    blocks = -(-shard // LANES)
    ends = jnp.pad(cross_weight[:, :, main:].transpose(0, 2, 1), ((0, 0), (0, 0), (0, blocks * LANES - shard)))
    ends = ends.reshape(layers, extra, blocks, LANES).transpose(0, 2, 1, 3).reshape(layers, blocks * extra, LANES)
    ends_bias = jnp.pad(cross_bias, ((0, 0), (0, blocks * LANES - shard))).reshape(layers, blocks, LANES)
    own_tail = jnp.concatenate([ends, ends_bias], axis=1)
    own_tail = jnp.pad(own_tail, ((0, 0), (0, 64 - own_tail.shape[1]), (0, 0)))
    part = chip * 2 + core
    own_block = jnp.concatenate(
        [
            lax.dynamic_slice_in_dim(cross_weight, part * LANES, LANES, 2),
            jnp.zeros((layers, gap - 8 - shard, LANES), BF16),
            lax.dynamic_slice_in_dim(own_tail, part * 8, 8, 1),
        ],
        axis=1,
    )
    foreign = links.cross_swap(lambda step: own_block)

    ids_t = feature_ids.T
    emb_rows = round_up(emb_end + 1, 8)
    looked = local(
        lookup_kernel,
        Shape((ways, emb_rows, rows), BF16),
        [at, emb_table.T, ids_t],
        scratch=[pltpu.VMEM((emb_rows, rows_here), F32), pltpu.VMEM((emb_rows, group), F32)],
        name="lookup",
        fields=fields,
        emb=emb,
    )
    *foreign, looked = lax.optimization_barrier((*foreign, looked))
    parts = links.cross_exchange(looked)
    own_ids = lax.dynamic_slice_in_dim(ids_t, place * rows, rows, 1)
    foreign = jnp.stack(foreign)
    foreign = [foreign, *links.chips_swap(lambda step: foreign)]
    pieces = [in_hbm(one) for one in links.both_cores(foreign)]

    own_dense = lax.dynamic_slice_in_dim(dense_input.T, place * rows, rows, 1)
    dense_t = jnp.pad(own_dense.astype(F32), ((0, round_up(dense_width, 8) - dense_width), (0, 0)))
    own_full = jnp.pad(cross_weight[:, :, :main], ((0, 0), (0, gap - shard), (0, 0)))
    turned_rows = round_up(full, LANES)
    emb_shape = Shape((wide + 16 * -(-turned_rows // rows) + 2 * ID_ROWS, rows), BF16)
    tower_factors = round_up(full + hidden, 16)
    cross_factors = layers * (ways * gap + extra)
    logits, dense_grad, *emb_send, tower_other, tower_mine, cross_other, cross_mine = local(
        step_kernel,
        [
            Shape((1, rows), F32),
            Shape((dense_width, rows), F32),
            *[emb_shape] * CHIPS,
            Shape((tower_factors + 2 * CHIPS * LANES, rows), BF16),
            Shape((2 * CHIPS * LANES, rows), BF16),
            Shape((cross_factors + layers * CHIPS * LANES, rows), BF16),
            Shape((layers * CHIPS * LANES, rows), BF16),
        ],
        [
            at,
            parts,
            dense_t,
            in_hbm(own_full),
            own_tail,
            *pieces,
            in_hbm(tower_one),
            bias_one[None, :],
            in_hbm(tower_two),
            bias_two[None, :],
            out_weight[None, :],
            out_bias[None, :],
            labels[None, :],
            own_ids,
        ],
        [],
        [
            pltpu.VMEM((ways, layers, gap, main), BF16),
            pltpu.VMEM((full, hidden), BF16),
            pltpu.VMEM((hidden, hidden), BF16),
            pltpu.VMEM((ways, layers, 64, LANES), F32),
            pltpu.VMEM((8, turned_rows), F32),
            pltpu.VMEM((8, turned_rows), F32),
            pltpu.VMEM((turned_rows, rows), F32),
            pltpu.VMEM((rows, full), F32),
            pltpu.VMEM((rows, full), F32),
            pltpu.VMEM((layers, rows, full), BF16),
            pltpu.VMEM((layers, rows, full), F32),
            pltpu.SemaphoreType.DMA((3 + 2 * CHIPS * (ways - 1),)),
        ],
        in_place=(3, *range(5, 6 + 2 * CHIPS), 7 + 2 * CHIPS),
        name="step",
        shard=shard,
        emb_end=emb_end,
        scale=scale,
    )

    tower_theirs = links.over_dp(tower_other, links.core)
    cross_theirs = links.over_dp(cross_other, links.core)
    emb_got = links.chips_swap(lambda step: emb_send[step])

    tower_rows = round_up(2 * (hidden // ways) + extra // ways, 16)
    tower_shape = (ways, tower_rows, LANES)
    split = lambda shape: Shape((2, shape[0] // 2, *shape[1:]), BF16)
    tower_parts = local(
        tower_product_kernel,
        [split(tower_shape)] * 4,
        [at, tower_other, tower_mine, tower_theirs],
        name="tower_products",
        full=full,
        hidden=hidden,
    )


    cross_rows = layers * gap + extra
    cross_shape = (ways, cross_rows, LANES)
    cross_parts = local(
        cross_product_kernel,
        [split(cross_shape)] * 4,
        [at, cross_other, cross_mine, cross_theirs],
        [tower_parts[0]],
        [pltpu.VMEM((ways, extra, main), F32)],
        name="cross_products",
        layers=layers,
        shard=shard,
        gap=gap,
    )
    tower_first = links.plane_first(tower_parts, [cross_parts[0]], "tower_first")

    *emb_got, _ = lax.optimization_barrier((*emb_got, cross_parts[0]))
    emb_parts = jnp.stack([emb_send[0], *emb_got])
    emb_theirs = links.over_dp(emb_parts, links.core)
    half = rows_here // LOW_ROWS // 2
    table_ends = 16 * -(-turned_rows // LOW_ROWS)
    table_parts = local(
        scatter_kernel,
        Shape((ways, half * wide + table_ends + 16 * half, LOW_ROWS), BF16),
        [at, emb_parts, emb_theirs],
        [tower_first[2]],
        [
            pltpu.VMEM((MARGIN + wide + 64, rows * 2 * CHIPS), F32),
            pltpu.VMEM((ways * half, MARGIN + wide + 64, LOW_ROWS), F32),
            pltpu.VMEM((rows * 2 * CHIPS, LANES), F32),
            pltpu.VMEM((ID_ROWS, rows * 2 * CHIPS), F32),
            pltpu.VMEM((ways * half, 8, LOW_ROWS), F32),
        ],
        name="scatter",
        emb=emb,
        half=half,
        fields=fields,
    )
    table_parts = links.add_others(table_parts)
    table_got = links.cross_exchange(table_parts)
    tower_sum = links.plane_second(tower_first, at, True, [table_parts], "tower_second")
    tower_got = links.cross_swap(lambda step: tower_sum[step])
    tower_fold = local(
        add_kernel, Shape(tower_shape[1:], BF16), [tower_sum[0], *tower_got], name="tower_fold", count=ways
    )
    keep_one, send_one, keep_two, send_two = cross_parts
    send_one, send_two, _ = lax.optimization_barrier((send_one, send_two, tower_first[2]))
    cross_first = links.plane_first((keep_one, send_one, keep_two, send_two), [tower_fold], "cross_first")
    cross_sum = links.plane_second(cross_first, at, False, [], "cross_second")
    table_fold, small = local(
        table_fold_kernel,
        [Shape((half * (wide + 16), LOW_ROWS), BF16), Shape((8, round_up(turned_rows, LOW_ROWS)), F32)],
        [table_got],
        [cross_sum],
        name="table_fold",
        half=half,
    )
    table_all = links.chips_swap(lambda step: table_fold)
    tower_all = jnp.stack([tower_fold, *links.cross_swap(lambda step: tower_fold)])
    cross_got = links.cross_exchange(cross_sum)
    *table_all, _ = lax.optimization_barrier((*table_all, cross_sum))
    table_all = links.both_cores([table_fold, *table_all])
    tower_blocks = links.chips_swap(lambda step: tower_all)
    table_grad, row_counts = local(
        table_kernel,
        [Shape((emb_end, rows_here), F32), Shape((fields, rows_here), jnp.int32)],
        [at, *table_all],
        [cross_sum],
        name="table",
        emb=emb,
    )
    cross_fold = local(fold_kernel, Shape(cross_shape[1:], BF16), [cross_got], [table_grad], name="cross_fold")
    *tower_blocks, _ = lax.optimization_barrier((*tower_blocks, cross_fold))
    tower_blocks = links.both_cores([tower_all, *tower_blocks])
    tower_one_grad, tower_two_grad = local(
        tower_kernel, [Shape((full, hidden), F32), Shape((hidden, hidden), F32)], [at, *tower_blocks], name="towers"
    )
    cross_weight_grad = local(
        cross_kernel,
        Shape((layers, shard, full), F32),
        [at, *links.plane_gather(cross_fold)],
        scratch=[pltpu.VMEM((LANES, main), F32)],
        name="cross",
        gap=gap,
    )
    cross_bias_grad = lax.dynamic_slice_in_dim(small[4 : 4 + layers], place * shard, shard, 1)
    return (
        small[7, 0],
        logits[0],
        dense_grad.T,
        table_grad.T,
        cross_weight_grad,
        cross_bias_grad,
        tower_one_grad,
        small[0, :hidden],
        tower_two_grad,
        small[1, :hidden],
        jnp.concatenate([small[2, :full], small[3, :hidden]]),
        small[7, 1:2],
        row_counts.T,
    )


def solution(mesh):
    in_specs = (
        P("cross", None),
        P("dp", None),
        P("dp", None),
        P(("dp", "cross")),
        P(None, "cross", None),
        P(None, "cross"),
        P(),
        P(),
        P(),
        P(),
        P(),
        P(),
    )
    out_specs = (
        P(),
        P(("dp", "cross")),
        P(("dp", "cross"), None),
        P("cross", None),
        P(None, "cross", None),
        P(None, "cross"),
        P(),
        P(),
        P(),
        P(),
        P(),
        P(),
        P("cross", None),
    )
    return jax.shard_map(body, mesh=mesh, in_specs=in_specs, out_specs=out_specs, check_vma=False)
```

```python
import collections
import functools
import math

import jax
import jax.numpy as jnp
from jax import lax
from jax.experimental import pallas as pl
from jax.experimental.pallas import tpu as pltpu
from jax.sharding import PartitionSpec as P

F32 = jnp.float32
BF16 = jnp.bfloat16
ROWS_IN_ROWS = (((0,), (0,)), ((), ()))
LANES_IN_LANES = (((1,), (1,)), ((), ()))
LANES = 128
LOW_BITS = 8
LOW_ROWS = 1 << LOW_BITS
CHIPS = 4
MARGIN = 48
ID_ROWS = 32
STEP_SPARE = 8 << 20
SPARE_BYTES = collections.defaultdict(lambda: 3 << 20, step=STEP_SPARE)
COST = 5.75e+09
MICROS = dict(
    lookup=7.4,
    count=5.2,
    step=23,
    tower_products=5.9,
    scatter=7,
    cross_products=8.9,
    tower_first=3.1,
    tower_second=2.3,
    table_fold=2,
    tower_fold=1.8,
    cross_first=4,
    cross_second=2.7,
    cross_fold=1.9,
    table=3.9,
    towers=6.8,
    cross=3.6,
)
IN_VMEM = pl.BlockSpec(memory_space=pltpu.VMEM)
IN_SMEM = pl.BlockSpec(memory_space=pltpu.SMEM)
IN_PLACE = pl.BlockSpec(memory_space=pl.ANY)
Shape = jax.ShapeDtypeStruct


def round_up(size, step):
    return -(-size // step) * step


def dot(left, right, dims=(((1,), (0,)), ((), ()))):
    return lax.dot_general(left, right, dims, preferred_element_type=F32)


def silu_slope(pre_act):
    sigmoid_part = jax.nn.sigmoid(pre_act)
    return sigmoid_part * (1.0 + pre_act * (1.0 - sigmoid_part))


def lookup_kernel(at, table, ids, out, floats, gathered, *, fields, emb):
    ways = out.shape[0]
    highs = table.shape[1] // LOW_ROWS
    group = ids.shape[1]
    part = group // ways
    slab = emb + 1
    floats[pl.ds(0, table.shape[0]), :] = table[...].astype(F32)
    low_iota = lax.broadcasted_iota(jnp.int32, (LOW_ROWS, group), 0)
    for field in range(fields):
        left = jnp.concatenate(
            [floats[pl.ds(field * emb, slab), pl.ds(high * LOW_ROWS, LOW_ROWS)] for high in range(highs)], axis=0
        ).astype(BF16)
        local = ids[pl.ds(field, 1), :] - at[0] * (highs * LOW_ROWS)
        low = jnp.bitwise_and(local, LOW_ROWS - 1)
        high_id = jnp.right_shift(local, LOW_BITS)
        hot = jnp.where(low_iota == low, 1.0, 0.0).astype(BF16)
        picked = dot(left, hot)
        total = jnp.zeros((slab, group), F32)
        for high in range(highs):
            total = total + jnp.where(high_id == high, picked[high * slab : (high + 1) * slab], 0.0)
        gathered[pl.ds(field * emb, slab), :] = total
    for block in range(ways):
        out[block] = gathered[:, pl.ds(block * part, part)].astype(BF16)


def column_of(at, rel):
    return pl.multiple_of(((at[1] ^ (rel // 2)) * 2 + (at[2] ^ (rel % 2))) * LANES, LANES)


def column_pick(at, values, mine):
    first = at[2] == 0 if mine else at[2] == 1
    blocks = []
    for one in range(CHIPS):
        low, high = values[:, 2 * one * LANES : (2 * one + 1) * LANES], values[:, (2 * one + 1) * LANES : (2 * one + 2) * LANES]
        blocks.append(jnp.where(first, low, high))
    picked = jnp.concatenate(blocks, axis=1).astype(BF16)
    rows = values.shape[0]
    return [picked[:, begin : begin + rows] for begin in range(0, CHIPS * LANES, rows)]


def step_kernel(at, *refs, shard, emb_end, scale):
    refs = list(refs)
    take = lambda count: [refs.pop(0) for _ in range(count)]
    (parts, dense_t, own, own_tail), pieces = take(4), take(2 * CHIPS)
    one_at, one_b, two_at, two_b, out_w, out_b, labels, ids = take(8)
    (logits_out, dense_grad), emb_send = take(2), take(CHIPS)
    tower_other, tower_mine, cross_other, cross_mine = take(4)
    weights, one_w, two_w, tails, bias, small, turned, first, state, lows, mixes, spread, edges, sems = take(14)
    place = at[0]
    ways, layers, gap, main = weights.shape
    rows = parts.shape[2]
    full = first.shape[1]
    extra = full - main
    hidden = one_w.shape[1]
    blocks = -(-shard // LANES)
    copies, count = [], 1 + len(pieces) * (ways - 1)
    for layer in range(layers):
        sem = iter(sems.at[layer * count + index] for index in range(count))
        copies.append([pltpu.make_async_copy(own.at[layer], weights.at[place, layer], next(sem))])
        for rel, piece in enumerate(pieces):
            for step in range(1, ways):
                target = weights.at[place ^ step, layer, :, pl.ds(column_of(at, rel), LANES)]
                copies[layer].append(pltpu.make_async_copy(piece.at[step - 1, layer], target, next(sem)))
    towers = [
        pltpu.make_async_copy(one_at, one_w, sems.at[layers * count]),
        pltpu.make_async_copy(two_at, two_w, sems.at[layers * count + 1]),
    ]
    for copy in sum(copies, []) + towers:
        copy.start()
    tails[place] = own_tail[...].astype(F32)
    spread[...] = jnp.zeros_like(spread)
    edges[...] = jnp.zeros_like(edges)
    wide_rows = ways * gap
    looked = parts[0].astype(F32)
    for block in range(1, ways):
        looked = looked + parts[block].astype(F32)
    turned[pl.ds(0, looked.shape[0]), :] = looked
    turned[pl.ds(emb_end, dense_t.shape[0]), :] = dense_t[...]
    used = emb_end + dense_t.shape[0]
    turned[pl.ds(used, turned.shape[0] - used), :] = jnp.zeros((turned.shape[0] - used, rows), F32)
    start = turned[...].T[:, :full]
    first[...] = start
    state[...] = start
    for layer in range(layers):
        for copy in copies[layer]:
            copy.wait()
        for block in range(ways):
            ends = weights[block, layer, pl.ds(gap - 16, 16), :].astype(F32)[8:]

            @pl.when(place != block)
            def _(block=block, layer=layer, ends=ends):
                for one in range(2 * CHIPS):
                    tails[block, layer, pl.ds(8 * one, 8), :] = ends[:, one * LANES : (one + 1) * LANES]

            row = [tails[block, layer, pl.ds(blocks * extra + one, 1), :] for one in range(blocks)]
            bias[pl.ds(layer, 1), pl.ds(block * shard, shard)] = jnp.concatenate(row, axis=1)[:, :shard]
            edge = [tails[block, layer, pl.ds(one * extra, extra), :] for one in range(blocks)]
            edges[layer, :, pl.ds(block * gap, shard)] = jnp.concatenate(edge, axis=1)[:, :shard]
        lows[layer] = state[...].astype(BF16)
        for block in range(ways):
            spread[:, pl.ds(block * gap, shard)] = state[:, pl.ds(block * shard, shard)]
        low = spread[:, pl.ds(0, wide_rows)].astype(BF16)
        body = dot(low, weights[:, layer].reshape(wide_rows, main))
        edge = dot(low, edges[layer, :, pl.ds(0, wide_rows)].astype(BF16), LANES_IN_LANES)
        mixed = jnp.concatenate([body, edge], axis=1) + bias[pl.ds(layer, 1), :full]
        mixes[layer] = mixed
        state[...] = first[...] * mixed + state[...]

    for copy in towers:
        copy.wait()
    top = state[...].astype(BF16)
    hid_one = dot(top, one_w[...]) + one_b[...]
    act_one = jax.nn.silu(hid_one).astype(BF16)
    hid_two = dot(act_one, two_w[...]) + two_b[...]
    act_two = jax.nn.silu(hid_two).astype(BF16)
    top_float, act_float = top.astype(F32), act_two.astype(F32)
    weight_top = out_w[:, :full].astype(F32)
    weight_act = out_w[:, full:].astype(F32)
    logits = (
        jnp.sum(top_float * weight_top, axis=1, keepdims=True)
        + jnp.sum(act_float * weight_act, axis=1, keepdims=True)
        + out_b[...]
    )
    logits_out[...] = jnp.broadcast_to(logits, (rows, LANES)).T[:1]
    label = jnp.broadcast_to(labels[...].astype(F32), (LANES, rows)).T[:, :1]
    loss = jnp.sum(jax.nn.softplus(logits) - label * logits, axis=0, keepdims=True) * scale
    g_logit = ((jax.nn.sigmoid(logits) - label) * scale).astype(BF16).astype(F32)
    g_two = (g_logit * weight_act * silu_slope(hid_two)).astype(BF16)
    g_one = (dot(g_two, two_w[...], LANES_IN_LANES) * silu_slope(hid_one)).astype(BF16)
    grad = (dot(g_one, one_w[...], LANES_IN_LANES) + g_logit * weight_top).astype(BF16).astype(F32)
    one_float, two_float = g_one.astype(F32), g_two.astype(F32)
    lane = lax.broadcasted_iota(jnp.int32, (1, LANES), 1)
    bias_grad = jnp.sum(g_logit, axis=0, keepdims=True)
    small[...] = jnp.zeros_like(small)
    small[pl.ds(0, 1), pl.ds(0, hidden)] = jnp.sum(one_float, axis=0, keepdims=True)
    small[pl.ds(1, 1), pl.ds(0, hidden)] = jnp.sum(two_float, axis=0, keepdims=True)
    small[pl.ds(2, 1), pl.ds(0, full)] = jnp.sum(top_float * g_logit, axis=0, keepdims=True)
    small[pl.ds(3, 1), pl.ds(0, hidden)] = jnp.sum(act_float * g_logit, axis=0, keepdims=True)
    small[pl.ds(7, 1), pl.ds(0, LANES)] = jnp.where(lane == 0, loss, jnp.where(lane == 1, bias_grad, 0.0))
    tower_other[pl.ds(0, full), :] = top_float.T.astype(BF16)
    tower_other[pl.ds(full, hidden), :] = act_one.astype(F32).T.astype(BF16)
    base = round_up(full + hidden, 16)
    span = CHIPS * LANES
    for which, values in enumerate((one_float, two_float)):
        for index, block in enumerate(column_pick(at, values, False)):
            tower_other[pl.ds(base + which * span + index * rows, rows), :] = block
        for index, block in enumerate(column_pick(at, values, True)):
            tower_mine[pl.ds(which * span + index * rows, rows), :] = block

    inputs = first[...]
    pad = jnp.zeros((rows, turned.shape[0] - full), F32)
    total = jnp.zeros_like(grad)
    low_rows = layers * ways * gap
    base = low_rows + layers * extra
    for layer in reversed(range(layers)):
        rounded = (grad * inputs).astype(BF16)
        values = rounded.astype(F32)
        small[pl.ds(4 + layer, 1), pl.ds(0, full)] = jnp.sum(values, axis=0, keepdims=True)
        total = total + grad * mixes[layer]
        spread[:, pl.ds(0, wide_rows)] = dot(
            rounded[:, :main], weights[:, layer].reshape(wide_rows, main), LANES_IN_LANES
        ) + dot(rounded[:, main:full], edges[layer, :, pl.ds(0, wide_rows)].astype(BF16))
        backs = [spread[:, pl.ds(block * gap, shard)] for block in range(ways)]
        grad = grad + jnp.concatenate(backs, axis=1)
        for index, block in enumerate(column_pick(at, values, False)):
            cross_other[pl.ds(base + layer * span + index * rows, rows), :] = block
        for index, block in enumerate(column_pick(at, values, True)):
            cross_mine[pl.ds(layer * span + index * rows, rows), :] = block
        edge = jnp.concatenate([values[:, main:full], jnp.zeros((rows, LANES - extra), F32)], axis=1).T
        cross_other[pl.ds(low_rows + layer * extra, extra), :] = edge[:extra].astype(BF16)
        turned[...] = jnp.concatenate([lows[layer].astype(F32), pad], axis=1).T
        for block in range(ways):
            low_t = jnp.concatenate([turned[pl.ds(block * shard, shard), :], jnp.zeros((gap - shard, rows), F32)], axis=0)
            cross_other[pl.ds((layer * ways + block) * gap, gap), :] = low_t.astype(BF16)
    total = total + grad
    turned[...] = jnp.concatenate([total, pad], axis=1).T
    dense_grad[...] = turned[pl.ds(emb_end, dense_grad.shape[0]), :]
    wide = 2 * LANES
    packed = pack_small(small[...], rows)
    fields = ids.shape[0]
    blank = jnp.zeros((ID_ROWS - fields, rows), F32)
    low_ids = jnp.bitwise_and(ids[...], LOW_ROWS - 1).astype(F32)
    high_ids = jnp.right_shift(ids[...], LOW_BITS).astype(F32)
    id_rows = jnp.concatenate([low_ids, blank, high_ids, blank], axis=0).astype(BF16)
    ids_at = wide + 16 * len(packed)
    for step in range(CHIPS):
        emb_send[step][pl.ds(0, wide), :] = turned[pl.ds(pl.multiple_of((at[1] ^ step) * wide, wide), wide), :].astype(BF16)
        for index, block in enumerate(packed):
            emb_send[step][pl.ds(wide + 16 * index, 16), :] = block
        emb_send[step][pl.ds(ids_at, 2 * ID_ROWS), :] = id_rows


def both_cores(at, mine, theirs, start, which, step, rows):
    begin = (at[1] ^ step) * LANES
    lanes = pl.ds(pl.multiple_of(begin % rows, LANES), LANES)
    row = pl.multiple_of(which * CHIPS * LANES + begin // rows * rows, LANES)
    return jnp.concatenate([mine[pl.ds(row, rows), lanes], theirs[pl.ds(start + row, rows), lanes]], axis=0)


def halves(refs, ways):
    keep_one, send_one, keep_two, send_two = refs
    half = ways // 2

    def place_of(step, block):
        if block < half:
            return (send_one if step & 1 else keep_one), (step >> 1, block)
        return (send_two if step & 2 else keep_two), (step & 1, block - half)

    return place_of


def pack_small(values, lanes):
    if values.shape[1] % lanes:
        values = jnp.concatenate([values, jnp.zeros((8, -values.shape[1] % lanes), F32)], axis=1)
    packed = []
    for begin in range(0, values.shape[1], lanes):
        block = values[:, begin : begin + lanes]
        high = block.astype(BF16).astype(F32)
        packed.append(jnp.concatenate([high, block - high], axis=0).astype(BF16))
    return packed


def unpack_small(rows):
    return jnp.concatenate([one[:8] + one[8:] for one in rows], axis=1)


def tower_product_kernel(at, sent, mine, theirs, *refs, full, hidden):
    refs = refs[-CHIPS:]
    ways = 2 * refs[0].shape[1]
    place_of = halves(refs, ways)
    rows = mine.shape[1]
    part = hidden // ways
    ends = (full - hidden) // ways
    last = refs[0].shape[2] - 2 * part
    base = round_up(full + hidden, 16)
    top_t = jnp.concatenate([sent[pl.ds(0, full), :], theirs[pl.ds(0, full), :]], axis=1)
    act_t = jnp.concatenate([sent[pl.ds(full, hidden), :], theirs[pl.ds(full, hidden), :]], axis=1)
    for step in range(CHIPS):
        one = dot(top_t, both_cores(at, mine, theirs, base, 0, step, rows))
        two = dot(act_t, both_cores(at, mine, theirs, base, 1, step, rows))
        for block in range(ways):
            own_rows = slice(block * part, (block + 1) * part)
            out, where = place_of(step, block)
            out[*where, pl.ds(0, part), :] = one[own_rows].astype(out.dtype)
            out[*where, pl.ds(part, part), :] = two[own_rows].astype(out.dtype)
            rest = one[hidden + block * ends : hidden + (block + 1) * ends]
            rest = jnp.concatenate([rest, jnp.zeros((last - ends, LANES), F32)], axis=0)
            out[*where, pl.ds(2 * part, last), :] = rest.astype(out.dtype)


def cross_product_kernel(at, sent, mine, theirs, *refs, layers, shard, gap):
    pack = refs[-1]
    ways, extra = pack.shape[0], pack.shape[1]
    place_of = halves(refs[-CHIPS - 1 : -1], ways)
    rows = mine.shape[1]
    low_rows = layers * ways * gap
    base = low_rows + layers * extra
    pack[...] = jnp.zeros_like(pack)

    def lows(layer, block):
        own_rows = pl.ds((layer * ways + block) * gap, gap)
        return jnp.concatenate([sent[own_rows, :], theirs[own_rows, :]], axis=1)

    for layer in range(layers):
        own_rows = pl.ds(low_rows + layer * extra, extra)
        edge = jnp.concatenate([sent[own_rows, :], theirs[own_rows, :]], axis=1)
        for block in range(ways):
            product = dot(edge, lows(layer, block), LANES_IN_LANES)
            pack[block, :, pl.ds(layer * shard, shard)] = product[:, :shard]
    for step in range(CHIPS):
        for layer in range(layers):
            columns = both_cores(at, mine, theirs, base, layer, step, rows)
            for block in range(ways):
                out, where = place_of(step, block)
                out[*where, pl.ds(layer * gap, gap), :] = dot(lows(layer, block), columns).astype(out.dtype)
        for block in range(ways):
            out, where = place_of(step, block)
            lanes = pl.ds(column_of(at, 2 * step), LANES)
            out[*where, pl.ds(layers * gap, extra), :] = pack[block, :, lanes].astype(out.dtype)


def count_rows(counts, base):
    high = jnp.floor(counts * (1.0 / base))
    return jnp.concatenate([high, counts - base * high], axis=0)


def scatter_kernel(at, sent, theirs, *refs, emb, half, fields):
    out, spread, table, columns, highs, counts = refs[-6:]
    chip, core = at[1], at[2]
    part, wide = theirs.shape[2], 2 * LANES
    group = 2 * CHIPS * part
    ways = out.shape[0]
    ids_at = theirs.shape[1] - 2 * ID_ROWS
    slab = emb + 1
    spread[pl.ds(0, MARGIN), :] = jnp.zeros((MARGIN, group), F32)
    spread[pl.ds(MARGIN + wide, 64), :] = jnp.zeros((64, group), F32)
    counts[...] = jnp.zeros_like(counts)
    pad = jnp.zeros((LANES - ID_ROWS, part), F32)
    for rel in range(2 * CHIPS):
        source = (theirs if rel % 2 else sent).at[rel // 2]
        spread[pl.ds(MARGIN, wide), pl.ds(rel * part, part)] = source[pl.ds(0, wide), :].astype(F32)
        low = source[pl.ds(ids_at, ID_ROWS), :].astype(F32)
        columns[pl.ds(rel * part, part), :] = jnp.concatenate([low, pad], axis=0).T
        highs[:, pl.ds(rel * part, part)] = source[pl.ds(ids_at + ID_ROWS, ID_ROWS), :].astype(F32)
    last_row = lax.broadcasted_iota(jnp.int32, (slab, group), 0) == emb
    first_high = (core * half).astype(F32)
    low_iota = lax.broadcasted_iota(jnp.int32, (group, LOW_ROWS), 1).astype(F32)
    for mine in range(CHIPS):

        @pl.when(chip == mine)
        def _(mine=mine):
            first_field = (mine * wide) // emb
            for field in range(first_field, min(fields, (mine * wide + wide - 1) // emb + 1)):
                begin = field * emb - mine * wide + MARGIN
                values = jnp.where(last_row, 1.0, spread[pl.ds(begin, slab), :])
                high_id = highs[pl.ds(field, 1), :] - first_high
                hot = jnp.where(low_iota == columns[:, field : field + 1], 1.0, 0.0).astype(BF16)
                stacked = jnp.concatenate(
                    [
                        jnp.where(high_id == block * 2 * half + piece, values, 0.0)
                        for block in range(ways)
                        for piece in range(half)
                    ],
                    axis=0,
                ).astype(BF16)
                got = dot(stacked, hot)
                for high in range(ways * half):
                    table[high, pl.ds(begin, emb), :] = got[high * slab : high * slab + emb]
                    counts[high, pl.ds(field - first_field, 1), :] = got[high * slab + emb : (high + 1) * slab]

    rows = []
    for begin in range(wide, ids_at, 16):
        rows.append(sum(one[step, pl.ds(begin, 16), :].astype(F32) for one in (sent, theirs) for step in range(CHIPS)))
    packed = pack_small(unpack_small(rows), LOW_ROWS)
    counts_at = half * wide + 16 * len(packed)
    for block in range(ways):
        for piece in range(half):
            values = table[block * half + piece, pl.ds(MARGIN, wide), :]
            out[block, pl.ds(piece * wide, wide), :] = values.astype(BF16)
            out[block, pl.ds(counts_at + 16 * piece, 16), :] = count_rows(counts[block * half + piece], 64.0).astype(BF16)
        for index, rows in enumerate(packed):
            out[block, pl.ds(half * wide + 16 * index, 16), :] = rows


def first_add_kernel(keep_one, got_one, keep_two, got_two, *refs):
    send_one, send_two = refs[-2:]
    send_one[...] = (keep_one[1].astype(F32) + got_one[1].astype(F32)).astype(BF16)
    send_two[...] = (keep_two[1].astype(F32) + got_two[1].astype(F32)).astype(BF16)


def second_add_kernel(at, keep_one, got_one, last_one, keep_two, got_two, last_two, *refs, by_step):
    out = refs[-1]
    half = last_one.shape[0]
    flip = at[0] if by_step else 0
    for first, keep, got, last in ((0, keep_one, got_one, last_one), (half, keep_two, got_two, last_two)):
        for block in range(half):
            total = keep[0, block].astype(F32) + got[0, block].astype(F32) + last[block].astype(F32)
            out[(first + block) ^ flip] = total.astype(BF16)


def add_kernel(*refs, count):
    total = refs[0][...].astype(F32)
    for other in refs[1:count]:
        total = total + other[...].astype(F32)
    refs[-1][...] = total.astype(refs[-1].dtype)


def fold_kernel(parts, *refs):
    total = parts[0].astype(F32)
    for block in range(1, parts.shape[0]):
        total = total + parts[block].astype(F32)
    refs[-1][...] = total.astype(refs[-1].dtype)


def table_fold_kernel(parts, *refs, half):
    out, small = refs[-2:]
    total = parts[0].astype(F32)
    for block in range(1, parts.shape[0]):
        total = total + parts[block].astype(F32)
    table_rows = out.shape[0] - 16 * half
    counts_at = total.shape[0] - 16 * half
    out[pl.ds(0, table_rows), :] = total[:table_rows].astype(BF16)
    small[...] = unpack_small([total[begin : begin + 16] for begin in range(table_rows, counts_at, 16)])
    for piece in range(half):
        rows = total[counts_at + 16 * piece : counts_at + 16 * (piece + 1)]
        out[pl.ds(table_rows + 16 * piece, 16), :] = count_rows(64.0 * rows[:8] + rows[8:], 256.0).astype(BF16)


def table_kernel(at, *refs, emb):
    pieces, (out, counts) = refs[: 2 * CHIPS], refs[-2:]
    wide, low = 2 * LANES, LOW_ROWS
    half = pieces[0].shape[0] // wide
    fields = counts.shape[0]
    last = CHIPS - 1
    for rel, piece in enumerate(pieces):
        chip = at[1] ^ (rel // 2)
        core = at[2] ^ (rel % 2)
        for block in range(half):
            lanes = pl.ds(pl.multiple_of((core * half + block) * low, low), low)
            values = piece[pl.ds(block * wide, wide), :].astype(F32)
            numbers = piece[pl.ds(half * wide + 16 * block, 16), :].astype(F32)
            numbers = (256.0 * numbers[:8] + numbers[8:]).astype(jnp.int32)
            for mine in range(CHIPS):

                @pl.when(chip == mine)
                def _(mine=mine, lanes=lanes, values=values, numbers=numbers):
                    height = wide if mine < last else out.shape[0] - last * wide
                    out[pl.ds(mine * wide, height), lanes] = values[:height]
                    first_field = (mine * wide) // emb
                    count = min(fields, (mine * wide + wide - 1) // emb + 1) - first_field
                    counts[pl.ds(first_field, count), lanes] = numbers[:count]


def tower_kernel(at, *refs):
    pieces, (one_out, two_out) = refs[: 2 * CHIPS], refs[-2:]
    ways = pieces[0].shape[0]
    hidden = two_out.shape[0]
    part = hidden // ways
    ends = (one_out.shape[0] - hidden) // ways
    for rel, piece in enumerate(pieces):
        lanes = pl.ds(column_of(at, rel), LANES)
        for block in range(ways):
            source = block ^ at[0]
            one_out[pl.ds(block * part, part), lanes] = piece[source, pl.ds(0, part), :].astype(F32)
            two_out[pl.ds(block * part, part), lanes] = piece[source, pl.ds(part, part), :].astype(F32)
            rest = piece[source, pl.ds(2 * part, 16), :].astype(F32)
            one_out[pl.ds(hidden + block * ends, ends), lanes] = rest[:ends]


def cross_kernel(at, *refs, gap):
    pieces, out, pack = refs[: 2 * CHIPS], refs[-2], refs[-1]
    layers, shard, full = out.shape
    main = pack.shape[1]
    extra = full - main
    for rel, piece in enumerate(pieces):
        lanes = pl.ds(column_of(at, rel), LANES)
        for layer in range(layers):
            out[layer, :, lanes] = piece[pl.ds(layer * gap, gap), :].astype(F32)[:shard]
        pack[pl.ds(0, extra), lanes] = piece[pl.ds(layers * gap, extra), :].astype(F32)
    pack[pl.ds(extra, pack.shape[0] - extra), :] = jnp.zeros((pack.shape[0] - extra, main), F32)
    turned = pack[...].T
    for layer in range(layers):
        out[layer, :, pl.ds(main, extra)] = turned[layer * shard : (layer + 1) * shard, :extra]


def in_hbm(value):
    return pltpu.with_memory_space_constraint(value, pltpu.HBM)


def vmem_bytes(one):
    *lead, rows, lanes = one.shape
    size = jnp.dtype(one.dtype).itemsize
    return math.prod(lead) * round_up(rows, 32 // size) * round_up(lanes, LANES) * size


def local(kernel, out_shape, operands, after=(), scratch=(), in_place=(), name=None, **options):
    operands = list(operands)
    smem = [index for index, one in enumerate(operands) if one.shape == (3,)]
    specs = [
        IN_SMEM if index in smem else IN_PLACE if index in in_place else IN_VMEM for index in range(len(operands))
    ]
    outs = out_shape if isinstance(out_shape, list) else [out_shape]
    held = [one for index, one in enumerate(operands) if index not in (*smem, *in_place)] + outs
    held += [one for one in scratch if len(one.shape) > 1]
    space = sum(vmem_bytes(one) for one in held) + SPARE_BYTES[name]
    got = pl.pallas_call(
        functools.partial(kernel, **options),
        out_shape=outs,
        in_specs=specs + [IN_PLACE] * len(after),
        out_specs=[IN_VMEM] * len(outs),
        scratch_shapes=list(scratch),
        compiler_params=pltpu.CompilerParams(vmem_limit_bytes=space),
        cost_estimate=pl.CostEstimate(flops=int(COST * MICROS[name]), bytes_accessed=0, transcendentals=0),
        name=name,
    )(*operands, *after)
    return got if isinstance(out_shape, list) else got[0]


class Links:
    def __init__(self, dp_size, cross_size):
        bits = dp_size.bit_length() - 1
        axis_bits = (bits - 1) // 2
        self.dp_size, self.cross_size = dp_size, cross_size
        self.core = 1
        self.chip_masks = (1 << 1, 1 << (1 + axis_bits))
        used = (self.core, *self.chip_masks)
        self.others = tuple(1 << bit for bit in range(bits) if 1 << bit not in used)

    def chip_mask(self, step):
        return sum(mask for bit, mask in enumerate(self.chip_masks) if step >> bit & 1)

    def chip(self, dp_place):
        return sum((dp_place // mask % 2) << bit for bit, mask in enumerate(self.chip_masks))

    def over_dp(self, value, mask):
        return lax.ppermute(value, "dp", [(one, one ^ mask) for one in range(self.dp_size)])

    def over_cross(self, value, mask):
        return lax.ppermute(value, "cross", [(one, one ^ mask) for one in range(self.cross_size)])

    def chips_swap(self, value_of):
        return [self.over_dp(value_of(step), self.chip_mask(step)) for step in range(1, CHIPS)]

    def cross_swap(self, value_of):
        return [self.over_cross(value_of(step), step) for step in range(1, self.cross_size)]

    def cross_exchange(self, value):
        return lax.all_to_all(value, "cross", split_axis=0, concat_axis=0, tiled=True)

    def add_others(self, value):
        for mask in self.others:
            value = (value.astype(F32) + self.over_dp(value, mask).astype(F32)).astype(BF16)
        return value

    def over_others(self, value):
        for mask in self.others:
            value = value + self.over_dp(value, mask)
        return value


    def plane_first(self, parts, after, name):
        keep_one, send_one, keep_two, send_two = parts
        one, two = self.chip_masks
        got_one, got_two = self.over_dp(send_one, one), self.over_dp(send_two, two)
        part = Shape(send_one.shape[1:], BF16)
        next_one, next_two = local(first_add_kernel, [part, part], [keep_one, got_one, keep_two, got_two], after, name=name)
        return keep_one, got_one, next_one, keep_two, got_two, next_two

    def plane_second(self, parts, at, by_step, after, name):
        keep_one, got_one, next_one, keep_two, got_two, next_two = parts
        one, two = self.chip_masks
        last_one, last_two = self.over_dp(next_one, two), self.over_dp(next_two, one)
        total = local(
            second_add_kernel,
            Shape((2 * next_one.shape[0], *next_one.shape[1:]), BF16),
            [at, keep_one, got_one, last_one, keep_two, got_two, last_two],
            after,
            name=name,
            by_step=by_step,
        )
        return self.add_others(total)

    def both_cores(self, arrays):
        return [each for one in arrays for each in (one, self.over_dp(one, self.core))]

    def plane_gather(self, value):
        return self.both_cores([value, *self.chips_swap(lambda step: value)])


def body(
    emb_table,
    dense_input,
    feature_ids,
    labels,
    cross_weight,
    cross_bias,
    tower_one,
    bias_one,
    tower_two,
    bias_two,
    out_weight,
    out_bias,
):
    layers, shard, full = cross_weight.shape
    group, fields = feature_ids.shape
    rows_here, emb_end = emb_table.shape
    emb = emb_end // fields
    dense_width = dense_input.shape[1]
    hidden = tower_one.shape[1]
    main = hidden
    extra = full - main
    ways = lax.axis_size("cross")
    place = lax.axis_index("cross")
    dp_place = lax.axis_index("dp")
    links = Links(lax.axis_size("dp"), ways)
    rows = group // ways
    scale = 1.0 / (group * links.dp_size)
    chip, core = links.chip(dp_place), dp_place % 2
    at = jnp.stack([place, chip, core]).astype(jnp.int32)
    wide = 2 * LANES
    gap = round_up(shard + 8, 16)

    blocks = -(-shard // LANES)
    ends = jnp.pad(cross_weight[:, :, main:].transpose(0, 2, 1), ((0, 0), (0, 0), (0, blocks * LANES - shard)))
    ends = ends.reshape(layers, extra, blocks, LANES).transpose(0, 2, 1, 3).reshape(layers, blocks * extra, LANES)
    ends_bias = jnp.pad(cross_bias, ((0, 0), (0, blocks * LANES - shard))).reshape(layers, blocks, LANES)
    own_tail = jnp.concatenate([ends, ends_bias], axis=1)
    own_tail = jnp.pad(own_tail, ((0, 0), (0, 64 - own_tail.shape[1]), (0, 0)))
    part = chip * 2 + core
    own_block = jnp.concatenate(
        [
            lax.dynamic_slice_in_dim(cross_weight, part * LANES, LANES, 2),
            jnp.zeros((layers, gap - 8 - shard, LANES), BF16),
            lax.dynamic_slice_in_dim(own_tail, part * 8, 8, 1),
        ],
        axis=1,
    )
    foreign = links.cross_swap(lambda step: own_block)

    ids_t = feature_ids.T
    emb_rows = round_up(emb_end + 1, 8)
    looked = local(
        lookup_kernel,
        Shape((ways, emb_rows, rows), BF16),
        [at, emb_table.T, ids_t],
        scratch=[pltpu.VMEM((emb_rows, rows_here), F32), pltpu.VMEM((emb_rows, group), F32)],
        name="lookup",
        fields=fields,
        emb=emb,
    )
    *foreign, looked = lax.optimization_barrier((*foreign, looked))
    parts = links.cross_exchange(looked)
    own_ids = lax.dynamic_slice_in_dim(ids_t, place * rows, rows, 1)
    foreign = jnp.stack(foreign)
    foreign = [foreign, *links.chips_swap(lambda step: foreign)]
    pieces = [in_hbm(one) for one in links.both_cores(foreign)]

    own_dense = lax.dynamic_slice_in_dim(dense_input.T, place * rows, rows, 1)
    dense_t = jnp.pad(own_dense.astype(F32), ((0, round_up(dense_width, 8) - dense_width), (0, 0)))
    own_full = jnp.pad(cross_weight[:, :, :main], ((0, 0), (0, gap - shard), (0, 0)))
    turned_rows = round_up(full, LANES)
    emb_shape = Shape((wide + 16 * -(-turned_rows // rows) + 2 * ID_ROWS, rows), BF16)
    tower_factors = round_up(full + hidden, 16)
    cross_factors = layers * (ways * gap + extra)
    logits, dense_grad, *emb_send, tower_other, tower_mine, cross_other, cross_mine = local(
        step_kernel,
        [
            Shape((1, rows), F32),
            Shape((dense_width, rows), F32),
            *[emb_shape] * CHIPS,
            Shape((tower_factors + 2 * CHIPS * LANES, rows), BF16),
            Shape((2 * CHIPS * LANES, rows), BF16),
            Shape((cross_factors + layers * CHIPS * LANES, rows), BF16),
            Shape((layers * CHIPS * LANES, rows), BF16),
        ],
        [
            at,
            parts,
            dense_t,
            in_hbm(own_full),
            own_tail,
            *pieces,
            in_hbm(tower_one),
            bias_one[None, :],
            in_hbm(tower_two),
            bias_two[None, :],
            out_weight[None, :],
            out_bias[None, :],
            labels[None, :],
            own_ids,
        ],
        [],
        [
            pltpu.VMEM((ways, layers, gap, main), BF16),
            pltpu.VMEM((full, hidden), BF16),
            pltpu.VMEM((hidden, hidden), BF16),
            pltpu.VMEM((ways, layers, 64, LANES), F32),
            pltpu.VMEM((8, turned_rows), F32),
            pltpu.VMEM((8, turned_rows), F32),
            pltpu.VMEM((turned_rows, rows), F32),
            pltpu.VMEM((rows, full), F32),
            pltpu.VMEM((rows, full), F32),
            pltpu.VMEM((layers, rows, full), BF16),
            pltpu.VMEM((layers, rows, full), F32),
            pltpu.VMEM((rows, round_up(ways * gap, LANES)), F32),
            pltpu.VMEM((layers, extra, round_up(ways * gap, LANES)), F32),
            pltpu.SemaphoreType.DMA((layers * (1 + 2 * CHIPS * (ways - 1)) + 2,)),
        ],
        in_place=(3, *range(5, 6 + 2 * CHIPS), 7 + 2 * CHIPS),
        name="step",
        shard=shard,
        emb_end=emb_end,
        scale=scale,
    )

    tower_theirs = links.over_dp(tower_other, links.core)
    cross_theirs = links.over_dp(cross_other, links.core)
    emb_got = links.chips_swap(lambda step: emb_send[step])

    tower_rows = round_up(2 * (hidden // ways) + extra // ways, 16)
    tower_shape = (ways, tower_rows, LANES)
    split = lambda shape: Shape((2, shape[0] // 2, *shape[1:]), BF16)
    tower_parts = local(
        tower_product_kernel,
        [split(tower_shape)] * 4,
        [at, tower_other, tower_mine, tower_theirs],
        name="tower_products",
        full=full,
        hidden=hidden,
    )


    cross_rows = layers * gap + extra
    cross_shape = (ways, cross_rows, LANES)
    cross_parts = local(
        cross_product_kernel,
        [split(cross_shape)] * 4,
        [at, cross_other, cross_mine, cross_theirs],
        [tower_parts[0]],
        [pltpu.VMEM((ways, extra, main), F32)],
        name="cross_products",
        layers=layers,
        shard=shard,
        gap=gap,
    )
    tower_first = links.plane_first(tower_parts, [cross_parts[0]], "tower_first")

    *emb_got, _ = lax.optimization_barrier((*emb_got, cross_parts[0]))
    emb_parts = jnp.stack([emb_send[0], *emb_got])
    emb_theirs = links.over_dp(emb_parts, links.core)
    half = rows_here // LOW_ROWS // 2
    table_ends = 16 * -(-turned_rows // LOW_ROWS)
    table_parts = local(
        scatter_kernel,
        Shape((ways, half * wide + table_ends + 16 * half, LOW_ROWS), BF16),
        [at, emb_parts, emb_theirs],
        [tower_first[2]],
        [
            pltpu.VMEM((MARGIN + wide + 64, rows * 2 * CHIPS), F32),
            pltpu.VMEM((ways * half, MARGIN + wide + 64, LOW_ROWS), F32),
            pltpu.VMEM((rows * 2 * CHIPS, LANES), F32),
            pltpu.VMEM((ID_ROWS, rows * 2 * CHIPS), F32),
            pltpu.VMEM((ways * half, 8, LOW_ROWS), F32),
        ],
        name="scatter",
        emb=emb,
        half=half,
        fields=fields,
    )
    table_parts = links.add_others(table_parts)
    table_got = links.cross_exchange(table_parts)
    tower_sum = links.plane_second(tower_first, at, True, [table_parts], "tower_second")
    tower_got = links.cross_swap(lambda step: tower_sum[step])
    tower_fold = local(
        add_kernel, Shape(tower_shape[1:], BF16), [tower_sum[0], *tower_got], name="tower_fold", count=ways
    )
    keep_one, send_one, keep_two, send_two = cross_parts
    send_one, send_two, _ = lax.optimization_barrier((send_one, send_two, tower_first[2]))
    cross_first = links.plane_first((keep_one, send_one, keep_two, send_two), [tower_fold], "cross_first")
    cross_sum = links.plane_second(cross_first, at, False, [], "cross_second")
    table_fold, small = local(
        table_fold_kernel,
        [Shape((half * (wide + 16), LOW_ROWS), BF16), Shape((8, round_up(turned_rows, LOW_ROWS)), F32)],
        [table_got],
        [cross_sum],
        name="table_fold",
        half=half,
    )
    table_all = links.chips_swap(lambda step: table_fold)
    tower_all = jnp.stack([tower_fold, *links.cross_swap(lambda step: tower_fold)])
    cross_got = links.cross_exchange(cross_sum)
    *table_all, _ = lax.optimization_barrier((*table_all, cross_sum))
    table_all = links.both_cores([table_fold, *table_all])
    tower_blocks = links.chips_swap(lambda step: tower_all)
    table_grad, row_counts = local(
        table_kernel,
        [Shape((emb_end, rows_here), F32), Shape((fields, rows_here), jnp.int32)],
        [at, *table_all],
        [cross_sum],
        name="table",
        emb=emb,
    )
    cross_fold = local(fold_kernel, Shape(cross_shape[1:], BF16), [cross_got], [table_grad], name="cross_fold")
    *tower_blocks, _ = lax.optimization_barrier((*tower_blocks, cross_fold))
    tower_blocks = links.both_cores([tower_all, *tower_blocks])
    tower_one_grad, tower_two_grad = local(
        tower_kernel, [Shape((full, hidden), F32), Shape((hidden, hidden), F32)], [at, *tower_blocks], name="towers"
    )
    cross_weight_grad = local(
        cross_kernel,
        Shape((layers, shard, full), F32),
        [at, *links.plane_gather(cross_fold)],
        scratch=[pltpu.VMEM((LANES, main), F32)],
        name="cross",
        gap=gap,
    )
    cross_bias_grad = lax.dynamic_slice_in_dim(small[4 : 4 + layers], place * shard, shard, 1)
    return (
        small[7, 0],
        logits[0],
        dense_grad.T,
        table_grad.T,
        cross_weight_grad,
        cross_bias_grad,
        tower_one_grad,
        small[0, :hidden],
        tower_two_grad,
        small[1, :hidden],
        jnp.concatenate([small[2, :full], small[3, :hidden]]),
        small[7, 1:2],
        row_counts.T,
    )


def solution(mesh):
    in_specs = (
        P("cross", None),
        P("dp", None),
        P("dp", None),
        P(("dp", "cross")),
        P(None, "cross", None),
        P(None, "cross"),
        P(),
        P(),
        P(),
        P(),
        P(),
        P(),
    )
    out_specs = (
        P(),
        P(("dp", "cross")),
        P(("dp", "cross"), None),
        P("cross", None),
        P(None, "cross", None),
        P(None, "cross"),
        P(),
        P(),
        P(),
        P(),
        P(),
        P(),
        P("cross", None),
    )
    return jax.shard_map(body, mesh=mesh, in_specs=in_specs, out_specs=out_specs, check_vma=False)
```

```python
import collections
import functools
import math

import jax
import jax.numpy as jnp
from jax import lax
from jax.experimental import pallas as pl
from jax.experimental.pallas import tpu as pltpu
from jax.sharding import PartitionSpec as P

F32 = jnp.float32
BF16 = jnp.bfloat16
ROWS_IN_ROWS = (((0,), (0,)), ((), ()))
LANES_IN_LANES = (((1,), (1,)), ((), ()))
LANES = 128
LOW_BITS = 8
LOW_ROWS = 1 << LOW_BITS
CHIPS = 4
MARGIN = 48
ID_ROWS = 32
STEP_SPARE = 8 << 20
SPARE_BYTES = collections.defaultdict(lambda: 3 << 20, step=STEP_SPARE)
COST = 5.175e+09
MICROS = dict(
    lookup=7.4,
    count=5.2,
    step=23,
    tower_products=5.9,
    scatter=7,
    cross_products=8.9,
    tower_first=3.1,
    tower_second=2.3,
    table_fold=2,
    tower_fold=1.8,
    cross_first=4,
    cross_second=2.7,
    cross_fold=1.9,
    table=3.9,
    towers=6.8,
    cross=3.6,
)
IN_VMEM = pl.BlockSpec(memory_space=pltpu.VMEM)
IN_SMEM = pl.BlockSpec(memory_space=pltpu.SMEM)
IN_PLACE = pl.BlockSpec(memory_space=pl.ANY)
Shape = jax.ShapeDtypeStruct


def round_up(size, step):
    return -(-size // step) * step


def dot(left, right, dims=(((1,), (0,)), ((), ()))):
    return lax.dot_general(left, right, dims, preferred_element_type=F32)


def silu_slope(pre_act):
    sigmoid_part = jax.nn.sigmoid(pre_act)
    return sigmoid_part * (1.0 + pre_act * (1.0 - sigmoid_part))


def lookup_kernel(at, table, ids, out, floats, gathered, *, fields, emb):
    ways = out.shape[0]
    highs = table.shape[1] // LOW_ROWS
    group = ids.shape[1]
    part = group // ways
    slab = emb + 1
    floats[pl.ds(0, table.shape[0]), :] = table[...].astype(F32)
    low_iota = lax.broadcasted_iota(jnp.int32, (LOW_ROWS, group), 0)
    for field in range(fields):
        left = jnp.concatenate(
            [floats[pl.ds(field * emb, slab), pl.ds(high * LOW_ROWS, LOW_ROWS)] for high in range(highs)], axis=0
        ).astype(BF16)
        local = ids[pl.ds(field, 1), :] - at[0] * (highs * LOW_ROWS)
        low = jnp.bitwise_and(local, LOW_ROWS - 1)
        high_id = jnp.right_shift(local, LOW_BITS)
        hot = jnp.where(low_iota == low, 1.0, 0.0).astype(BF16)
        picked = dot(left, hot)
        total = jnp.zeros((slab, group), F32)
        for high in range(highs):
            total = total + jnp.where(high_id == high, picked[high * slab : (high + 1) * slab], 0.0)
        gathered[pl.ds(field * emb, slab), :] = total
    for block in range(ways):
        out[block] = gathered[:, pl.ds(block * part, part)].astype(BF16)


def column_of(at, rel):
    return pl.multiple_of(((at[1] ^ (rel // 2)) * 2 + (at[2] ^ (rel % 2))) * LANES, LANES)


def column_pick(at, values, mine):
    first = at[2] == 0 if mine else at[2] == 1
    blocks = []
    for one in range(CHIPS):
        low, high = values[:, 2 * one * LANES : (2 * one + 1) * LANES], values[:, (2 * one + 1) * LANES : (2 * one + 2) * LANES]
        blocks.append(jnp.where(first, low, high))
    picked = jnp.concatenate(blocks, axis=1).astype(BF16)
    rows = values.shape[0]
    return [picked[:, begin : begin + rows] for begin in range(0, CHIPS * LANES, rows)]


def step_kernel(at, *refs, shard, emb_end, scale):
    refs = list(refs)
    take = lambda count: [refs.pop(0) for _ in range(count)]
    (parts, dense_t, own, own_tail), pieces = take(4), take(2 * CHIPS)
    one_at, one_b, two_at, two_b, out_w, out_b, labels, ids = take(8)
    (logits_out, dense_grad), emb_send = take(2), take(CHIPS)
    tower_other, tower_mine, cross_other, cross_mine = take(4)
    weights, one_w, two_w, tails, bias, small, turned, first, state, lows, mixes, spread, edges, sems = take(14)
    place = at[0]
    ways, layers, gap, main = weights.shape
    rows = parts.shape[2]
    full = first.shape[1]
    extra = full - main
    hidden = one_w.shape[1]
    blocks = -(-shard // LANES)
    copies, count = [], 1 + len(pieces) * (ways - 1)
    for layer in range(layers):
        sem = iter(sems.at[layer * count + index] for index in range(count))
        copies.append([pltpu.make_async_copy(own.at[layer], weights.at[place, layer], next(sem))])
        for rel, piece in enumerate(pieces):
            for step in range(1, ways):
                target = weights.at[place ^ step, layer, :, pl.ds(column_of(at, rel), LANES)]
                copies[layer].append(pltpu.make_async_copy(piece.at[step - 1, layer], target, next(sem)))
    towers = [
        pltpu.make_async_copy(one_at, one_w, sems.at[layers * count]),
        pltpu.make_async_copy(two_at, two_w, sems.at[layers * count + 1]),
    ]
    for copy in sum(copies, []) + towers:
        copy.start()
    tails[place] = own_tail[...].astype(F32)
    spread[...] = jnp.zeros_like(spread)
    edges[...] = jnp.zeros_like(edges)
    wide_rows = ways * gap
    looked = parts[0].astype(F32)
    for block in range(1, ways):
        looked = looked + parts[block].astype(F32)
    turned[pl.ds(0, looked.shape[0]), :] = looked
    turned[pl.ds(emb_end, dense_t.shape[0]), :] = dense_t[...]
    used = emb_end + dense_t.shape[0]
    turned[pl.ds(used, turned.shape[0] - used), :] = jnp.zeros((turned.shape[0] - used, rows), F32)
    start = turned[...].T[:, :full]
    first[...] = start
    state[...] = start
    for layer in range(layers):
        for copy in copies[layer]:
            copy.wait()
        for block in range(ways):
            ends = weights[block, layer, pl.ds(gap - 16, 16), :].astype(F32)[8:]

            @pl.when(place != block)
            def _(block=block, layer=layer, ends=ends):
                for one in range(2 * CHIPS):
                    tails[block, layer, pl.ds(8 * one, 8), :] = ends[:, one * LANES : (one + 1) * LANES]

            row = [tails[block, layer, pl.ds(one * (extra + 1) + extra, 1), :] for one in range(blocks)]
            bias[pl.ds(layer, 1), pl.ds(block * shard, shard)] = jnp.concatenate(row, axis=1)[:, :shard]
            edge = [tails[block, layer, pl.ds(one * (extra + 1), extra), :] for one in range(blocks)]
            edges[layer, :, pl.ds(block * gap, shard)] = jnp.concatenate(edge, axis=1)[:, :shard]
        lows[layer] = state[...].astype(BF16)
        for block in range(ways):
            spread[:, pl.ds(block * gap, shard)] = state[:, pl.ds(block * shard, shard)]
        low = spread[:, pl.ds(0, wide_rows)].astype(BF16)
        body = dot(low, weights[:, layer].reshape(wide_rows, main))
        edge = dot(low, edges[layer, :, pl.ds(0, wide_rows)].astype(BF16), LANES_IN_LANES)
        mixed = jnp.concatenate([body, edge], axis=1) + bias[pl.ds(layer, 1), :full]
        mixes[layer] = mixed
        state[...] = first[...] * mixed + state[...]

    for copy in towers:
        copy.wait()
    top = state[...].astype(BF16)
    hid_one = dot(top, one_w[...]) + one_b[...]
    act_one = jax.nn.silu(hid_one).astype(BF16)
    hid_two = dot(act_one, two_w[...]) + two_b[...]
    act_two = jax.nn.silu(hid_two).astype(BF16)
    top_float, act_float = top.astype(F32), act_two.astype(F32)
    weight_top = out_w[:, :full].astype(F32)
    weight_act = out_w[:, full:].astype(F32)
    logits = (
        jnp.sum(top_float * weight_top, axis=1, keepdims=True)
        + jnp.sum(act_float * weight_act, axis=1, keepdims=True)
        + out_b[...]
    )
    logits_out[...] = jnp.broadcast_to(logits, (rows, LANES)).T[:1]
    label = jnp.broadcast_to(labels[...].astype(F32), (LANES, rows)).T[:, :1]
    loss = jnp.sum(jax.nn.softplus(logits) - label * logits, axis=0, keepdims=True) * scale
    g_logit = ((jax.nn.sigmoid(logits) - label) * scale).astype(BF16).astype(F32)
    g_two = (g_logit * weight_act * silu_slope(hid_two)).astype(BF16)
    g_one = (dot(g_two, two_w[...], LANES_IN_LANES) * silu_slope(hid_one)).astype(BF16)
    grad = (dot(g_one, one_w[...], LANES_IN_LANES) + g_logit * weight_top).astype(BF16).astype(F32)
    one_float, two_float = g_one.astype(F32), g_two.astype(F32)
    lane = lax.broadcasted_iota(jnp.int32, (1, LANES), 1)
    bias_grad = jnp.sum(g_logit, axis=0, keepdims=True)
    small[...] = jnp.zeros_like(small)
    small[pl.ds(0, 1), pl.ds(0, hidden)] = jnp.sum(one_float, axis=0, keepdims=True)
    small[pl.ds(1, 1), pl.ds(0, hidden)] = jnp.sum(two_float, axis=0, keepdims=True)
    small[pl.ds(2, 1), pl.ds(0, full)] = jnp.sum(top_float * g_logit, axis=0, keepdims=True)
    small[pl.ds(3, 1), pl.ds(0, hidden)] = jnp.sum(act_float * g_logit, axis=0, keepdims=True)
    small[pl.ds(7, 1), pl.ds(0, LANES)] = jnp.where(lane == 0, loss, jnp.where(lane == 1, bias_grad, 0.0))
    tower_other[pl.ds(0, full), :] = top_float.T.astype(BF16)
    tower_other[pl.ds(full, hidden), :] = act_one.astype(F32).T.astype(BF16)
    base = round_up(full + hidden, 16)
    span = CHIPS * LANES
    for which, values in enumerate((one_float, two_float)):
        for index, block in enumerate(column_pick(at, values, False)):
            tower_other[pl.ds(base + which * span + index * rows, rows), :] = block
        for index, block in enumerate(column_pick(at, values, True)):
            tower_mine[pl.ds(which * span + index * rows, rows), :] = block

    inputs = first[...]
    pad = jnp.zeros((rows, turned.shape[0] - full), F32)
    total = jnp.zeros_like(grad)
    low_rows = layers * ways * gap
    base = low_rows + layers * extra
    for layer in reversed(range(layers)):
        rounded = (grad * inputs).astype(BF16)
        values = rounded.astype(F32)
        small[pl.ds(4 + layer, 1), pl.ds(0, full)] = jnp.sum(values, axis=0, keepdims=True)
        total = total + grad * mixes[layer]
        spread[:, pl.ds(0, wide_rows)] = dot(
            rounded[:, :main], weights[:, layer].reshape(wide_rows, main), LANES_IN_LANES
        ) + dot(rounded[:, main:full], edges[layer, :, pl.ds(0, wide_rows)].astype(BF16))
        backs = [spread[:, pl.ds(block * gap, shard)] for block in range(ways)]
        grad = grad + jnp.concatenate(backs, axis=1)
        for index, block in enumerate(column_pick(at, values, False)):
            cross_other[pl.ds(base + layer * span + index * rows, rows), :] = block
        for index, block in enumerate(column_pick(at, values, True)):
            cross_mine[pl.ds(layer * span + index * rows, rows), :] = block
        edge = jnp.concatenate([values[:, main:full], jnp.zeros((rows, LANES - extra), F32)], axis=1).T
        cross_other[pl.ds(low_rows + layer * extra, extra), :] = edge[:extra].astype(BF16)
        turned[...] = jnp.concatenate([lows[layer].astype(F32), pad], axis=1).T
        for block in range(ways):
            low_t = jnp.concatenate([turned[pl.ds(block * shard, shard), :], jnp.zeros((gap - shard, rows), F32)], axis=0)
            cross_other[pl.ds((layer * ways + block) * gap, gap), :] = low_t.astype(BF16)
    total = total + grad
    turned[...] = jnp.concatenate([total, pad], axis=1).T
    dense_grad[...] = turned[pl.ds(emb_end, dense_grad.shape[0]), :]
    wide = 2 * LANES
    packed = pack_small(small[...], rows)
    fields = ids.shape[0]
    blank = jnp.zeros((ID_ROWS - fields, rows), F32)
    low_ids = jnp.bitwise_and(ids[...], LOW_ROWS - 1).astype(F32)
    high_ids = jnp.right_shift(ids[...], LOW_BITS).astype(F32)
    id_rows = jnp.concatenate([low_ids, blank, high_ids, blank], axis=0).astype(BF16)
    ids_at = wide + 16 * len(packed)
    for step in range(CHIPS):
        emb_send[step][pl.ds(0, wide), :] = turned[pl.ds(pl.multiple_of((at[1] ^ step) * wide, wide), wide), :].astype(BF16)
        for index, block in enumerate(packed):
            emb_send[step][pl.ds(wide + 16 * index, 16), :] = block
        emb_send[step][pl.ds(ids_at, 2 * ID_ROWS), :] = id_rows


def both_cores(at, mine, theirs, start, which, step, rows):
    begin = (at[1] ^ step) * LANES
    lanes = pl.ds(pl.multiple_of(begin % rows, LANES), LANES)
    row = pl.multiple_of(which * CHIPS * LANES + begin // rows * rows, LANES)
    return jnp.concatenate([mine[pl.ds(row, rows), lanes], theirs[pl.ds(start + row, rows), lanes]], axis=0)


def halves(refs, ways):
    keep_one, send_one, keep_two, send_two = refs
    half = ways // 2

    def place_of(step, block):
        if block < half:
            return (send_one if step & 1 else keep_one), (step >> 1, block)
        return (send_two if step & 2 else keep_two), (step & 1, block - half)

    return place_of


def pack_small(values, lanes):
    if values.shape[1] % lanes:
        values = jnp.concatenate([values, jnp.zeros((8, -values.shape[1] % lanes), F32)], axis=1)
    packed = []
    for begin in range(0, values.shape[1], lanes):
        block = values[:, begin : begin + lanes]
        high = block.astype(BF16).astype(F32)
        packed.append(jnp.concatenate([high, block - high], axis=0).astype(BF16))
    return packed


def unpack_small(rows):
    return jnp.concatenate([one[:8] + one[8:] for one in rows], axis=1)


def tower_product_kernel(at, sent, mine, theirs, *refs, full, hidden):
    refs = refs[-CHIPS:]
    ways = 2 * refs[0].shape[1]
    place_of = halves(refs, ways)
    rows = mine.shape[1]
    part = hidden // ways
    ends = (full - hidden) // ways
    last = refs[0].shape[2] - 2 * part
    base = round_up(full + hidden, 16)
    top_t = jnp.concatenate([sent[pl.ds(0, full), :], theirs[pl.ds(0, full), :]], axis=1)
    act_t = jnp.concatenate([sent[pl.ds(full, hidden), :], theirs[pl.ds(full, hidden), :]], axis=1)
    for step in range(CHIPS):
        one = dot(top_t, both_cores(at, mine, theirs, base, 0, step, rows))
        two = dot(act_t, both_cores(at, mine, theirs, base, 1, step, rows))
        for block in range(ways):
            own_rows = slice(block * part, (block + 1) * part)
            out, where = place_of(step, block)
            out[*where, pl.ds(0, part), :] = one[own_rows].astype(out.dtype)
            out[*where, pl.ds(part, part), :] = two[own_rows].astype(out.dtype)
            rest = one[hidden + block * ends : hidden + (block + 1) * ends]
            rest = jnp.concatenate([rest, jnp.zeros((last - ends, LANES), F32)], axis=0)
            out[*where, pl.ds(2 * part, last), :] = rest.astype(out.dtype)


def cross_product_kernel(at, sent, mine, theirs, *refs, layers, shard, gap):
    pack = refs[-1]
    ways, extra = pack.shape[0], pack.shape[1]
    place_of = halves(refs[-CHIPS - 1 : -1], ways)
    rows = mine.shape[1]
    low_rows = layers * ways * gap
    base = low_rows + layers * extra
    pack[...] = jnp.zeros_like(pack)

    def lows(layer, block):
        own_rows = pl.ds((layer * ways + block) * gap, gap)
        return jnp.concatenate([sent[own_rows, :], theirs[own_rows, :]], axis=1)

    for layer in range(layers):
        own_rows = pl.ds(low_rows + layer * extra, extra)
        edge = jnp.concatenate([sent[own_rows, :], theirs[own_rows, :]], axis=1)
        for block in range(ways):
            product = dot(edge, lows(layer, block), LANES_IN_LANES)
            pack[block, :, pl.ds(layer * shard, shard)] = product[:, :shard]
    for step in range(CHIPS):
        for layer in range(layers):
            columns = both_cores(at, mine, theirs, base, layer, step, rows)
            for block in range(ways):
                out, where = place_of(step, block)
                out[*where, pl.ds(layer * gap, gap), :] = dot(lows(layer, block), columns).astype(out.dtype)
        for block in range(ways):
            out, where = place_of(step, block)
            lanes = pl.ds(column_of(at, 2 * step), LANES)
            out[*where, pl.ds(layers * gap, extra), :] = pack[block, :, lanes].astype(out.dtype)


def count_rows(counts, base):
    high = jnp.floor(counts * (1.0 / base))
    return jnp.concatenate([high, counts - base * high], axis=0)


def scatter_kernel(at, sent, theirs, *refs, emb, half, fields):
    out, spread, table, columns, highs, counts = refs[-6:]
    chip, core = at[1], at[2]
    part, wide = theirs.shape[2], 2 * LANES
    group = 2 * CHIPS * part
    ways = out.shape[0]
    ids_at = theirs.shape[1] - 2 * ID_ROWS
    slab = emb + 1
    spread[pl.ds(0, MARGIN), :] = jnp.zeros((MARGIN, group), F32)
    spread[pl.ds(MARGIN + wide, 64), :] = jnp.zeros((64, group), F32)
    counts[...] = jnp.zeros_like(counts)
    pad = jnp.zeros((LANES - ID_ROWS, part), F32)
    for rel in range(2 * CHIPS):
        source = (theirs if rel % 2 else sent).at[rel // 2]
        spread[pl.ds(MARGIN, wide), pl.ds(rel * part, part)] = source[pl.ds(0, wide), :].astype(F32)
        low = source[pl.ds(ids_at, ID_ROWS), :].astype(F32)
        columns[pl.ds(rel * part, part), :] = jnp.concatenate([low, pad], axis=0).T
        highs[:, pl.ds(rel * part, part)] = source[pl.ds(ids_at + ID_ROWS, ID_ROWS), :].astype(F32)
    last_row = lax.broadcasted_iota(jnp.int32, (slab, group), 0) == emb
    first_high = (core * half).astype(F32)
    low_iota = lax.broadcasted_iota(jnp.int32, (group, LOW_ROWS), 1).astype(F32)
    for mine in range(CHIPS):

        @pl.when(chip == mine)
        def _(mine=mine):
            first_field = (mine * wide) // emb
            for field in range(first_field, min(fields, (mine * wide + wide - 1) // emb + 1)):
                begin = field * emb - mine * wide + MARGIN
                values = jnp.where(last_row, 1.0, spread[pl.ds(begin, slab), :])
                high_id = highs[pl.ds(field, 1), :] - first_high
                hot = jnp.where(low_iota == columns[:, field : field + 1], 1.0, 0.0).astype(BF16)
                stacked = jnp.concatenate(
                    [
                        jnp.where(high_id == block * 2 * half + piece, values, 0.0)
                        for block in range(ways)
                        for piece in range(half)
                    ],
                    axis=0,
                ).astype(BF16)
                got = dot(stacked, hot)
                for high in range(ways * half):
                    table[high, pl.ds(begin, emb), :] = got[high * slab : high * slab + emb]
                    counts[high, pl.ds(field - first_field, 1), :] = got[high * slab + emb : (high + 1) * slab]

    rows = []
    for begin in range(wide, ids_at, 16):
        rows.append(sum(one[step, pl.ds(begin, 16), :].astype(F32) for one in (sent, theirs) for step in range(CHIPS)))
    packed = pack_small(unpack_small(rows), LOW_ROWS)
    counts_at = half * wide + 16 * len(packed)
    for block in range(ways):
        for piece in range(half):
            values = table[block * half + piece, pl.ds(MARGIN, wide), :]
            out[block, pl.ds(piece * wide, wide), :] = values.astype(BF16)
            out[block, pl.ds(counts_at + 16 * piece, 16), :] = count_rows(counts[block * half + piece], 64.0).astype(BF16)
        for index, rows in enumerate(packed):
            out[block, pl.ds(half * wide + 16 * index, 16), :] = rows


def first_add_kernel(keep_one, got_one, keep_two, got_two, *refs):
    send_one, send_two = refs[-2:]
    send_one[...] = (keep_one[1].astype(F32) + got_one[1].astype(F32)).astype(BF16)
    send_two[...] = (keep_two[1].astype(F32) + got_two[1].astype(F32)).astype(BF16)


def second_add_kernel(at, keep_one, got_one, last_one, keep_two, got_two, last_two, *refs, by_step):
    out = refs[-1]
    half = last_one.shape[0]
    flip = at[0] if by_step else 0
    for first, keep, got, last in ((0, keep_one, got_one, last_one), (half, keep_two, got_two, last_two)):
        for block in range(half):
            total = keep[0, block].astype(F32) + got[0, block].astype(F32) + last[block].astype(F32)
            out[(first + block) ^ flip] = total.astype(BF16)


def add_kernel(*refs, count):
    total = refs[0][...].astype(F32)
    for other in refs[1:count]:
        total = total + other[...].astype(F32)
    refs[-1][...] = total.astype(refs[-1].dtype)


def fold_kernel(parts, *refs):
    total = parts[0].astype(F32)
    for block in range(1, parts.shape[0]):
        total = total + parts[block].astype(F32)
    refs[-1][...] = total.astype(refs[-1].dtype)


def table_fold_kernel(parts, *refs, half):
    out, small = refs[-2:]
    total = parts[0].astype(F32)
    for block in range(1, parts.shape[0]):
        total = total + parts[block].astype(F32)
    table_rows = out.shape[0] - 16 * half
    counts_at = total.shape[0] - 16 * half
    out[pl.ds(0, table_rows), :] = total[:table_rows].astype(BF16)
    small[...] = unpack_small([total[begin : begin + 16] for begin in range(table_rows, counts_at, 16)])
    for piece in range(half):
        rows = total[counts_at + 16 * piece : counts_at + 16 * (piece + 1)]
        out[pl.ds(table_rows + 16 * piece, 16), :] = count_rows(64.0 * rows[:8] + rows[8:], 256.0).astype(BF16)


def table_kernel(at, *refs, emb):
    pieces, (out, counts) = refs[: 2 * CHIPS], refs[-2:]
    wide, low = 2 * LANES, LOW_ROWS
    half = pieces[0].shape[0] // wide
    fields = counts.shape[0]
    last = CHIPS - 1
    for rel, piece in enumerate(pieces):
        chip = at[1] ^ (rel // 2)
        core = at[2] ^ (rel % 2)
        for block in range(half):
            lanes = pl.ds(pl.multiple_of((core * half + block) * low, low), low)
            values = piece[pl.ds(block * wide, wide), :].astype(F32)
            numbers = piece[pl.ds(half * wide + 16 * block, 16), :].astype(F32)
            numbers = (256.0 * numbers[:8] + numbers[8:]).astype(jnp.int32)
            for mine in range(CHIPS):

                @pl.when(chip == mine)
                def _(mine=mine, lanes=lanes, values=values, numbers=numbers):
                    height = wide if mine < last else out.shape[0] - last * wide
                    out[pl.ds(mine * wide, height), lanes] = values[:height]
                    first_field = (mine * wide) // emb
                    count = min(fields, (mine * wide + wide - 1) // emb + 1) - first_field
                    counts[pl.ds(first_field, count), lanes] = numbers[:count]


def tower_kernel(at, *refs):
    pieces, (one_out, two_out) = refs[: 2 * CHIPS], refs[-2:]
    ways = pieces[0].shape[0]
    hidden = two_out.shape[0]
    part = hidden // ways
    ends = (one_out.shape[0] - hidden) // ways
    for rel, piece in enumerate(pieces):
        lanes = pl.ds(column_of(at, rel), LANES)
        for block in range(ways):
            source = block ^ at[0]
            one_out[pl.ds(block * part, part), lanes] = piece[source, pl.ds(0, part), :].astype(F32)
            two_out[pl.ds(block * part, part), lanes] = piece[source, pl.ds(part, part), :].astype(F32)
            rest = piece[source, pl.ds(2 * part, 16), :].astype(F32)
            one_out[pl.ds(hidden + block * ends, ends), lanes] = rest[:ends]


def cross_kernel(at, *refs, gap):
    pieces, out, pack = refs[: 2 * CHIPS], refs[-2], refs[-1]
    layers, shard, full = out.shape
    main = pack.shape[1]
    extra = full - main
    for rel, piece in enumerate(pieces):
        lanes = pl.ds(column_of(at, rel), LANES)
        for layer in range(layers):
            out[layer, :, lanes] = piece[pl.ds(layer * gap, gap), :].astype(F32)[:shard]
        pack[pl.ds(0, extra), lanes] = piece[pl.ds(layers * gap, extra), :].astype(F32)
    pack[pl.ds(extra, pack.shape[0] - extra), :] = jnp.zeros((pack.shape[0] - extra, main), F32)
    turned = pack[...].T
    for layer in range(layers):
        out[layer, :, pl.ds(main, extra)] = turned[layer * shard : (layer + 1) * shard, :extra]


def in_hbm(value):
    return pltpu.with_memory_space_constraint(value, pltpu.HBM)


def vmem_bytes(one):
    *lead, rows, lanes = one.shape
    size = jnp.dtype(one.dtype).itemsize
    return math.prod(lead) * round_up(rows, 32 // size) * round_up(lanes, LANES) * size


def local(kernel, out_shape, operands, after=(), scratch=(), in_place=(), name=None, **options):
    operands = list(operands)
    smem = [index for index, one in enumerate(operands) if one.shape == (3,)]
    specs = [
        IN_SMEM if index in smem else IN_PLACE if index in in_place else IN_VMEM for index in range(len(operands))
    ]
    outs = out_shape if isinstance(out_shape, list) else [out_shape]
    held = [one for index, one in enumerate(operands) if index not in (*smem, *in_place)] + outs
    held += [one for one in scratch if len(one.shape) > 1]
    space = sum(vmem_bytes(one) for one in held) + SPARE_BYTES[name]
    got = pl.pallas_call(
        functools.partial(kernel, **options),
        out_shape=outs,
        in_specs=specs + [IN_PLACE] * len(after),
        out_specs=[IN_VMEM] * len(outs),
        scratch_shapes=list(scratch),
        compiler_params=pltpu.CompilerParams(vmem_limit_bytes=space),
        cost_estimate=pl.CostEstimate(flops=int(COST * MICROS[name]), bytes_accessed=0, transcendentals=0),
        name=name,
    )(*operands, *after)
    return got if isinstance(out_shape, list) else got[0]


class Links:
    def __init__(self, dp_size, cross_size):
        bits = dp_size.bit_length() - 1
        axis_bits = (bits - 1) // 2
        self.dp_size, self.cross_size = dp_size, cross_size
        self.core = 1
        self.chip_masks = (1 << 1, 1 << (1 + axis_bits))
        used = (self.core, *self.chip_masks)
        self.others = tuple(1 << bit for bit in range(bits) if 1 << bit not in used)

    def chip_mask(self, step):
        return sum(mask for bit, mask in enumerate(self.chip_masks) if step >> bit & 1)

    def chip(self, dp_place):
        return sum((dp_place // mask % 2) << bit for bit, mask in enumerate(self.chip_masks))

    def over_dp(self, value, mask):
        return lax.ppermute(value, "dp", [(one, one ^ mask) for one in range(self.dp_size)])

    def over_cross(self, value, mask):
        return lax.ppermute(value, "cross", [(one, one ^ mask) for one in range(self.cross_size)])

    def chips_swap(self, value_of):
        return [self.over_dp(value_of(step), self.chip_mask(step)) for step in range(1, CHIPS)]

    def cross_swap(self, value_of):
        return [self.over_cross(value_of(step), step) for step in range(1, self.cross_size)]

    def cross_exchange(self, value):
        return lax.all_to_all(value, "cross", split_axis=0, concat_axis=0, tiled=True)

    def add_others(self, value):
        for mask in self.others:
            value = (value.astype(F32) + self.over_dp(value, mask).astype(F32)).astype(BF16)
        return value

    def over_others(self, value):
        for mask in self.others:
            value = value + self.over_dp(value, mask)
        return value


    def plane_first(self, parts, after, name):
        keep_one, send_one, keep_two, send_two = parts
        one, two = self.chip_masks
        got_one, got_two = self.over_dp(send_one, one), self.over_dp(send_two, two)
        part = Shape(send_one.shape[1:], BF16)
        next_one, next_two = local(first_add_kernel, [part, part], [keep_one, got_one, keep_two, got_two], after, name=name)
        return keep_one, got_one, next_one, keep_two, got_two, next_two

    def plane_second(self, parts, at, by_step, after, name):
        keep_one, got_one, next_one, keep_two, got_two, next_two = parts
        one, two = self.chip_masks
        last_one, last_two = self.over_dp(next_one, two), self.over_dp(next_two, one)
        total = local(
            second_add_kernel,
            Shape((2 * next_one.shape[0], *next_one.shape[1:]), BF16),
            [at, keep_one, got_one, last_one, keep_two, got_two, last_two],
            after,
            name=name,
            by_step=by_step,
        )
        return self.add_others(total)

    def both_cores(self, arrays):
        return [each for one in arrays for each in (one, self.over_dp(one, self.core))]

    def plane_gather(self, value):
        return self.both_cores([value, *self.chips_swap(lambda step: value)])


def body(
    emb_table,
    dense_input,
    feature_ids,
    labels,
    cross_weight,
    cross_bias,
    tower_one,
    bias_one,
    tower_two,
    bias_two,
    out_weight,
    out_bias,
):
    layers, shard, full = cross_weight.shape
    group, fields = feature_ids.shape
    rows_here, emb_end = emb_table.shape
    emb = emb_end // fields
    dense_width = dense_input.shape[1]
    hidden = tower_one.shape[1]
    main = hidden
    extra = full - main
    ways = lax.axis_size("cross")
    place = lax.axis_index("cross")
    dp_place = lax.axis_index("dp")
    links = Links(lax.axis_size("dp"), ways)
    rows = group // ways
    scale = 1.0 / (group * links.dp_size)
    chip, core = links.chip(dp_place), dp_place % 2
    at = jnp.stack([place, chip, core]).astype(jnp.int32)
    wide = 2 * LANES
    gap = round_up(shard + 8, 16)

    blocks = -(-shard // LANES)
    ends = jnp.concatenate([cross_weight[:, :, main:], cross_bias[:, :, None]], axis=2)
    ends = jnp.pad(ends, ((0, 0), (0, blocks * LANES - shard), (0, 0))).reshape(layers, blocks, LANES, extra + 1)
    own_tail = ends.transpose(0, 1, 3, 2).reshape(layers, blocks * (extra + 1), LANES)
    own_tail = jnp.pad(own_tail, ((0, 0), (0, 64 - own_tail.shape[1]), (0, 0)))
    part = chip * 2 + core
    own_block = jnp.concatenate(
        [
            lax.dynamic_slice_in_dim(cross_weight, part * LANES, LANES, 2),
            jnp.zeros((layers, gap - 8 - shard, LANES), BF16),
            lax.dynamic_slice_in_dim(own_tail, part * 8, 8, 1),
        ],
        axis=1,
    )
    foreign = links.cross_swap(lambda step: own_block)

    ids_t = feature_ids.T
    emb_rows = round_up(emb_end + 1, 8)
    looked = local(
        lookup_kernel,
        Shape((ways, emb_rows, rows), BF16),
        [at, emb_table.T, ids_t],
        scratch=[pltpu.VMEM((emb_rows, rows_here), F32), pltpu.VMEM((emb_rows, group), F32)],
        name="lookup",
        fields=fields,
        emb=emb,
    )
    *foreign, looked = lax.optimization_barrier((*foreign, looked))
    parts = links.cross_exchange(looked)
    own_ids = lax.dynamic_slice_in_dim(ids_t, place * rows, rows, 1)
    foreign = jnp.stack(foreign)
    foreign = [foreign, *links.chips_swap(lambda step: foreign)]
    pieces = [in_hbm(one) for one in links.both_cores(foreign)]

    own_dense = lax.dynamic_slice_in_dim(dense_input.T, place * rows, rows, 1)
    dense_t = jnp.pad(own_dense.astype(F32), ((0, round_up(dense_width, 8) - dense_width), (0, 0)))
    own_full = jnp.pad(cross_weight[:, :, :main], ((0, 0), (0, gap - shard), (0, 0)))
    turned_rows = round_up(full, LANES)
    emb_shape = Shape((wide + 16 * -(-turned_rows // rows) + 2 * ID_ROWS, rows), BF16)
    tower_factors = round_up(full + hidden, 16)
    cross_factors = layers * (ways * gap + extra)
    logits, dense_grad, *emb_send, tower_other, tower_mine, cross_other, cross_mine = local(
        step_kernel,
        [
            Shape((1, rows), F32),
            Shape((dense_width, rows), F32),
            *[emb_shape] * CHIPS,
            Shape((tower_factors + 2 * CHIPS * LANES, rows), BF16),
            Shape((2 * CHIPS * LANES, rows), BF16),
            Shape((cross_factors + layers * CHIPS * LANES, rows), BF16),
            Shape((layers * CHIPS * LANES, rows), BF16),
        ],
        [
            at,
            parts,
            dense_t,
            in_hbm(own_full),
            own_tail,
            *pieces,
            in_hbm(tower_one),
            bias_one[None, :],
            in_hbm(tower_two),
            bias_two[None, :],
            out_weight[None, :],
            out_bias[None, :],
            labels[None, :],
            own_ids,
        ],
        [],
        [
            pltpu.VMEM((ways, layers, gap, main), BF16),
            pltpu.VMEM((full, hidden), BF16),
            pltpu.VMEM((hidden, hidden), BF16),
            pltpu.VMEM((ways, layers, 64, LANES), F32),
            pltpu.VMEM((8, turned_rows), F32),
            pltpu.VMEM((8, turned_rows), F32),
            pltpu.VMEM((turned_rows, rows), F32),
            pltpu.VMEM((rows, full), F32),
            pltpu.VMEM((rows, full), F32),
            pltpu.VMEM((layers, rows, full), BF16),
            pltpu.VMEM((layers, rows, full), F32),
            pltpu.VMEM((rows, round_up(ways * gap, LANES)), F32),
            pltpu.VMEM((layers, extra, round_up(ways * gap, LANES)), F32),
            pltpu.SemaphoreType.DMA((layers * (1 + 2 * CHIPS * (ways - 1)) + 2,)),
        ],
        in_place=(3, *range(5, 6 + 2 * CHIPS), 7 + 2 * CHIPS),
        name="step",
        shard=shard,
        emb_end=emb_end,
        scale=scale,
    )

    tower_theirs = links.over_dp(tower_other, links.core)
    cross_theirs = links.over_dp(cross_other, links.core)
    emb_got = links.chips_swap(lambda step: emb_send[step])

    tower_rows = round_up(2 * (hidden // ways) + extra // ways, 16)
    tower_shape = (ways, tower_rows, LANES)
    split = lambda shape: Shape((2, shape[0] // 2, *shape[1:]), BF16)
    tower_parts = local(
        tower_product_kernel,
        [split(tower_shape)] * 4,
        [at, tower_other, tower_mine, tower_theirs],
        name="tower_products",
        full=full,
        hidden=hidden,
    )


    cross_rows = layers * gap + extra
    cross_shape = (ways, cross_rows, LANES)
    cross_parts = local(
        cross_product_kernel,
        [split(cross_shape)] * 4,
        [at, cross_other, cross_mine, cross_theirs],
        [tower_parts[0]],
        [pltpu.VMEM((ways, extra, main), F32)],
        name="cross_products",
        layers=layers,
        shard=shard,
        gap=gap,
    )
    tower_first = links.plane_first(tower_parts, [cross_parts[0]], "tower_first")

    *emb_got, _ = lax.optimization_barrier((*emb_got, cross_parts[0]))
    emb_parts = jnp.stack([emb_send[0], *emb_got])
    emb_theirs = links.over_dp(emb_parts, links.core)
    half = rows_here // LOW_ROWS // 2
    table_ends = 16 * -(-turned_rows // LOW_ROWS)
    table_parts = local(
        scatter_kernel,
        Shape((ways, half * wide + table_ends + 16 * half, LOW_ROWS), BF16),
        [at, emb_parts, emb_theirs],
        [tower_first[2]],
        [
            pltpu.VMEM((MARGIN + wide + 64, rows * 2 * CHIPS), F32),
            pltpu.VMEM((ways * half, MARGIN + wide + 64, LOW_ROWS), F32),
            pltpu.VMEM((rows * 2 * CHIPS, LANES), F32),
            pltpu.VMEM((ID_ROWS, rows * 2 * CHIPS), F32),
            pltpu.VMEM((ways * half, 8, LOW_ROWS), F32),
        ],
        name="scatter",
        emb=emb,
        half=half,
        fields=fields,
    )
    table_parts = links.add_others(table_parts)
    table_got = links.cross_exchange(table_parts)
    tower_sum = links.plane_second(tower_first, at, True, [table_parts], "tower_second")
    tower_got = links.cross_swap(lambda step: tower_sum[step])
    tower_fold = local(
        add_kernel, Shape(tower_shape[1:], BF16), [tower_sum[0], *tower_got], name="tower_fold", count=ways
    )
    keep_one, send_one, keep_two, send_two = cross_parts
    send_one, send_two, _ = lax.optimization_barrier((send_one, send_two, tower_first[2]))
    cross_first = links.plane_first((keep_one, send_one, keep_two, send_two), [tower_fold], "cross_first")
    cross_sum = links.plane_second(cross_first, at, False, [], "cross_second")
    table_fold, small = local(
        table_fold_kernel,
        [Shape((half * (wide + 16), LOW_ROWS), BF16), Shape((8, round_up(turned_rows, LOW_ROWS)), F32)],
        [table_got],
        [cross_sum],
        name="table_fold",
        half=half,
    )
    table_all = links.chips_swap(lambda step: table_fold)
    tower_all = jnp.stack([tower_fold, *links.cross_swap(lambda step: tower_fold)])
    cross_got = links.cross_exchange(cross_sum)
    *table_all, _ = lax.optimization_barrier((*table_all, cross_sum))
    table_all = links.both_cores([table_fold, *table_all])
    tower_blocks = links.chips_swap(lambda step: tower_all)
    table_grad, row_counts = local(
        table_kernel,
        [pltpu.HBM((emb_end, rows_here), F32), Shape((fields, rows_here), jnp.int32)],
        [at, *table_all],
        [cross_sum],
        name="table",
        emb=emb,
    )
    cross_fold = local(fold_kernel, Shape(cross_shape[1:], BF16), [cross_got], [table_grad], name="cross_fold")
    *tower_blocks, _ = lax.optimization_barrier((*tower_blocks, cross_fold))
    tower_blocks = links.both_cores([tower_all, *tower_blocks])
    tower_one_grad, tower_two_grad = local(
        tower_kernel, [Shape((full, hidden), F32), Shape((hidden, hidden), F32)], [at, *tower_blocks], name="towers"
    )
    cross_weight_grad = local(
        cross_kernel,
        Shape((layers, shard, full), F32),
        [at, *links.plane_gather(cross_fold)],
        scratch=[pltpu.VMEM((LANES, main), F32)],
        name="cross",
        gap=gap,
    )
    cross_bias_grad = lax.dynamic_slice_in_dim(small[4 : 4 + layers], place * shard, shard, 1)
    return (
        small[7, 0],
        logits[0],
        dense_grad.T,
        table_grad.T,
        cross_weight_grad,
        cross_bias_grad,
        tower_one_grad,
        small[0, :hidden],
        tower_two_grad,
        small[1, :hidden],
        jnp.concatenate([small[2, :full], small[3, :hidden]]),
        small[7, 1:2],
        row_counts.T,
    )


def solution(mesh):
    in_specs = (
        P("cross", None),
        P("dp", None),
        P("dp", None),
        P(("dp", "cross")),
        P(None, "cross", None),
        P(None, "cross"),
        P(),
        P(),
        P(),
        P(),
        P(),
        P(),
    )
    out_specs = (
        P(),
        P(("dp", "cross")),
        P(("dp", "cross"), None),
        P("cross", None),
        P(None, "cross", None),
        P(None, "cross"),
        P(),
        P(),
        P(),
        P(),
        P(),
        P(),
        P("cross", None),
    )
    return jax.shard_map(body, mesh=mesh, in_specs=in_specs, out_specs=out_specs, check_vma=False)
```
